32 devices in a mesh: dp: 4 (over z), tensor: 8 (over y, x, core).
Axes of the slice: x: 2, y: 2, z: 4, core: 2. Of those that a mesh axis runs over, the one named last changes fastest.
Arguments:
- queries: bfloat16 [4, 133, 1024], P('dp', None, 'tensor'), may hold values from -50 to 50
- keys: bfloat16 [4, 1024, 1024], P('dp', None, 'tensor'), may hold values from -4 to 4
- values: bfloat16 [4, 1024, 1024], P('dp', None, 'tensor'), may hold values from -6 to 6
- conv_kernel: float32 [8, 6, 11], P('tensor'), may hold values from -0.9 to 1.9
- span_start: int32 [4], P('dp'), may hold values from 0 to 896, as said below
- out_grad: bfloat16 [4, 128, 1024], P('dp', None, 'tensor'), may hold values from -6 to 6
- proj_weight: float32 [1024, 1024], P('tensor', 'dp'), may hold values from -0.1875 to 0.1875
- moment_one: float32 [1024, 1024], P('tensor', 'dp'), may hold values from -12 to 12
- moment_two: float32 [1024, 1024], P('tensor', 'dp'), may hold values from 1 to 100
Outputs:
- query_grad: bfloat16 [4, 133, 1024], P('dp', None, 'tensor')
- key_grad: bfloat16 [4, 1024, 1024], P('dp', None, 'tensor')
- value_grad: bfloat16 [4, 1024, 1024], P('dp', None, 'tensor')
- kernel_grad: float32 [8, 6, 11], P('tensor')
- proj_new: float32 [1024, 1024], P('tensor', 'dp')
- moment_one_new: float32 [1024, 1024], P('tensor', 'dp')
- moment_two_new: float32 [1024, 1024], P('tensor', 'dp')
The draws below stay inside these ranges and needn't reach their ends.
Inputs may be any that keep to these rules, and one draw needn't show every extreme that they name: `span_start`: each sequence's first block row; one sequence starts at 0 and one at 896.
All inputs are finite; a program needn't handle non-finite values.
Results may differ from the reference program's by a relative error of at most 0.0029.
The reference program's roundings to bfloat16 on the way count: a program that leaves them out, or rounds other values in their place, can miss the bound.
Values may be sent and summed in bfloat16 or wider, within the bound.
No kernel may reach another device: no remote copies, remote signals or barrier semaphores. Data moves between devices by JAX's collectives and lax.ppermute only.
A program may use at most 64 MiB of HBM per device.

```python
import math
import jax
import jax.numpy as jnp
from jax import lax

HEADS = 8
D = 1024
CQ = 6
CK = 11
SPAN = 128
KEYS = 1024
QROWS = 133
GROUPS = 4


def draw_keys(key, part):
    return jnp.clip(jax.random.normal(jax.random.fold_in(key, 24), (GROUPS, KEYS, D), jnp.float32), -4.0, 4.0).astype(jnp.bfloat16)


def draw_queries(key, part):
    return jnp.clip(jax.random.normal(jax.random.fold_in(key, 32), (GROUPS, QROWS, D), jnp.float32), -4.0, 4.0).astype(jnp.bfloat16)


def draw_conv_kernel(key, part):
    taps = jnp.clip(0.3 * jax.random.normal(jax.random.fold_in(key, 42), (HEADS, CQ, CK), jnp.float32), -0.9, 0.9)
    centre = (jnp.arange(CQ)[:, None] == 0) & (jnp.arange(CK)[None, :] == (CK - 1) // 2)
    return taps + centre.astype(jnp.float32)[None, :, :]


def draw_span_start(key, part):
    picks = jax.random.randint(jax.random.fold_in(key, 51), (GROUPS,), 0, KEYS - SPAN + 1)
    order = jax.random.permutation(jax.random.fold_in(key, 52), GROUPS)
    picks = picks.at[order[0]].set(KEYS - SPAN)
    picks = picks.at[order[1]].set(0)
    return picks.astype(jnp.int32)


def block_scale(stream_key, shape, pieces, low, top_value):
    factor_of, own = 1.0, jax.random.fold_in(stream_key, 6)
    for axis_at, blocks in pieces:
        heights = jnp.exp(jax.random.uniform(jax.random.fold_in(own, axis_at), (blocks,), jnp.float32, low / len(pieces), top_value / len(pieces)))
        factor_of = factor_of * jnp.repeat(heights, shape[axis_at] // blocks).reshape([-1 if axis == axis_at else 1 for axis in range(len(shape))])
    return factor_of


def gaussian(rng, dims, deviation, limit, split=(), held_as=jnp.bfloat16):
    factor_of = block_scale(rng, dims, split, -0.22, 0.18) if split else 1.0
    drawn = jax.random.normal(rng, dims, jnp.float32) * deviation * factor_of
    return jnp.minimum(jnp.maximum(drawn, -limit), limit).astype(held_as)


def setup_inputs(seed: int = 0) -> dict:
    arg_keys = jax.random.split(jax.random.key(seed), 10)
    return {
        "queries": draw_queries(jax.random.fold_in(arg_keys[9], 71), 0),
        "keys": draw_keys(jax.random.fold_in(arg_keys[9], 71), 0),
        "values": gaussian(arg_keys[2], (GROUPS, KEYS, D), 1.0, 6.0, ((0, 4), (2, 8))),
        "conv_kernel": draw_conv_kernel(jax.random.fold_in(arg_keys[9], 71), 0),
        "span_start": draw_span_start(jax.random.fold_in(arg_keys[9], 71), 0),
        "out_grad": gaussian(arg_keys[5], (GROUPS, SPAN, D), 1.0, 6.0, ((0, 4), (2, 8))),
        "proj_weight": gaussian(arg_keys[6], (D, D), D ** -0.5, 0.1875, ((0, 8), (1, 4)), jnp.float32),
        "moment_one": gaussian(arg_keys[7], (D, D), 3.0, 12.0, ((0, 8), (1, 4)), jnp.float32),
        "moment_two": jnp.clip(jnp.exp(math.log(100.0) - 4.6051702 * jax.random.uniform(arg_keys[8], (D, D), jnp.float32) ** block_scale(arg_keys[8], (D, D), ((0, 8), (1, 4)), -0.2, 0.2)), 1.0, 100.0),
    }


beta_one = 0.9
beta_two = 0.95
learn_rate = 0.01
decay_rate = 0.1
adam_eps = 1e-08
bias_one = 1.0 - 0.9 ** 10
bias_two = 1.0 - 0.95 ** 10

def head_backward(query_rows, key_rows, value_rows, kernel, proj_rows, first_pos, upstream):
    conv_rows = kernel.shape[0]
    conv_cols = kernel.shape[1]
    half_width = (conv_cols - 1) // 2
    span_len = upstream.shape[0]
    key_count = key_rows.shape[0]
    query_count = query_rows.shape[0]
    score_scale = 1.0 / query_rows.shape[1] ** 0.5
    key_pos = jnp.arange(key_count, dtype=jnp.int32)
    row_pos = first_pos - (conv_rows - 1) + jnp.arange(query_count, dtype=jnp.int32)
    visible = key_pos[None, :] <= row_pos[:, None]
    raw_scores = jnp.dot(query_rows, key_rows.T, preferred_element_type=jnp.float32) * score_scale
    masked = jnp.where(visible, raw_scores, 0.0)
    padded = jnp.pad(masked, ((0, 0), (half_width, half_width)))
    mixed_scores = jnp.zeros((span_len, key_count), jnp.float32)
    for tap_row in range(conv_rows):
        for tap_col in range(conv_cols):
            row_first = conv_rows - 1 - tap_row
            mixed_scores = mixed_scores + kernel[tap_row, tap_col] * padded[row_first:row_first + span_len, tap_col:tap_col + key_count]
    live_mask = visible[conv_rows - 1:]
    row_top = lax.optimization_barrier(jnp.max(jnp.where(live_mask, mixed_scores, -jnp.inf), axis=1, keepdims=True))
    exp_terms = jnp.where(live_mask, jnp.exp(mixed_scores - row_top), 0.0)
    weights_soft = exp_terms / lax.optimization_barrier(jnp.sum(exp_terms, axis=1, keepdims=True))
    weights_bf = weights_soft.astype(jnp.bfloat16)
    attended = jnp.dot(weights_bf, value_rows, preferred_element_type=jnp.float32).astype(jnp.bfloat16)
    grad_out = jnp.dot(upstream, proj_rows.T, preferred_element_type=jnp.float32).astype(jnp.bfloat16)
    grad_values = jnp.dot(weights_bf.T, grad_out, preferred_element_type=jnp.float32).astype(jnp.bfloat16)
    grad_weights = jnp.dot(grad_out, value_rows.T, preferred_element_type=jnp.float32)
    row_inner = lax.optimization_barrier(jnp.sum(weights_soft * grad_weights, axis=1, keepdims=True))
    grad_mixed = weights_soft * (grad_weights - row_inner)
    grad_pad = jnp.pad(grad_mixed, ((conv_rows - 1, conv_rows - 1), (half_width, half_width)))
    grad_masked = jnp.zeros((query_count, key_count), jnp.float32)
    kernel_terms = []
    for tap_row in range(conv_rows):
        for tap_col in range(conv_cols):
            col_first = 2 * half_width - tap_col
            grad_masked = grad_masked + kernel[tap_row, tap_col] * grad_pad[tap_row:tap_row + query_count, col_first:col_first + key_count]
            row_first = conv_rows - 1 - tap_row
            kernel_terms.append(jnp.sum(grad_mixed * padded[row_first:row_first + span_len, tap_col:tap_col + key_count]))
    kernel_grad = jnp.stack(kernel_terms).reshape(conv_rows, conv_cols)
    grad_scores = jnp.where(visible, grad_masked, 0.0).astype(jnp.bfloat16)
    grad_query = (score_scale * jnp.dot(grad_scores, key_rows, preferred_element_type=jnp.float32)).astype(jnp.bfloat16)
    grad_keys = (score_scale * jnp.dot(grad_scores.T, query_rows, preferred_element_type=jnp.float32)).astype(jnp.bfloat16)
    proj_term = jnp.dot(attended.T, upstream, preferred_element_type=jnp.float32)
    return (grad_query, grad_keys, grad_values, kernel_grad, proj_term)

def split_heads(array_in, head_count):
    return array_in.reshape(array_in.shape[0], head_count, -1).transpose(1, 0, 2)

def join_heads(array_in):
    return array_in.transpose(1, 0, 2).reshape(array_in.shape[1], -1)

def reference(queries, keys, values, conv_kernel, span_start, out_grad, proj_weight, moment_one, moment_two):
    head_count = conv_kernel.shape[0]
    width = proj_weight.shape[0]
    head_dim = width // head_count
    group_count = queries.shape[0]
    span_len = out_grad.shape[1]
    proj_bf = proj_weight.astype(jnp.bfloat16).reshape(head_count, head_dim, width)

    def group_step(state_pair, group_items):
        proj_total, kernel_total = state_pair
        query_g, key_g, value_g, first_pos, upstream = group_items

        def per_head(head_items):
            return head_backward(head_items[0], head_items[1], head_items[2], head_items[3], head_items[4], first_pos, upstream)
        results = lax.map(per_head, (split_heads(query_g, head_count), split_heads(key_g, head_count), split_heads(value_g, head_count), conv_kernel, proj_bf))
        grad_query, grad_keys, grad_values, kernel_part, proj_part = results
        proj_total = proj_total + proj_part.reshape(width, width)
        kernel_total = kernel_total + kernel_part
        return ((proj_total, kernel_total), (join_heads(grad_query), join_heads(grad_keys), join_heads(grad_values)))
    start_state = (jnp.zeros((width, width), jnp.float32), jnp.zeros(conv_kernel.shape, jnp.float32))
    finals, grads = lax.scan(group_step, start_state, (queries, keys, values, span_start, out_grad))
    proj_sum, kernel_sum = finals
    grad_proj = proj_sum / float(group_count)
    kernel_grad = kernel_sum / float(group_count * span_len)
    query_grad, key_grad, value_grad = grads
    moment_one_new = beta_one * moment_one + (1.0 - beta_one) * grad_proj
    moment_two_new = beta_two * moment_two + (1.0 - beta_two) * grad_proj * grad_proj
    first_hat = moment_one_new / bias_one
    second_hat = moment_two_new / bias_two
    proj_new = proj_weight - learn_rate * (first_hat / (jnp.sqrt(second_hat) + adam_eps) + decay_rate * proj_weight)
    return (query_grad, key_grad, value_grad, kernel_grad, proj_new, moment_one_new, moment_two_new)
```

```python
import functools
import math

import jax
import jax.numpy as jnp
from jax import lax
from jax.experimental import pallas as pl
from jax.experimental.pallas import tpu as pltpu
from jax.sharding import PartitionSpec as P

beta_one = 0.9
beta_two = 0.95
learn_rate = 0.01
decay_rate = 0.1
adam_eps = 1e-08
bias_one = 1.0 - 0.9**10
bias_two = 1.0 - 0.95**10

LANES = 128
HALF = LANES // 2
F32 = jnp.float32
BF16 = jnp.bfloat16


def dot(left, right, dims=((1,), (0,))):
    return lax.dot_general(left, right, (dims, ((), ())), preferred_element_type=F32)


def split(x):
    high = x.astype(BF16)
    return high, (x - high.astype(F32)).astype(BF16)


def up_to(n, multiple):
    return -(-n // multiple) * multiple


def iota(shape, axis):
    return lax.broadcasted_iota(jnp.int32, shape, axis)


def bands(kernel_ref, taps_a, taps_b, flipped):
    half = (taps_b - 1) // 2
    place = iota((2 * LANES, LANES), 0) - iota((2 * LANES, LANES), 1) - (HALF - half)
    out = [jnp.zeros((2 * LANES, LANES), F32) for _ in range(taps_a)]
    for b in range(taps_b):
        here = place == (taps_b - 1 - b if flipped else b)
        for a in range(taps_a):
            out[a] = jnp.where(here, kernel_ref[0, a, b], out[a])
    return out


def forward(
    first_ref, kernel_ref, q_ref, k_ref, v_ref,
    p_ref, pt_ref, o_ref, xth_ref, xtl_ref, bh_ref, bl_ref,
    q32, fh, fl, xh, xl, y, kpad, vpad,
):
    _, taps_a, taps_b = kernel_ref.shape
    _, rows, depth = q_ref.shape
    keys = k_ref.shape[1]
    span = rows - taps_a + 1
    rows_up = q32.shape[0]
    blocks = keys // LANES
    scale = 1.0 / math.sqrt(depth)
    first = first_ref[0]

    q32[...] = jnp.zeros_like(q32)
    q32[:rows] = q_ref[0].astype(F32)
    for a, (f, t) in enumerate(
        zip(bands(kernel_ref, taps_a, taps_b, False), bands(kernel_ref, taps_a, taps_b, True), strict=True)
    ):
        cols = pl.ds(a * LANES, LANES)
        fh[:, cols], fl[:, cols] = split(f)
        bh_ref[:, cols], bl_ref[:, cols] = split(t)

    q_all = q32[...].astype(BF16)
    zero = jnp.zeros((rows_up, LANES), BF16)
    for ref in (xh, xl):
        ref[:rows_up, :LANES] = zero
        ref[blocks * rows_up :, LANES:] = zero
    for n in range(blocks):
        x = dot(q_all, k_ref[0, n * LANES : (n + 1) * LANES], ((1,), (1,))) * scale
        key = n * LANES + iota(x.shape, 1)
        pos = first - (taps_a - 1) + iota(x.shape, 0)
        high, low = split(jnp.where(key <= pos, x, 0.0))
        for ref, part in ((xh, high), (xl, low)):
            ref[n * rows_up : (n + 1) * rows_up, LANES:] = part
            ref[(n + 1) * rows_up : (n + 2) * rows_up, :LANES] = part

    for at in range(0, taps_a * LANES, 2 * LANES):
        cols = pl.ds(at, 2 * LANES)
        y[:, cols] = dot(xh[...], fh[:, cols]) + dot(xh[...], fl[:, cols]) + dot(xl[...], fh[:, cols])
    mixed = []
    for w in range(blocks + 1):
        total = None
        for a in range(taps_a):
            start = w * rows_up + taps_a - 1 - a
            term = y[start : start + span, a * LANES : (a + 1) * LANES]
            total = term if total is None else total + term
        mixed.append(total)
    c = jnp.concatenate(mixed, axis=1)
    key = iota(c.shape, 1) - HALF
    live = (key >= 0) & (key <= first + iota(c.shape, 0))
    top = jnp.max(jnp.where(live, c, -jnp.inf), axis=1, keepdims=True)
    terms = jnp.where(live, jnp.exp(c - top), 0.0)
    p = terms / jnp.sum(terms, axis=1, keepdims=True)
    p_ref[...] = p
    pt_ref[...] = p.T.astype(BF16)
    vpad[...] = jnp.zeros_like(vpad)
    vpad[HALF : HALF + keys] = v_ref[0]
    o_ref[...] = dot(p.astype(BF16), vpad[...]).astype(BF16)

    edge = (kpad.shape[0] - keys) // 2
    kpad[...] = jnp.zeros_like(kpad)
    flip = (iota((LANES, LANES), 0) + iota((LANES, LANES), 1) == LANES - 1).astype(F32).astype(BF16)
    for n in range(blocks):
        kpad[edge + n * LANES : edge + (n + 1) * LANES] = dot(
            flip, k_ref[0, keys - (n + 1) * LANES : keys - n * LANES]
        ).astype(BF16)
    for a in range(taps_a):
        start = taps_a - 1 - a
        xt = dot(kpad[...], q32[start : start + span].astype(BF16), ((1,), (1,))) * scale
        key = keys - 1 + edge - iota(xt.shape, 0)
        pos = first - a + iota(xt.shape, 1)
        cols = pl.ds(a * LANES, LANES)
        xth_ref[:, cols], xtl_ref[:, cols] = split(jnp.where(key <= pos, xt, 0.0))


def backward(
    taps_b, first_ref, up_ref, w_ref, p_ref, pt_ref, xth_ref, xtl_ref, bh_ref, bl_ref, q_ref, k_ref, v_ref,
    dq_ref, dk_ref, dv_ref, taps_ref,
    vpad, ch, cl, z, q16,
):
    _, rows, depth = q_ref.shape
    keys = k_ref.shape[1]
    span = p_ref.shape[0]
    taps_a = rows - span + 1
    blocks = keys // LANES
    scale = 1.0 / math.sqrt(depth)
    first = first_ref[0]
    half = (taps_b - 1) // 2
    edge = (xth_ref.shape[0] - keys) // 2

    vpad[...] = jnp.zeros_like(vpad)
    vpad[HALF : HALF + keys] = v_ref[0]
    do = dot(up_ref[...], w_ref[...], ((1,), (1,))).astype(BF16)
    dp = dot(do, vpad[...], ((1,), (1,)))
    p = p_ref[...]
    dc = p * (dp - jnp.sum(p * dp, axis=1, keepdims=True))
    high, low = split(dc)
    for w in range(blocks + 1):
        cols = slice(w * LANES, (w + 1) * LANES)
        here = slice(w * span, (w + 1) * span)
        ch[here] = high[:, cols]
        cl[here] = low[:, cols]

    window = up_to(LANES + edge - HALF + half, 16)
    right = jnp.concatenate([ch[...], cl[...]], axis=1)
    spot = window - 1 - (edge - HALF - half) - iota((window, LANES), 0) - iota((window, LANES), 1)
    wanted = (spot >= 0) & (spot < taps_b)
    for a in range(taps_a):
        total = None
        for ref in (xth_ref, xtl_ref):
            left = jnp.concatenate(
                [ref[w * LANES : w * LANES + window, a * LANES : (a + 1) * LANES] for w in range(blocks, -1, -1)], axis=1
            )
            term = dot(left, right)
            total = term if total is None else total + term
        total = jnp.where(wanted, total[:, :LANES] + total[:, LANES:], 0.0)
        turned = pltpu.roll(total, 0, 1, stride=1, stride_axis=0)
        taps_ref[a : a + 1] = jnp.sum(turned, axis=0, keepdims=True)

    rows_up = up_to(rows, 16)
    depth_z = z.shape[0] // blocks
    for n in range(blocks):
        left_h = jnp.concatenate([ch[n * span : (n + 1) * span], ch[(n + 1) * span : (n + 2) * span]], axis=1)
        left_l = jnp.concatenate([cl[n * span : (n + 1) * span], cl[(n + 1) * span : (n + 2) * span]], axis=1)
        z[n * depth_z : n * depth_z + 8] = jnp.zeros((8, z.shape[1]), F32)
        z[n * depth_z + 8 + span : (n + 1) * depth_z] = jnp.zeros((depth_z - 8 - span, z.shape[1]), F32)
        for at in range(0, taps_a * LANES, 2 * LANES):
            cols = pl.ds(at, 2 * LANES)
            z[n * depth_z + 8 : n * depth_z + 8 + span, cols] = (
                dot(left_h, bh_ref[:, cols]) + dot(left_h, bl_ref[:, cols]) + dot(left_l, bh_ref[:, cols])
            )
    q16[...] = jnp.zeros_like(q16)
    q16[:rows] = q_ref[0]
    dq = jnp.zeros((rows_up, depth), F32)
    for n in range(blocks):
        total = None
        for a in range(taps_a):
            start = n * depth_z + 8 - (taps_a - 1) + a
            term = z[start : start + rows_up, a * LANES : (a + 1) * LANES]
            total = term if total is None else total + term
        key = n * LANES + iota(total.shape, 1)
        pos = first - (taps_a - 1) + iota(total.shape, 0)
        ds = jnp.where(key <= pos, total, 0.0)
        here = slice(n * LANES, (n + 1) * LANES)
        dq = dq + dot(ds.astype(BF16), k_ref[0, here])
        dk_ref[0, here] = (scale * dot(ds.T.astype(BF16), q16[...])).astype(BF16)
    dq_ref[0] = (scale * dq)[:rows].astype(BF16)
    dv_ref[0] = dot(pt_ref[...], do)[HALF : HALF + keys].astype(BF16)


def exchange(x, axis):
    n = lax.axis_size(axis)
    return [x] + [lax.ppermute(x, axis, [(i, (i + s) % n) for i in range(n)]) for s in range(1, n)]


def shards(queries, keys, values, conv_kernel, span_start, out_grad, proj_weight, moment_one, moment_two):
    _, rows, depth = queries.shape
    key_count = keys.shape[1]
    _, taps_a, taps_b = conv_kernel.shape
    span = out_grad.shape[1]
    blocks = key_count // LANES
    rows_up = up_to(rows, 16)
    padded = key_count + LANES
    edge = up_to(HALF + (taps_b - 1) // 2, 16)
    wide = key_count + 2 * edge
    group_count = lax.axis_size("dp")
    vmem = pltpu.CompilerParams(vmem_limit_bytes=40 * 2**20)
    smem = pl.BlockSpec(memory_space=pltpu.SMEM)
    whole = pl.BlockSpec(memory_space=pltpu.VMEM)

    upstream = lax.all_gather(out_grad[0], "tensor", axis=1, tiled=True)
    proj_all = lax.all_gather(proj_weight.astype(BF16), "dp", axis=1, tiled=True)

    p, pt, attended, xth, xtl, bh, bl = pl.pallas_call(
        forward,
        out_shape=(
            jax.ShapeDtypeStruct((span, padded), F32),
            jax.ShapeDtypeStruct((padded, span), BF16),
            jax.ShapeDtypeStruct((span, depth), BF16),
            jax.ShapeDtypeStruct((wide, taps_a * span), BF16),
            jax.ShapeDtypeStruct((wide, taps_a * span), BF16),
            jax.ShapeDtypeStruct((2 * LANES, taps_a * LANES), BF16),
            jax.ShapeDtypeStruct((2 * LANES, taps_a * LANES), BF16),
        ),
        in_specs=[smem, smem, whole, whole, whole],
        out_specs=(whole,) * 7,
        scratch_shapes=[
            pltpu.VMEM((rows_up, depth), F32),
            pltpu.VMEM((2 * LANES, taps_a * LANES), BF16),
            pltpu.VMEM((2 * LANES, taps_a * LANES), BF16),
            pltpu.VMEM(((blocks + 1) * rows_up, 2 * LANES), BF16),
            pltpu.VMEM(((blocks + 1) * rows_up, 2 * LANES), BF16),
            pltpu.VMEM(((blocks + 1) * rows_up, taps_a * LANES), F32),
            pltpu.VMEM((wide, depth), BF16),
            pltpu.VMEM((padded, depth), BF16),
        ],
        compiler_params=vmem,
        name="attention_forward",
    )(span_start, conv_kernel, queries, keys, values)

    query_grad, key_grad, value_grad, taps = pl.pallas_call(
        functools.partial(backward, taps_b),
        out_shape=(
            jax.ShapeDtypeStruct(queries.shape, BF16),
            jax.ShapeDtypeStruct(keys.shape, BF16),
            jax.ShapeDtypeStruct(values.shape, BF16),
            jax.ShapeDtypeStruct((taps_a, LANES), F32),
        ),
        in_specs=[smem] + [whole] * 11,
        out_specs=(whole,) * 4,
        scratch_shapes=[
            pltpu.VMEM((padded, depth), BF16),
            pltpu.VMEM(((blocks + 1) * span, LANES), BF16),
            pltpu.VMEM(((blocks + 1) * span, LANES), BF16),
            pltpu.VMEM((blocks * (span + 32), taps_a * LANES), F32),
            pltpu.VMEM((rows_up, depth), BF16),
        ],
        compiler_params=vmem,
        name="attention_backward",
    )(span_start, upstream, proj_all, p, pt, xth, xtl, bh, bl, queries, keys, values)

    me = lax.axis_index("dp")
    share = proj_weight.shape[1]
    part = dot(attended, upstream, ((0,), (0,)))
    grad_proj = lax.dynamic_slice_in_dim(part, me * share, share, axis=1)
    for s in range(1, group_count):
        owner = lax.rem(me + s, group_count)
        piece = lax.dynamic_slice_in_dim(part, owner * share, share, axis=1)
        grad_proj = grad_proj + lax.ppermute(piece, "dp", [(i, (i + s) % group_count) for i in range(group_count)])
    grad_proj = grad_proj / float(group_count)
    half = (taps_b - 1) // 2
    last = up_to(LANES + edge - HALF + half, 16) - 1 - (edge - HALF - half) - LANES
    taps = sum(exchange(taps, "dp"))[:, last - taps_b + 1 : last + 1][:, ::-1]
    kernel_total = taps / float(group_count * span)
    moment_one_new = beta_one * moment_one + (1.0 - beta_one) * grad_proj
    moment_two_new = beta_two * moment_two + (1.0 - beta_two) * grad_proj * grad_proj
    first_hat = moment_one_new / bias_one
    second_hat = moment_two_new / bias_two
    proj_new = proj_weight - learn_rate * (first_hat / (jnp.sqrt(second_hat) + adam_eps) + decay_rate * proj_weight)
    return (query_grad, key_grad, value_grad, kernel_total[None], proj_new, moment_one_new, moment_two_new)


def solution(mesh):
    heads, rows_of, blocks_of = P("dp", None, "tensor"), P("tensor", None, None), P("tensor", "dp")
    return jax.shard_map(
        shards,
        mesh=mesh,
        in_specs=(heads, heads, heads, rows_of, P("dp"), heads, blocks_of, blocks_of, blocks_of),
        out_specs=(heads, heads, heads, rows_of, blocks_of, blocks_of, blocks_of),
        check_vma=False,
    )
```

```python
import functools
import math

import jax
import jax.numpy as jnp
from jax import lax
from jax.experimental import pallas as pl
from jax.experimental.pallas import tpu as pltpu
from jax.sharding import PartitionSpec as P

beta_one = 0.9
beta_two = 0.95
learn_rate = 0.01
decay_rate = 0.1
adam_eps = 1e-08
bias_one = 1.0 - 0.9**10
bias_two = 1.0 - 0.95**10

LANES = 128
HALF = LANES // 2
F32 = jnp.float32
BF16 = jnp.bfloat16


def dot(left, right, dims=((1,), (0,))):
    return lax.dot_general(left, right, (dims, ((), ())), preferred_element_type=F32)


def split(x):
    high = x.astype(BF16)
    return high, (x - high.astype(F32)).astype(BF16)


def up_to(n, multiple):
    return -(-n // multiple) * multiple


def iota(shape, axis):
    return lax.broadcasted_iota(jnp.int32, shape, axis)


def bands(kernel_ref, flipped):
    taps_a, _, taps_b = kernel_ref.shape
    half = (taps_b - 1) // 2
    place = iota((2 * LANES, LANES), 0) - iota((2 * LANES, LANES), 1) - (HALF - half)
    out = [jnp.zeros((2 * LANES, LANES), F32) for _ in range(taps_a)]
    for b in range(taps_b):
        here = place == (taps_b - 1 - b if flipped else b)
        for a in range(taps_a):
            out[a] = jnp.where(here, kernel_ref[a, 0, b], out[a])
    return out


def forward(
    first_ref, kernel_ref, q_hbm, k_hbm, v_hbm,
    p_ref, pt_ref, o_ref, xth_ref, xtl_ref, bh_ref, bl_ref, vpad, q16,
    q_in, k_in, v_in, q32, fh, fl, xh, xl, y, kpad, sems,
):
    taps_a, _, taps_b = kernel_ref.shape
    rows, depth = q_in.shape
    keys = k_in.shape[0]
    span = rows - taps_a + 1
    rows_up = q32.shape[0]
    blocks = keys // LANES
    scale = 1.0 / math.sqrt(depth)
    first = first_ref[0]
    copies = [
        pltpu.make_async_copy(src.at[0], dst, sems.at[n])
        for n, (src, dst) in enumerate(((q_hbm, q_in), (k_hbm, k_in), (v_hbm, v_in)))
    ]
    for copy in copies:
        copy.start()

    for a, (f, t) in enumerate(zip(bands(kernel_ref, False), bands(kernel_ref, True), strict=True)):
        cols = pl.ds(a * LANES, LANES)
        fh[:, cols], fl[:, cols] = split(f)
        bh_ref[:, cols], bl_ref[:, cols] = split(t)
    q32[...] = jnp.zeros_like(q32)
    vpad[...] = jnp.zeros_like(vpad)
    kpad[...] = jnp.zeros_like(kpad)
    for copy in copies:
        copy.wait()
    q32[:rows] = q_in[...].astype(F32)
    q_all = q32[...].astype(BF16)
    q16[...] = q_all
    vpad[HALF : HALF + keys] = v_in[...]

    zero = jnp.zeros((rows_up, LANES), BF16)
    for ref in (xh, xl):
        ref[:rows_up, :LANES] = zero
        ref[blocks * rows_up :, LANES:] = zero
    for n in range(blocks):
        x = dot(q_all, k_in[n * LANES : (n + 1) * LANES], ((1,), (1,))) * scale
        key = n * LANES + iota(x.shape, 1)
        pos = first - (taps_a - 1) + iota(x.shape, 0)
        high, low = split(jnp.where(key <= pos, x, 0.0))
        for ref, part in ((xh, high), (xl, low)):
            ref[n * rows_up : (n + 1) * rows_up, LANES:] = part
            ref[(n + 1) * rows_up : (n + 2) * rows_up, :LANES] = part

    for at in range(0, taps_a * LANES, 2 * LANES):
        cols = pl.ds(at, 2 * LANES)
        y[:, cols] = dot(xh[...], fh[:, cols]) + dot(xh[...], fl[:, cols]) + dot(xl[...], fh[:, cols])
    mixed = []
    for w in range(blocks + 1):
        total = None
        for a in range(taps_a):
            start = w * rows_up + taps_a - 1 - a
            term = y[start : start + span, a * LANES : (a + 1) * LANES]
            total = term if total is None else total + term
        mixed.append(total)
    c = jnp.concatenate(mixed, axis=1)
    key = iota(c.shape, 1) - HALF
    live = (key >= 0) & (key <= first + iota(c.shape, 0))
    top = jnp.max(jnp.where(live, c, -jnp.inf), axis=1, keepdims=True)
    terms = jnp.where(live, jnp.exp(c - top), 0.0)
    p = terms / jnp.sum(terms, axis=1, keepdims=True)
    p_ref[...] = p
    pt_ref[...] = p.T.astype(BF16)
    o_ref[...] = dot(p.astype(BF16), vpad[...]).astype(BF16)

    edge = (kpad.shape[0] - keys) // 2
    flip = (iota((LANES, LANES), 0) + iota((LANES, LANES), 1) == LANES - 1).astype(F32).astype(BF16)
    for n in range(blocks):
        kpad[edge + n * LANES : edge + (n + 1) * LANES] = dot(
            flip, k_in[keys - (n + 1) * LANES : keys - n * LANES]
        ).astype(BF16)
    for a in range(taps_a):
        start = taps_a - 1 - a
        xt = dot(kpad[...], q32[start : start + span].astype(BF16), ((1,), (1,))) * scale
        key = keys - 1 + edge - iota(xt.shape, 0)
        pos = first - a + iota(xt.shape, 1)
        cols = pl.ds(a * LANES, LANES)
        xth_ref[:, cols], xtl_ref[:, cols] = split(jnp.where(key <= pos, xt, 0.0))


def backward_scores(taps_b, up_places, w_places, payloads, by_distance, *refs):
    n_up, n_w = len({p[0] for p in up_places}), len({p[0] for p in w_places})
    up_refs, w_refs, refs = refs[:n_up], refs[n_up : n_up + n_w], refs[n_up + n_w :]
    p_ref, vpad, xth_ref, xtl_ref, o_ref, do_ref, ch, cl = refs[:8]
    out_refs, (up, w) = refs[8 : 8 + payloads], refs[8 + payloads :]
    span = p_ref.shape[0]
    keys = vpad.shape[0] - LANES
    taps_a = xth_ref.shape[1] // span
    blocks = keys // LANES
    half = (taps_b - 1) // 2
    edge = (xth_ref.shape[0] - keys) // 2

    for refs_in, places, axis, whole in ((up_refs, up_places, "tensor", up), (w_refs, w_places, "dp", w)):
        me = lax.axis_index(axis)
        for n, part, shift, at in places:
            block = refs_in[n][part]
            width = block.shape[1]
            spot = at if shift is None else lax.bitwise_xor(me, shift)
            whole[:, pl.ds(pl.multiple_of(spot * width, width), width)] = block
    do = dot(up[...], w[...], ((1,), (1,))).astype(BF16)
    do_ref[...] = do
    dp = dot(do, vpad[...], ((1,), (1,)))
    p = p_ref[...]
    high, low = split(p * (dp - jnp.sum(p * dp, axis=1, keepdims=True)))
    for n in range(blocks + 1):
        cols = slice(n * LANES, (n + 1) * LANES)
        here = slice(n * span, (n + 1) * span)
        ch[here] = high[:, cols]
        cl[here] = low[:, cols]

    window = up_to(LANES + edge - HALF + half, 16)
    right = jnp.concatenate([ch[...], cl[...]], axis=1)
    spot = window - 1 - (edge - HALF - half) - iota((window, LANES), 0) - iota((window, LANES), 1)
    wanted = (spot >= 0) & (spot < taps_b)
    sums = []
    for a in range(taps_a):
        total = None
        for ref in (xth_ref, xtl_ref):
            left = jnp.concatenate(
                [ref[n * LANES : n * LANES + window, a * LANES : (a + 1) * LANES] for n in range(blocks, -1, -1)], axis=1
            )
            term = dot(left, right)
            total = term if total is None else total + term
        total = jnp.where(wanted, total[:, :LANES] + total[:, LANES:], 0.0)
        sums.append(jnp.sum(pltpu.roll(total, 0, 1, stride=1, stride_axis=0), axis=0, keepdims=True))
    taps = jnp.concatenate(sums + [jnp.zeros((8 - taps_a, LANES), F32)], axis=0)

    high, low = split(taps)
    mid, low = low, (taps - high.astype(F32) - low.astype(F32)).astype(BF16)
    parts = jnp.concatenate([high.astype(F32), mid.astype(F32)], axis=0).astype(BF16)
    rest = jnp.concatenate([low.astype(F32), jnp.zeros((8, LANES), F32)], axis=0).astype(BF16)
    me = lax.axis_index("dp")
    for s, ref in enumerate(out_refs):
        share = ref.shape[1] - LANES
        spot = lax.bitwise_xor(me, s) if by_distance else s
        ref[:span, :share] = up[:, pl.ds(pl.multiple_of(spot * share, share), share)]
        ref[:span, share:] = o_ref[...]
        ref[span:, :LANES] = parts
        ref[span:, LANES : 2 * LANES] = rest


def backward_inputs(rows, taps_a, first_ref, do_ref, ch, cl, pt_ref, bh_ref, bl_ref, q16, k_hbm, dq_ref, dk_ref, dv_ref, k_in, z, sem):
    keys, depth = k_in.shape
    rows_up = q16.shape[0]
    span = do_ref.shape[0]
    blocks = keys // LANES
    scale = 1.0 / math.sqrt(depth)
    first = first_ref[0]
    copy = pltpu.make_async_copy(k_hbm.at[0], k_in, sem.at[0])
    copy.start()
    dv_ref[0] = dot(pt_ref[HALF : HALF + keys], do_ref[...]).astype(BF16)
    depth_z = z.shape[0] // blocks
    for n in range(blocks):
        left_h = jnp.concatenate([ch[n * span : (n + 1) * span], ch[(n + 1) * span : (n + 2) * span]], axis=1)
        left_l = jnp.concatenate([cl[n * span : (n + 1) * span], cl[(n + 1) * span : (n + 2) * span]], axis=1)
        z[n * depth_z : n * depth_z + 8] = jnp.zeros((8, z.shape[1]), F32)
        z[n * depth_z + 8 + span : (n + 1) * depth_z] = jnp.zeros((depth_z - 8 - span, z.shape[1]), F32)
        for at in range(0, taps_a * LANES, 2 * LANES):
            cols = pl.ds(at, 2 * LANES)
            z[n * depth_z + 8 : n * depth_z + 8 + span, cols] = (
                dot(left_h, bh_ref[:, cols]) + dot(left_h, bl_ref[:, cols]) + dot(left_l, bh_ref[:, cols])
            )
    copy.wait()
    dq = jnp.zeros((rows_up, depth), F32)
    for n in range(blocks):
        total = None
        for a in range(taps_a):
            start = n * depth_z + 8 - (taps_a - 1) + a
            term = z[start : start + rows_up, a * LANES : (a + 1) * LANES]
            total = term if total is None else total + term
        key = n * LANES + iota(total.shape, 1)
        pos = first - (taps_a - 1) + iota(total.shape, 0)
        ds = jnp.where(key <= pos, total, 0.0)
        here = slice(n * LANES, (n + 1) * LANES)
        dq = dq + dot(ds.astype(BF16), k_in[here])
        dk_ref[0, here] = (scale * dot(ds.T.astype(BF16), q16[...])).astype(BF16)
    dq_ref[0] = (scale * dq)[:rows].astype(BF16)


def update(last, *refs):
    payload_refs, (w_ref, one_ref, two_ref, new_ref, one_new_ref, two_new_ref, taps_ref) = refs[:-7], refs[-7:]
    count = len(payload_refs)
    taps_a, _, taps_b = taps_ref.shape
    span = payload_refs[0].shape[0] - 16
    share = w_ref.shape[1]
    grad, taps = None, None
    for ref in payload_refs:
        term = dot(ref[:span, share:], ref[:span, :share], ((0,), (0,)))
        parts, rest = ref[span:, :LANES].astype(F32), ref[span:, LANES : 2 * LANES].astype(F32)
        tap = parts[:8] + (parts[8:] + rest[:8])
        grad, taps = (term, tap) if grad is None else (grad + term, taps + tap)
    grad = grad / float(count)
    taps = taps / float(count * span)
    lane = iota((8, LANES), 1)
    turned = jnp.zeros((8, LANES), F32)
    for b in range(taps_b):
        turned = jnp.where(lane == b, taps[:, last - b : last - b + 1], turned)
    for a in range(taps_a):
        taps_ref[a] = turned[a : a + 1, :taps_b]
    one = beta_one * one_ref[...] + (1.0 - beta_one) * grad
    two = beta_two * two_ref[...] + (1.0 - beta_two) * grad * grad
    one_new_ref[...] = one
    two_new_ref[...] = two
    old = w_ref[...]
    new_ref[...] = old - learn_rate * ((one / bias_one) / (jnp.sqrt(two / bias_two) + adam_eps) + decay_rate * old)


def swap(x, axis, shift):
    n = lax.axis_size(axis)
    return lax.ppermute(x, axis, [(i, i ^ shift) for i in range(n)])


def few(axis):
    n = lax.axis_size(axis)
    return n <= 8 and n & (n - 1) == 0


def gathered(x, axis):
    if few(axis):
        shifts = range(lax.axis_size(axis))
        return [x] + [swap(x, axis, s) for s in shifts[1:]], [(s, slice(None), s, None) for s in shifts]
    n = lax.axis_size(axis)
    return [lax.all_gather(x, axis)], [(0, i, None, i) for i in range(n)]


def gathered_by_pairs(x, axis):
    n = lax.axis_size(axis)
    if not few(axis) or n < 4:
        return gathered(x, axis)
    rows = x.shape[0]
    pair = jnp.concatenate([x, swap(x, axis, 1)], axis=0)
    arrays = [pair] + [swap(pair, axis, s) for s in range(2, n, 2)]
    return arrays, [(s // 2, slice(c * rows, (c + 1) * rows), s + c, None) for s in range(0, n, 2) for c in (0, 1)]


def shards(queries, keys, values, conv_kernel, span_start, out_grad, proj_weight, moment_one, moment_two):
    _, rows, depth = queries.shape
    key_count = keys.shape[1]
    _, taps_a, taps_b = conv_kernel.shape
    span = out_grad.shape[1]
    blocks = key_count // LANES
    rows_up = up_to(rows, 16)
    padded = key_count + LANES
    half = (taps_b - 1) // 2
    edge = up_to(HALF + half, 16)
    wide = key_count + 2 * edge
    group_count = lax.axis_size("dp")
    share = proj_weight.shape[1]
    columns = share * group_count
    vmem = pltpu.CompilerParams(vmem_limit_bytes=24 * 2**20)
    smem = pl.BlockSpec(memory_space=pltpu.SMEM)
    whole = pl.BlockSpec(memory_space=pltpu.VMEM)
    hbm = pl.BlockSpec(memory_space=pltpu.HBM)
    shape = jax.ShapeDtypeStruct

    up_arrays, up_places = gathered_by_pairs(out_grad[0], "tensor")
    w_arrays, w_places = gathered(proj_weight.astype(BF16), "dp")
    taps_by_row = conv_kernel.transpose(1, 0, 2)

    p, pt, attended, xth, xtl, bh, bl, vpad, q16 = pl.pallas_call(
        forward,
        out_shape=(
            shape((span, padded), F32),
            shape((padded, span), BF16),
            shape((span, depth), BF16),
            shape((wide, taps_a * span), BF16),
            shape((wide, taps_a * span), BF16),
            shape((2 * LANES, taps_a * LANES), BF16),
            shape((2 * LANES, taps_a * LANES), BF16),
            shape((padded, depth), BF16),
            shape((rows_up, depth), BF16),
        ),
        in_specs=[smem, smem, hbm, hbm, hbm],
        out_specs=(whole,) * 9,
        scratch_shapes=[
            pltpu.VMEM((rows, depth), BF16),
            pltpu.VMEM((key_count, depth), BF16),
            pltpu.VMEM((key_count, depth), BF16),
            pltpu.VMEM((rows_up, depth), F32),
            pltpu.VMEM((2 * LANES, taps_a * LANES), BF16),
            pltpu.VMEM((2 * LANES, taps_a * LANES), BF16),
            pltpu.VMEM(((blocks + 1) * rows_up, 2 * LANES), BF16),
            pltpu.VMEM(((blocks + 1) * rows_up, 2 * LANES), BF16),
            pltpu.VMEM(((blocks + 1) * rows_up, taps_a * LANES), F32),
            pltpu.VMEM((wide, depth), BF16),
            pltpu.SemaphoreType.DMA((3,)),
        ],
        compiler_params=vmem,
        cost_estimate=pl.CostEstimate(flops=5 * 10**9, bytes_accessed=10**6, transcendentals=span * padded),
        name="attention_forward",
    )(span_start, taps_by_row, queries, keys, values)

    payload = shape((span + 16, share + LANES), BF16)
    do, ch, cl, *payloads = pl.pallas_call(
        functools.partial(backward_scores, taps_b, up_places, w_places, group_count, few("dp")),
        out_shape=(
            shape((span, depth), BF16),
            shape(((blocks + 1) * span, LANES), BF16),
            shape(((blocks + 1) * span, LANES), BF16),
        ) + (payload,) * group_count,
        in_specs=[whole] * (len(up_arrays) + len(w_arrays) + 5),
        out_specs=(whole,) * (3 + group_count),
        scratch_shapes=[pltpu.VMEM((span, columns), BF16), pltpu.VMEM((depth, columns), BF16)],
        compiler_params=vmem,
        cost_estimate=pl.CostEstimate(flops=2 * 10**9, bytes_accessed=10**6, transcendentals=0),
        name="attention_backward_scores",
    )(*up_arrays, *w_arrays, p, vpad, xth, xtl, attended)

    if few("dp"):
        payloads = payloads[:1] + [swap(payloads[s], "dp", s) for s in range(1, group_count)]
    else:
        sent = lax.all_to_all(jnp.stack(payloads), "dp", 0, 0)
        payloads = [sent[s] for s in range(group_count)]

    query_grad, key_grad, value_grad = pl.pallas_call(
        functools.partial(backward_inputs, rows, taps_a),
        out_shape=(shape(queries.shape, BF16), shape(keys.shape, BF16), shape(values.shape, BF16)),
        in_specs=[smem] + [whole] * 7 + [hbm],
        out_specs=(whole,) * 3,
        scratch_shapes=[
            pltpu.VMEM((key_count, depth), BF16),
            pltpu.VMEM((blocks * (span + 32), taps_a * LANES), F32),
            pltpu.SemaphoreType.DMA((1,)),
        ],
        compiler_params=vmem,
        cost_estimate=pl.CostEstimate(flops=3 * 10**9, bytes_accessed=10**6, transcendentals=0),
        name="attention_backward_inputs",
    )(span_start, do, ch, cl, pt, bh, bl, q16, keys)

    last = up_to(LANES + edge - HALF + half, 16) - 1 - (edge - HALF - half) - LANES
    proj_new, moment_one_new, moment_two_new, kernel_total = pl.pallas_call(
        functools.partial(update, last),
        out_shape=(shape(proj_weight.shape, F32),) * 3 + (shape((taps_a, 1, taps_b), F32),),
        in_specs=[whole] * (group_count + 3),
        out_specs=(whole,) * 4,
        compiler_params=vmem,
        name="projection_update",
    )(*payloads, proj_weight, moment_one, moment_two)
    return (
        query_grad,
        key_grad,
        value_grad,
        kernel_total.transpose(1, 0, 2),
        proj_new,
        moment_one_new,
        moment_two_new,
    )


def solution(mesh):
    heads, rows_of, blocks_of = P("dp", None, "tensor"), P("tensor", None, None), P("tensor", "dp")
    return jax.shard_map(
        shards,
        mesh=mesh,
        in_specs=(heads, heads, heads, rows_of, P("dp"), heads, blocks_of, blocks_of, blocks_of),
        out_specs=(heads, heads, heads, rows_of, blocks_of, blocks_of, blocks_of),
        check_vma=False,
    )
```

```python
import functools
import math

import jax
import jax.numpy as jnp
from jax import lax
from jax.experimental import pallas as pl
from jax.experimental.pallas import tpu as pltpu
from jax.sharding import PartitionSpec as P

beta_one = 0.9
beta_two = 0.95
learn_rate = 0.01
decay_rate = 0.1
adam_eps = 1e-08
bias_one = 1.0 - 0.9**10
bias_two = 1.0 - 0.95**10

LANES = 128
HALF = LANES // 2
F32 = jnp.float32
BF16 = jnp.bfloat16


def dot(left, right, dims=((1,), (0,))):
    return lax.dot_general(left, right, (dims, ((), ())), preferred_element_type=F32)


def split(x):
    high = x.astype(BF16)
    return high, (x - high.astype(F32)).astype(BF16)


def up_to(n, multiple):
    return -(-n // multiple) * multiple


def iota(shape, axis):
    return lax.broadcasted_iota(jnp.int32, shape, axis)


def bands(taps_ref, flipped):
    taps_a, _, taps_b = taps_ref.shape
    half = (taps_b - 1) // 2
    place = iota((2 * LANES, LANES), 0) - iota((2 * LANES, LANES), 1) - (HALF - half)
    out = [jnp.zeros((2 * LANES, LANES), F32) for _ in range(taps_a)]
    for b in range(taps_b):
        here = place == (taps_b - 1 - b if flipped else b)
        for a in range(taps_a):
            out[a] = jnp.where(here, taps_ref[a, 0, b], out[a])
    return out


def fetch(pairs, sems):
    copies = [pltpu.make_async_copy(src, dst, sems.at[n]) for n, (src, dst) in enumerate(pairs)]
    for copy in copies:
        copy.start()
    return copies


def forward(pieces, *refs):
    piece_refs, (first_ref, taps_hbm, q_hbm, k_hbm, v_hbm) = refs[:pieces], refs[pieces : pieces + 5]
    p_ref, o_ref, vpad, q16, q32, pack_ref = refs[pieces + 5 : pieces + 11]
    taps_ref, q_in, k_in, v_in, fh, fl, xh, xl, y, sems = refs[pieces + 11 :]
    taps_a, _, _ = taps_ref.shape
    rows, depth = q_in.shape
    keys = k_in.shape[0]
    span = rows - taps_a + 1
    rows_up = q32.shape[0]
    blocks = keys // LANES
    scale = 1.0 / math.sqrt(depth)
    copies = fetch(
        (
            (taps_hbm, taps_ref),
            (q_hbm.at[0], q_in),
            (k_hbm.at[0], k_in),
            (v_hbm.at[0], v_in),
            (piece_refs[0].at[0], pack_ref.at[pl.ds(0, span)]),
        ),
        sems,
    )
    for n, ref in enumerate(piece_refs[1:]):
        pack_ref[(n + 1) * span : (n + 2) * span] = ref[0]
    q32[...] = jnp.zeros_like(q32)
    vpad[...] = jnp.zeros_like(vpad)
    copies[0].wait()
    for a, f in enumerate(bands(taps_ref, False)):
        cols = pl.ds(a * LANES, LANES)
        fh[:, cols], fl[:, cols] = split(f)
    for copy in copies[1:]:
        copy.wait()
    first = first_ref[0]
    q32[:rows] = q_in[...].astype(F32)
    q_all = q32[...].astype(BF16)
    q16[...] = q_all
    vpad[HALF : HALF + keys] = v_in[...]

    zero = jnp.zeros((rows_up, LANES), BF16)
    for ref in (xh, xl):
        ref[:rows_up, :LANES] = zero
        ref[blocks * rows_up :, LANES:] = zero
    for n in range(blocks):
        x = dot(q_all, k_in[n * LANES : (n + 1) * LANES], ((1,), (1,))) * scale
        key = n * LANES + iota(x.shape, 1)
        pos = first - (taps_a - 1) + iota(x.shape, 0)
        high, low = split(jnp.where(key <= pos, x, 0.0))
        for ref, part in ((xh, high), (xl, low)):
            ref[n * rows_up : (n + 1) * rows_up, LANES:] = part
            ref[(n + 1) * rows_up : (n + 2) * rows_up, :LANES] = part

    for at in range(0, taps_a * LANES, 2 * LANES):
        cols = pl.ds(at, 2 * LANES)
        y[:, cols] = dot(xh[...], fh[:, cols]) + dot(xh[...], fl[:, cols]) + dot(xl[...], fh[:, cols])
    mixed = []
    for w in range(blocks + 1):
        total = None
        for a in range(taps_a):
            start = w * rows_up + taps_a - 1 - a
            term = y[start : start + span, a * LANES : (a + 1) * LANES]
            total = term if total is None else total + term
        mixed.append(total)
    c = jnp.concatenate(mixed, axis=1)
    key = iota(c.shape, 1) - HALF
    live = (key >= 0) & (key <= first + iota(c.shape, 0))
    top = jnp.max(jnp.where(live, c, -jnp.inf), axis=1, keepdims=True)
    terms = jnp.where(live, jnp.exp(c - top), 0.0)
    p = terms / jnp.sum(terms, axis=1, keepdims=True)
    p_ref[...] = p
    o_ref[...] = dot(p.astype(BF16), vpad[...]).astype(BF16)


def forward_turned(taps_a, first_ref, k_hbm, q32, xth_ref, xtl_ref, k_in, kpad, sems):
    keys, depth = k_in.shape
    span = xth_ref.shape[1] // taps_a
    blocks = keys // LANES
    scale = 1.0 / math.sqrt(depth)
    copies = fetch(((k_hbm.at[0], k_in),), sems)
    kpad[...] = jnp.zeros_like(kpad)
    edge = (kpad.shape[0] - keys) // 2
    flip = (iota((LANES, LANES), 0) + iota((LANES, LANES), 1) == LANES - 1).astype(F32).astype(BF16)
    for copy in copies:
        copy.wait()
    first = first_ref[0]
    for n in range(blocks):
        kpad[edge + n * LANES : edge + (n + 1) * LANES] = dot(
            flip, k_in[keys - (n + 1) * LANES : keys - n * LANES]
        ).astype(BF16)
    for a in range(taps_a):
        start = taps_a - 1 - a
        xt = dot(kpad[...], q32[start : start + span].astype(BF16), ((1,), (1,))) * scale
        key = keys - 1 + edge - iota(xt.shape, 0)
        pos = first - a + iota(xt.shape, 1)
        cols = pl.ds(a * LANES, LANES)
        xth_ref[:, cols], xtl_ref[:, cols] = split(jnp.where(key <= pos, xt, 0.0))


def backward_scores(taps_b, up_places, w_places, payloads, by_distance, *refs):
    n_up, n_w = len({p[0] for p in up_places}), len({p[0] for p in w_places})
    up_refs, w_refs, refs = refs[:n_up], refs[n_up : n_up + n_w], refs[n_up + n_w :]
    p_ref, vpad, xth_ref, xtl_ref, o_ref, do_ref, ch, cl, own_ref, own_taps_ref = refs[:10]
    out_refs, (up, w, grad) = refs[10 : 10 + payloads], refs[10 + payloads :]
    span = p_ref.shape[0]
    keys = vpad.shape[0] - LANES
    taps_a = xth_ref.shape[1] // span
    blocks = keys // LANES
    half = (taps_b - 1) // 2
    edge = (xth_ref.shape[0] - keys) // 2

    for refs_in, places, axis, whole in ((up_refs, up_places, "tensor", up), (w_refs, w_places, "dp", w)):
        me = lax.axis_index(axis)
        for n, part, shift, at in places:
            block = refs_in[n][part]
            width = block.shape[1]
            spot = at if shift is None else lax.bitwise_xor(me, shift)
            whole[:, pl.ds(pl.multiple_of(spot * width, width), width)] = block.astype(BF16)
    do = dot(up[...], w[...], ((1,), (1,))).astype(BF16)
    do_ref[...] = do
    grad[...] = dot(o_ref[...], up[...], ((0,), (0,)))
    dp = dot(do, vpad[...], ((1,), (1,)))
    p = p_ref[...]
    high, low = split(p * (dp - jnp.sum(p * dp, axis=1, keepdims=True)))
    for n in range(blocks + 1):
        cols = slice(n * LANES, (n + 1) * LANES)
        here = slice(n * span, (n + 1) * span)
        ch[here] = high[:, cols]
        cl[here] = low[:, cols]

    window = up_to(LANES + edge - HALF + half, 16)
    right = jnp.concatenate([ch[...], cl[...]], axis=1)
    spot = window - 1 - (edge - HALF - half) - iota((window, LANES), 0) - iota((window, LANES), 1)
    wanted = (spot >= 0) & (spot < taps_b)
    sums = []
    for a in range(taps_a):
        total = None
        for ref in (xth_ref, xtl_ref):
            left = jnp.concatenate(
                [ref[n * LANES : n * LANES + window, a * LANES : (a + 1) * LANES] for n in range(blocks, -1, -1)], axis=1
            )
            term = dot(left, right)
            total = term if total is None else total + term
        total = jnp.where(wanted, total[:, :LANES] + total[:, LANES:], 0.0)
        sums.append(jnp.sum(pltpu.roll(total, 0, 1, stride=1, stride_axis=0), axis=0, keepdims=True))
    taps = jnp.concatenate(sums + [jnp.zeros((8 - taps_a, LANES), F32)], axis=0)

    high, low = split(taps)
    mid, low = low, (taps - high.astype(F32) - low.astype(F32)).astype(BF16)
    parts = jnp.concatenate([high.astype(F32), mid.astype(F32)], axis=0).astype(BF16)
    rest = jnp.concatenate([low.astype(F32), jnp.zeros((8, LANES), F32)], axis=0).astype(BF16)
    own_taps_ref[...] = taps
    depth, share = own_ref.shape
    me = lax.axis_index("dp")

    def owned(spot):
        return grad[:, pl.ds(pl.multiple_of(spot * share, share), share)]

    own_ref[...] = owned(me)
    for n, ref in enumerate(out_refs):
        ref[:depth, :share] = owned(lax.bitwise_xor(me, n + 1) if by_distance else n).astype(BF16)
        ref[depth:, :LANES] = parts
        ref[depth:, LANES : 2 * LANES] = rest


def backward_inputs(
    rows, first_ref, taps_hbm, k_hbm, do_ref, ch, cl, p_ref, q16,
    dq_ref, dk_ref, dv_ref,
    taps_ref, k_in, bh, bl, z, sems,
):
    taps_a = taps_ref.shape[0]
    keys, depth = k_in.shape
    rows_up = q16.shape[0]
    span = do_ref.shape[0]
    blocks = keys // LANES
    scale = 1.0 / math.sqrt(depth)
    copies = fetch(((taps_hbm, taps_ref), (k_hbm.at[0], k_in)), sems)
    do = do_ref[...]
    turned = jnp.concatenate([p_ref[:, n * LANES : (n + 1) * LANES].T for n in range(blocks + 1)], axis=0).astype(BF16)
    dv_ref[0] = dot(turned, do)[HALF : HALF + keys].astype(BF16)
    copies[0].wait()
    for a, f in enumerate(bands(taps_ref, True)):
        cols = pl.ds(a * LANES, LANES)
        bh[:, cols], bl[:, cols] = split(f)
    depth_z = z.shape[0] // blocks
    for n in range(blocks):
        left_h = jnp.concatenate([ch[n * span : (n + 1) * span], ch[(n + 1) * span : (n + 2) * span]], axis=1)
        left_l = jnp.concatenate([cl[n * span : (n + 1) * span], cl[(n + 1) * span : (n + 2) * span]], axis=1)
        z[n * depth_z : n * depth_z + 8] = jnp.zeros((8, z.shape[1]), F32)
        z[n * depth_z + 8 + span : (n + 1) * depth_z] = jnp.zeros((depth_z - 8 - span, z.shape[1]), F32)
        for at in range(0, taps_a * LANES, 2 * LANES):
            cols = pl.ds(at, 2 * LANES)
            z[n * depth_z + 8 : n * depth_z + 8 + span, cols] = (
                dot(left_h, bh[:, cols]) + dot(left_h, bl[:, cols]) + dot(left_l, bh[:, cols])
            )
    for copy in copies[1:]:
        copy.wait()
    first = first_ref[0]
    dq = jnp.zeros((rows_up, depth), F32)
    for n in range(blocks):
        total = None
        for a in range(taps_a):
            start = n * depth_z + 8 - (taps_a - 1) + a
            term = z[start : start + rows_up, a * LANES : (a + 1) * LANES]
            total = term if total is None else total + term
        key = n * LANES + iota(total.shape, 1)
        pos = first - (taps_a - 1) + iota(total.shape, 0)
        ds = jnp.where(key <= pos, total, 0.0)
        here = slice(n * LANES, (n + 1) * LANES)
        dq = dq + dot(ds.astype(BF16), k_in[here])
        dk_ref[0, here] = (scale * dot(ds.T.astype(BF16), q16[...])).astype(BF16)
    dq_ref[0] = (scale * dq)[:rows].astype(BF16)


def update(last, count, span, *refs):
    payload_refs, (own_ref, own_taps_ref, w_ref, one_ref, two_ref) = refs[:-9], refs[-9:-4]
    new_ref, one_new_ref, two_new_ref, taps_ref = refs[-4:]
    taps_a, _, taps_b = taps_ref.shape
    depth, share = own_ref.shape
    grad, taps = own_ref[...], own_taps_ref[...]
    for ref in payload_refs:
        grad = grad + ref[:depth, :share].astype(F32)
        parts, rest = ref[depth:, :LANES].astype(F32), ref[depth:, LANES : 2 * LANES].astype(F32)
        taps = taps + (parts[:8] + (parts[8:] + rest[:8]))
    grad = grad / float(count)
    taps = taps / float(count * span)
    lane = iota((8, LANES), 1)
    turned = jnp.zeros((8, LANES), F32)
    for b in range(taps_b):
        turned = jnp.where(lane == b, taps[:, last - b : last - b + 1], turned)
    for a in range(taps_a):
        taps_ref[a] = turned[a : a + 1, :taps_b]
    one = beta_one * one_ref[...] + (1.0 - beta_one) * grad
    two = beta_two * two_ref[...] + (1.0 - beta_two) * grad * grad
    one_new_ref[...] = one
    two_new_ref[...] = two
    old = w_ref[...]
    new_ref[...] = old - learn_rate * ((one / bias_one) / (jnp.sqrt(two / bias_two) + adam_eps) + decay_rate * old)


def swap(x, axis, shift):
    n = lax.axis_size(axis)
    return lax.ppermute(x, axis, [(i, i ^ shift) for i in range(n)])


def few(axis):
    n = lax.axis_size(axis)
    return n <= 8 and n & (n - 1) == 0


def gathered(x, axis):
    if few(axis):
        shifts = range(lax.axis_size(axis))
        return [x] + [swap(x, axis, s) for s in shifts[1:]], [(s, slice(None), s, None) for s in shifts]
    n = lax.axis_size(axis)
    return [lax.all_gather(x, axis)], [(0, i, None, i) for i in range(n)]


def shards(queries, keys, values, conv_kernel, span_start, out_grad, proj_weight, moment_one, moment_two):
    _, rows, depth = queries.shape
    key_count = keys.shape[1]
    _, taps_a, taps_b = conv_kernel.shape
    span = out_grad.shape[1]
    blocks = key_count // LANES
    rows_up = up_to(rows, 16)
    padded = key_count + LANES
    half = (taps_b - 1) // 2
    edge = up_to(HALF + half, 16)
    wide = key_count + 2 * edge
    group_count = lax.axis_size("dp")
    share = proj_weight.shape[1]
    columns = share * group_count
    vmem = pltpu.CompilerParams(vmem_limit_bytes=24 * 2**20)
    whole = pl.BlockSpec(memory_space=pltpu.VMEM)
    hbm = pl.BlockSpec(memory_space=pltpu.HBM)
    shape = jax.ShapeDtypeStruct
    stay = lambda x: pltpu.with_memory_space_constraint(x, pltpu.HBM)
    q_hbm, k_hbm, v_hbm = stay(queries), stay(keys), stay(values)
    taps_hbm = stay(conv_kernel.transpose(1, 0, 2))
    smem = pl.BlockSpec(memory_space=pltpu.SMEM)
    taps_ref = pltpu.SMEM((taps_a, 1, taps_b), F32)
    k_in = pltpu.VMEM((key_count, depth), BF16)

    def cost(flops):
        return pl.CostEstimate(flops=flops, bytes_accessed=10**6, transcendentals=0)

    w_arrays, w_places = gathered(proj_weight, "dp")
    cores_last = few("tensor") and lax.axis_size("tensor") > 2
    pieces = [stay(out_grad)]
    if cores_last:
        pieces += [swap(out_grad, "tensor", s) for s in range(2, lax.axis_size("tensor"), 2)]
    p, attended, vpad, q16, q32, pack = pl.pallas_call(
        functools.partial(forward, len(pieces)),
        out_shape=(
            shape((span, padded), F32),
            shape((span, depth), BF16),
            shape((padded, depth), BF16),
            shape((rows_up, depth), BF16),
            shape((rows_up, depth), F32),
            shape((len(pieces) * span, out_grad.shape[2]), BF16),
        ),
        in_specs=[hbm] + [whole] * (len(pieces) - 1) + [smem] + [hbm] * 4,
        out_specs=(whole,) * 6,
        scratch_shapes=[
            taps_ref,
            pltpu.VMEM((rows, depth), BF16),
            k_in,
            k_in,
            pltpu.VMEM((2 * LANES, taps_a * LANES), BF16),
            pltpu.VMEM((2 * LANES, taps_a * LANES), BF16),
            pltpu.VMEM(((blocks + 1) * rows_up, 2 * LANES), BF16),
            pltpu.VMEM(((blocks + 1) * rows_up, 2 * LANES), BF16),
            pltpu.VMEM(((blocks + 1) * rows_up, taps_a * LANES), F32),
            pltpu.SemaphoreType.DMA((5,)),
        ],
        compiler_params=vmem,
        cost_estimate=cost(5 * 10**9),
        name="attention_forward",
    )(*pieces, span_start, taps_hbm, q_hbm, k_hbm, v_hbm)
    if cores_last:
        up_arrays = [pack, swap(pack, "tensor", 1)]
        up_places = [
            (c, slice(n * span, (n + 1) * span), 2 * n + c, None) for n in range(len(pieces)) for c in (0, 1)
        ]
    else:
        up_arrays, up_places = gathered(out_grad[0], "tensor")
    xth, xtl = pl.pallas_call(
        functools.partial(forward_turned, taps_a),
        out_shape=(shape((wide, taps_a * span), BF16),) * 2,
        in_specs=[smem, hbm, whole],
        out_specs=(whole,) * 2,
        scratch_shapes=[k_in, pltpu.VMEM((wide, depth), BF16), pltpu.SemaphoreType.DMA((1,))],
        compiler_params=vmem,
        cost_estimate=cost(2 * 10**9),
        name="attention_forward_turned",
    )(span_start, k_hbm, q32)

    others = group_count - 1 if few("dp") else group_count
    do, ch, cl, own, own_taps, *payloads = pl.pallas_call(
        functools.partial(backward_scores, taps_b, up_places, w_places, others, few("dp")),
        out_shape=(
            shape((span, depth), BF16),
            shape(((blocks + 1) * span, LANES), BF16),
            shape(((blocks + 1) * span, LANES), BF16),
            shape((depth, share), F32),
            shape((8, LANES), F32),
        ) + (shape((depth + 16, max(share, 2 * LANES)), BF16),) * others,
        in_specs=[whole] * (len(up_arrays) + len(w_arrays) + 5),
        out_specs=(whole,) * (5 + others),
        scratch_shapes=[
            pltpu.VMEM((span, columns), BF16),
            pltpu.VMEM((depth, columns), BF16),
            pltpu.VMEM((depth, columns), F32),
        ],
        compiler_params=vmem,
        cost_estimate=cost(2 * 10**9),
        name="attention_backward_scores",
    )(*up_arrays, *w_arrays, p, vpad, xth, xtl, attended)

    if few("dp"):
        payloads = [swap(payload, "dp", n + 1) for n, payload in enumerate(payloads)]
    else:
        sent = lax.all_to_all(jnp.stack(payloads), "dp", 0, 0)
        payloads = [jnp.where(lax.axis_index("dp") == n, jnp.zeros_like(sent[n]), sent[n]) for n in range(group_count)]

    query_grad, key_grad, value_grad = pl.pallas_call(
        functools.partial(backward_inputs, rows),
        out_shape=(shape(queries.shape, BF16), shape(keys.shape, BF16), shape(values.shape, BF16)),
        in_specs=[smem, hbm, hbm] + [whole] * 5,
        out_specs=(whole,) * 3,
        scratch_shapes=[
            taps_ref,
            k_in,
            pltpu.VMEM((2 * LANES, taps_a * LANES), BF16),
            pltpu.VMEM((2 * LANES, taps_a * LANES), BF16),
            pltpu.VMEM((blocks * (span + 32), taps_a * LANES), F32),
            pltpu.SemaphoreType.DMA((2,)),
        ],
        compiler_params=vmem,
        cost_estimate=cost(3 * 10**9),
        name="attention_backward_inputs",
    )(span_start, taps_hbm, k_hbm, do, ch, cl, p, q16)

    last = up_to(LANES + edge - HALF + half, 16) - 1 - (edge - HALF - half) - LANES
    proj_new, moment_one_new, moment_two_new, kernel_total = pl.pallas_call(
        functools.partial(update, last, group_count, span),
        out_shape=(shape(proj_weight.shape, F32),) * 3 + (shape((taps_a, 1, taps_b), F32),),
        in_specs=[whole] * (len(payloads) + 5),
        out_specs=(whole,) * 4,
        compiler_params=vmem,
        name="projection_update",
    )(*payloads, own, own_taps, proj_weight, moment_one, moment_two)
    return (
        query_grad,
        key_grad,
        value_grad,
        kernel_total.transpose(1, 0, 2),
        proj_new,
        moment_one_new,
        moment_two_new,
    )


def solution(mesh):
    heads, rows_of, blocks_of = P("dp", None, "tensor"), P("tensor", None, None), P("tensor", "dp")
    return jax.shard_map(
        shards,
        mesh=mesh,
        in_specs=(heads, heads, heads, rows_of, P("dp"), heads, blocks_of, blocks_of, blocks_of),
        out_specs=(heads, heads, heads, rows_of, blocks_of, blocks_of, blocks_of),
        check_vma=False,
    )
```

```python
import functools
import math

import jax
import jax.numpy as jnp
from jax import lax
from jax.experimental import pallas as pl
from jax.experimental.pallas import tpu as pltpu
from jax.sharding import PartitionSpec as P

beta_one = 0.9
beta_two = 0.95
learn_rate = 0.01
decay_rate = 0.1
adam_eps = 1e-08
bias_one = 1.0 - 0.9**10
bias_two = 1.0 - 0.95**10

LANES = 128
HALF = LANES // 2
F32 = jnp.float32
BF16 = jnp.bfloat16


def dot(left, right, dims=((1,), (0,))):
    return lax.dot_general(left, right, (dims, ((), ())), preferred_element_type=F32)


def split(x):
    high = x.astype(BF16)
    return high, (x - high.astype(F32)).astype(BF16)


def up_to(n, multiple):
    return -(-n // multiple) * multiple


def iota(shape, axis):
    return lax.broadcasted_iota(jnp.int32, shape, axis)


def bands(taps_ref, flipped):
    taps_a, _, taps_b = taps_ref.shape
    half = (taps_b - 1) // 2
    place = iota((2 * LANES, LANES), 0) - iota((2 * LANES, LANES), 1) - (HALF - half)
    out = [jnp.zeros((2 * LANES, LANES), F32) for _ in range(taps_a)]
    for b in range(taps_b):
        here = place == (taps_b - 1 - b if flipped else b)
        for a in range(taps_a):
            out[a] = jnp.where(here, taps_ref[a, 0, b], out[a])
    return out


def fetch(pairs, sems):
    copies = [pltpu.make_async_copy(src, dst, sems.at[n]) for n, (src, dst) in enumerate(pairs)]
    for copy in copies:
        copy.start()
    return copies


def prepare(taps_hbm, w_hbm, w_ref, fh, fl, taps_ref, w_in, sems):
    copies = fetch(((w_hbm, w_in), (taps_hbm, taps_ref)), sems)
    copies[1].wait()
    for a, f in enumerate(bands(taps_ref, False)):
        cols = pl.ds(a * LANES, LANES)
        fh[:, cols], fl[:, cols] = split(f)
    copies[0].wait()
    w_ref[...] = w_in[...].astype(BF16)


def forward(pieces, taps_a, *refs):
    piece_refs, (first_ref, fh, fl, q_hbm, k_hbm, v_hbm) = refs[:pieces], refs[pieces : pieces + 6]
    p_ref, o_ref, vpad, q16, q32, pack_ref = refs[pieces + 6 : pieces + 12]
    q_in, k_in, v_in, xh, xl, y, sems = refs[pieces + 12 :]
    rows, depth = q_in.shape
    keys = k_in.shape[0]
    span = rows - taps_a + 1
    rows_up = q32.shape[0]
    blocks = keys // LANES
    scale = 1.0 / math.sqrt(depth)
    copies = fetch(
        (
            (q_hbm.at[0], q_in),
            (k_hbm.at[0], k_in),
            (v_hbm.at[0], v_in),
            (piece_refs[0].at[0], pack_ref.at[pl.ds(0, span)]),
        ),
        sems,
    )
    for n, ref in enumerate(piece_refs[1:]):
        pack_ref[(n + 1) * span : (n + 2) * span] = ref[0]
    q32[...] = jnp.zeros_like(q32)
    vpad[...] = jnp.zeros_like(vpad)
    for copy in copies:
        copy.wait()
    first = first_ref[0]
    q32[:rows] = q_in[...].astype(F32)
    q_all = q32[...].astype(BF16)
    q16[...] = q_all
    vpad[HALF : HALF + keys] = v_in[...]

    zero = jnp.zeros((rows_up, LANES), BF16)
    for ref in (xh, xl):
        ref[:rows_up, :LANES] = zero
        ref[blocks * rows_up :, LANES:] = zero
    for n in range(blocks):
        x = dot(q_all, k_in[n * LANES : (n + 1) * LANES], ((1,), (1,))) * scale
        key = n * LANES + iota(x.shape, 1)
        pos = first - (taps_a - 1) + iota(x.shape, 0)
        high, low = split(jnp.where(key <= pos, x, 0.0))
        for ref, part in ((xh, high), (xl, low)):
            ref[n * rows_up : (n + 1) * rows_up, LANES:] = part
            ref[(n + 1) * rows_up : (n + 2) * rows_up, :LANES] = part

    for at in range(0, taps_a * LANES, 2 * LANES):
        cols = pl.ds(at, 2 * LANES)
        y[:, cols] = dot(xh[...], fh[:, cols]) + dot(xh[...], fl[:, cols]) + dot(xl[...], fh[:, cols])
    mixed = []
    for w in range(blocks + 1):
        total = None
        for a in range(taps_a):
            start = w * rows_up + taps_a - 1 - a
            term = y[start : start + span, a * LANES : (a + 1) * LANES]
            total = term if total is None else total + term
        mixed.append(total)
    c = jnp.concatenate(mixed, axis=1)
    key = iota(c.shape, 1) - HALF
    live = (key >= 0) & (key <= first + iota(c.shape, 0))
    top = jnp.max(jnp.where(live, c, -jnp.inf), axis=1, keepdims=True)
    terms = jnp.where(live, jnp.exp(c - top), 0.0)
    p = terms / jnp.sum(terms, axis=1, keepdims=True)
    p_ref[...] = p
    o_ref[...] = dot(p.astype(BF16), vpad[...]).astype(BF16)


def forward_turned(taps_a, first_ref, k_hbm, q32, xth_ref, xtl_ref, k_in, kpad, sems):
    keys, depth = k_in.shape
    span = xth_ref.shape[1] // taps_a
    blocks = keys // LANES
    scale = 1.0 / math.sqrt(depth)
    copies = fetch(((k_hbm.at[0], k_in),), sems)
    kpad[...] = jnp.zeros_like(kpad)
    edge = (kpad.shape[0] - keys) // 2
    flip = (iota((LANES, LANES), 0) + iota((LANES, LANES), 1) == LANES - 1).astype(F32).astype(BF16)
    for copy in copies:
        copy.wait()
    first = first_ref[0]
    for n in range(blocks):
        kpad[edge + n * LANES : edge + (n + 1) * LANES] = dot(
            flip, k_in[keys - (n + 1) * LANES : keys - n * LANES]
        ).astype(BF16)
    for a in range(taps_a):
        start = taps_a - 1 - a
        xt = dot(kpad[...], q32[start : start + span].astype(BF16), ((1,), (1,))) * scale
        key = keys - 1 + edge - iota(xt.shape, 0)
        pos = first - a + iota(xt.shape, 1)
        cols = pl.ds(a * LANES, LANES)
        xth_ref[:, cols], xtl_ref[:, cols] = split(jnp.where(key <= pos, xt, 0.0))


def backward_scores(taps_b, up_places, w_places, payloads, by_distance, *refs):
    n_up, n_w = len({p[0] for p in up_places}), len({p[0] for p in w_places})
    up_refs, w_refs, refs = refs[:n_up], refs[n_up : n_up + n_w], refs[n_up + n_w :]
    p_ref, vpad, xth_ref, xtl_ref, o_ref, do_ref, ch, cl, own_ref, own_taps_ref = refs[:10]
    out_refs, (up, w, grad) = refs[10 : 10 + payloads], refs[10 + payloads :]
    span = p_ref.shape[0]
    keys = vpad.shape[0] - LANES
    taps_a = xth_ref.shape[1] // span
    blocks = keys // LANES
    half = (taps_b - 1) // 2
    edge = (xth_ref.shape[0] - keys) // 2

    for refs_in, places, axis, whole in ((up_refs, up_places, "tensor", up), (w_refs, w_places, "dp", w)):
        me = lax.axis_index(axis)
        for n, part, shift, at in places:
            block = refs_in[n][part]
            width = block.shape[1]
            spot = at if shift is None else lax.bitwise_xor(me, shift)
            whole[:, pl.ds(pl.multiple_of(spot * width, width), width)] = block
    do = dot(up[...], w[...], ((1,), (1,))).astype(BF16)
    do_ref[...] = do
    grad[...] = dot(o_ref[...], up[...], ((0,), (0,)))
    dp = dot(do, vpad[...], ((1,), (1,)))
    p = p_ref[...]
    high, low = split(p * (dp - jnp.sum(p * dp, axis=1, keepdims=True)))
    for n in range(blocks + 1):
        cols = slice(n * LANES, (n + 1) * LANES)
        here = slice(n * span, (n + 1) * span)
        ch[here] = high[:, cols]
        cl[here] = low[:, cols]

    window = up_to(LANES + edge - HALF + half, 16)
    right = jnp.concatenate([ch[...], cl[...]], axis=1)
    spot = window - 1 - (edge - HALF - half) - iota((window, LANES), 0) - iota((window, LANES), 1)
    wanted = (spot >= 0) & (spot < taps_b)
    sums = []
    for a in range(taps_a):
        total = None
        for ref in (xth_ref, xtl_ref):
            left = jnp.concatenate(
                [ref[n * LANES : n * LANES + window, a * LANES : (a + 1) * LANES] for n in range(blocks, -1, -1)], axis=1
            )
            term = dot(left, right)
            total = term if total is None else total + term
        total = jnp.where(wanted, total[:, :LANES] + total[:, LANES:], 0.0)
        sums.append(jnp.sum(pltpu.roll(total, 0, 1, stride=1, stride_axis=0), axis=0, keepdims=True))
    taps = jnp.concatenate(sums + [jnp.zeros((8 - taps_a, LANES), F32)], axis=0)

    high, low = split(taps)
    mid, low = low, (taps - high.astype(F32) - low.astype(F32)).astype(BF16)
    parts = jnp.concatenate([high.astype(F32), mid.astype(F32)], axis=0).astype(BF16)
    rest = jnp.concatenate([low.astype(F32), jnp.zeros((8, LANES), F32)], axis=0).astype(BF16)
    own_taps_ref[...] = taps
    depth, share = own_ref.shape
    me = lax.axis_index("dp")

    def owned(spot):
        return grad[:, pl.ds(pl.multiple_of(spot * share, share), share)]

    own_ref[...] = owned(me)
    for n, ref in enumerate(out_refs):
        ref[:depth, :share] = owned(lax.bitwise_xor(me, n + 1) if by_distance else n).astype(BF16)
        ref[depth:, :LANES] = parts
        ref[depth:, LANES : 2 * LANES] = rest


def backward_inputs(
    rows, first_ref, taps_hbm, k_hbm, do_ref, ch, cl, p_ref, q16,
    dq_ref, dk_ref, dv_ref,
    taps_ref, k_in, bh, bl, z, sems,
):
    taps_a = taps_ref.shape[0]
    keys, depth = k_in.shape
    rows_up = q16.shape[0]
    span = do_ref.shape[0]
    blocks = keys // LANES
    scale = 1.0 / math.sqrt(depth)
    copies = fetch(((taps_hbm, taps_ref), (k_hbm.at[0], k_in)), sems)
    do = do_ref[...]
    turned = jnp.concatenate([p_ref[:, n * LANES : (n + 1) * LANES].T for n in range(blocks + 1)], axis=0).astype(BF16)
    dv_ref[0] = dot(turned, do)[HALF : HALF + keys].astype(BF16)
    copies[0].wait()
    for a, f in enumerate(bands(taps_ref, True)):
        cols = pl.ds(a * LANES, LANES)
        bh[:, cols], bl[:, cols] = split(f)
    depth_z = z.shape[0] // blocks
    for n in range(blocks):
        left_h = jnp.concatenate([ch[n * span : (n + 1) * span], ch[(n + 1) * span : (n + 2) * span]], axis=1)
        left_l = jnp.concatenate([cl[n * span : (n + 1) * span], cl[(n + 1) * span : (n + 2) * span]], axis=1)
        z[n * depth_z : n * depth_z + 8] = jnp.zeros((8, z.shape[1]), F32)
        z[n * depth_z + 8 + span : (n + 1) * depth_z] = jnp.zeros((depth_z - 8 - span, z.shape[1]), F32)
        for at in range(0, taps_a * LANES, 2 * LANES):
            cols = pl.ds(at, 2 * LANES)
            z[n * depth_z + 8 : n * depth_z + 8 + span, cols] = (
                dot(left_h, bh[:, cols]) + dot(left_h, bl[:, cols]) + dot(left_l, bh[:, cols])
            )
    for copy in copies[1:]:
        copy.wait()
    first = first_ref[0]
    dq = jnp.zeros((rows_up, depth), F32)
    for n in range(blocks):
        total = None
        for a in range(taps_a):
            start = n * depth_z + 8 - (taps_a - 1) + a
            term = z[start : start + rows_up, a * LANES : (a + 1) * LANES]
            total = term if total is None else total + term
        key = n * LANES + iota(total.shape, 1)
        pos = first - (taps_a - 1) + iota(total.shape, 0)
        ds = jnp.where(key <= pos, total, 0.0)
        here = slice(n * LANES, (n + 1) * LANES)
        dq = dq + dot(ds.astype(BF16), k_in[here])
        dk_ref[0, here] = (scale * dot(ds.T.astype(BF16), q16[...])).astype(BF16)
    dq_ref[0] = (scale * dq)[:rows].astype(BF16)


def update(last, count, span, *refs):
    payload_refs, (own_ref, own_taps_ref, w_ref, one_ref, two_ref) = refs[:-9], refs[-9:-4]
    new_ref, one_new_ref, two_new_ref, taps_ref = refs[-4:]
    taps_a, _, taps_b = taps_ref.shape
    depth, share = own_ref.shape
    grad, taps = own_ref[...], own_taps_ref[...]
    for ref in payload_refs:
        grad = grad + ref[:depth, :share].astype(F32)
        parts, rest = ref[depth:, :LANES].astype(F32), ref[depth:, LANES : 2 * LANES].astype(F32)
        taps = taps + (parts[:8] + (parts[8:] + rest[:8]))
    grad = grad / float(count)
    taps = taps / float(count * span)
    lane = iota((8, LANES), 1)
    turned = jnp.zeros((8, LANES), F32)
    for b in range(taps_b):
        turned = jnp.where(lane == b, taps[:, last - b : last - b + 1], turned)
    for a in range(taps_a):
        taps_ref[a] = turned[a : a + 1, :taps_b]
    one = beta_one * one_ref[...] + (1.0 - beta_one) * grad
    two = beta_two * two_ref[...] + (1.0 - beta_two) * grad * grad
    one_new_ref[...] = one
    two_new_ref[...] = two
    old = w_ref[...]
    new_ref[...] = old - learn_rate * ((one / bias_one) / (jnp.sqrt(two / bias_two) + adam_eps) + decay_rate * old)


def swap(x, axis, shift):
    n = lax.axis_size(axis)
    return lax.ppermute(x, axis, [(i, i ^ shift) for i in range(n)])


def few(axis):
    n = lax.axis_size(axis)
    return n <= 8 and n & (n - 1) == 0


def gathered(x, axis):
    if few(axis):
        shifts = range(lax.axis_size(axis))
        return [x] + [swap(x, axis, s) for s in shifts[1:]], [(s, slice(None), s, None) for s in shifts]
    n = lax.axis_size(axis)
    return [lax.all_gather(x, axis)], [(0, i, None, i) for i in range(n)]


def shards(queries, keys, values, conv_kernel, span_start, out_grad, proj_weight, moment_one, moment_two):
    _, rows, depth = queries.shape
    key_count = keys.shape[1]
    _, taps_a, taps_b = conv_kernel.shape
    span = out_grad.shape[1]
    blocks = key_count // LANES
    rows_up = up_to(rows, 16)
    padded = key_count + LANES
    half = (taps_b - 1) // 2
    edge = up_to(HALF + half, 16)
    wide = key_count + 2 * edge
    group_count = lax.axis_size("dp")
    share = proj_weight.shape[1]
    columns = share * group_count
    vmem = pltpu.CompilerParams(vmem_limit_bytes=24 * 2**20)
    whole = pl.BlockSpec(memory_space=pltpu.VMEM)
    hbm = pl.BlockSpec(memory_space=pltpu.HBM)
    shape = jax.ShapeDtypeStruct
    stay = lambda x: pltpu.with_memory_space_constraint(x, pltpu.HBM)
    q_hbm, k_hbm, v_hbm = stay(queries), stay(keys), stay(values)
    taps_hbm = stay(conv_kernel.transpose(1, 0, 2))
    smem = pl.BlockSpec(memory_space=pltpu.SMEM)
    taps_ref = pltpu.SMEM((taps_a, 1, taps_b), F32)
    k_in = pltpu.VMEM((key_count, depth), BF16)

    def cost(flops):
        return pl.CostEstimate(flops=flops, bytes_accessed=10**6, transcendentals=0)

    band = shape((2 * LANES, taps_a * LANES), BF16)
    proj_bf, fh, fl = pl.pallas_call(
        prepare,
        out_shape=(shape(proj_weight.shape, BF16), band, band),
        in_specs=[hbm, hbm],
        out_specs=(whole,) * 3,
        scratch_shapes=[taps_ref, pltpu.VMEM(proj_weight.shape, F32), pltpu.SemaphoreType.DMA((2,))],
        compiler_params=vmem,
        cost_estimate=cost(10**9),
        name="prepare",
    )(taps_hbm, stay(proj_weight))
    w_arrays, w_places = gathered(proj_bf, "dp")
    cores_last = few("tensor") and lax.axis_size("tensor") > 2
    pieces = [stay(out_grad)]
    if cores_last:
        pieces += [swap(out_grad, "tensor", s) for s in range(2, lax.axis_size("tensor"), 2)]
    p, attended, vpad, q16, q32, pack = pl.pallas_call(
        functools.partial(forward, len(pieces), taps_a),
        out_shape=(
            shape((span, padded), F32),
            shape((span, depth), BF16),
            shape((padded, depth), BF16),
            shape((rows_up, depth), BF16),
            shape((rows_up, depth), F32),
            shape((len(pieces) * span, out_grad.shape[2]), BF16),
        ),
        in_specs=[hbm] + [whole] * (len(pieces) - 1) + [smem, whole, whole] + [hbm] * 3,
        out_specs=(whole,) * 6,
        scratch_shapes=[
            pltpu.VMEM((rows, depth), BF16),
            k_in,
            k_in,
            pltpu.VMEM(((blocks + 1) * rows_up, 2 * LANES), BF16),
            pltpu.VMEM(((blocks + 1) * rows_up, 2 * LANES), BF16),
            pltpu.VMEM(((blocks + 1) * rows_up, taps_a * LANES), F32),
            pltpu.SemaphoreType.DMA((4,)),
        ],
        compiler_params=vmem,
        cost_estimate=cost(5 * 10**9),
        name="attention_forward",
    )(*pieces, span_start, fh, fl, q_hbm, k_hbm, v_hbm)
    if cores_last:
        up_arrays = [pack, swap(pack, "tensor", 1)]
        up_places = [
            (c, slice(n * span, (n + 1) * span), 2 * n + c, None) for n in range(len(pieces)) for c in (0, 1)
        ]
    else:
        up_arrays, up_places = gathered(out_grad[0], "tensor")
    xth, xtl = pl.pallas_call(
        functools.partial(forward_turned, taps_a),
        out_shape=(shape((wide, taps_a * span), BF16),) * 2,
        in_specs=[smem, hbm, whole],
        out_specs=(whole,) * 2,
        scratch_shapes=[k_in, pltpu.VMEM((wide, depth), BF16), pltpu.SemaphoreType.DMA((1,))],
        compiler_params=vmem,
        cost_estimate=cost(2 * 10**9),
        name="attention_forward_turned",
    )(span_start, k_hbm, q32)

    others = group_count - 1 if few("dp") else group_count
    do, ch, cl, own, own_taps, *payloads = pl.pallas_call(
        functools.partial(backward_scores, taps_b, up_places, w_places, others, few("dp")),
        out_shape=(
            shape((span, depth), BF16),
            shape(((blocks + 1) * span, LANES), BF16),
            shape(((blocks + 1) * span, LANES), BF16),
            shape((depth, share), F32),
            shape((8, LANES), F32),
        ) + (shape((depth + 16, max(share, 2 * LANES)), BF16),) * others,
        in_specs=[whole] * (len(up_arrays) + len(w_arrays) + 5),
        out_specs=(whole,) * (5 + others),
        scratch_shapes=[
            pltpu.VMEM((span, columns), BF16),
            pltpu.VMEM((depth, columns), BF16),
            pltpu.VMEM((depth, columns), F32),
        ],
        compiler_params=vmem,
        cost_estimate=cost(2 * 10**9),
        name="attention_backward_scores",
    )(*up_arrays, *w_arrays, p, vpad, xth, xtl, attended)

    if few("dp"):
        payloads = [swap(payload, "dp", n + 1) for n, payload in enumerate(payloads)]
    else:
        sent = lax.all_to_all(jnp.stack(payloads), "dp", 0, 0)
        payloads = [jnp.where(lax.axis_index("dp") == n, jnp.zeros_like(sent[n]), sent[n]) for n in range(group_count)]

    query_grad, key_grad, value_grad = pl.pallas_call(
        functools.partial(backward_inputs, rows),
        out_shape=(shape(queries.shape, BF16), shape(keys.shape, BF16), shape(values.shape, BF16)),
        in_specs=[smem, hbm, hbm] + [whole] * 5,
        out_specs=(whole,) * 3,
        scratch_shapes=[
            taps_ref,
            k_in,
            pltpu.VMEM((2 * LANES, taps_a * LANES), BF16),
            pltpu.VMEM((2 * LANES, taps_a * LANES), BF16),
            pltpu.VMEM((blocks * (span + 32), taps_a * LANES), F32),
            pltpu.SemaphoreType.DMA((2,)),
        ],
        compiler_params=vmem,
        cost_estimate=cost(3 * 10**9),
        name="attention_backward_inputs",
    )(span_start, taps_hbm, k_hbm, do, ch, cl, p, q16)

    last = up_to(LANES + edge - HALF + half, 16) - 1 - (edge - HALF - half) - LANES
    proj_new, moment_one_new, moment_two_new, kernel_total = pl.pallas_call(
        functools.partial(update, last, group_count, span),
        out_shape=(shape(proj_weight.shape, F32),) * 3 + (shape((taps_a, 1, taps_b), F32),),
        in_specs=[whole] * (len(payloads) + 5),
        out_specs=(whole,) * 4,
        compiler_params=vmem,
        name="projection_update",
    )(*payloads, own, own_taps, proj_weight, moment_one, moment_two)
    return (
        query_grad,
        key_grad,
        value_grad,
        kernel_total.transpose(1, 0, 2),
        proj_new,
        moment_one_new,
        moment_two_new,
    )


def solution(mesh):
    heads, rows_of, blocks_of = P("dp", None, "tensor"), P("tensor", None, None), P("tensor", "dp")
    return jax.shard_map(
        shards,
        mesh=mesh,
        in_specs=(heads, heads, heads, rows_of, P("dp"), heads, blocks_of, blocks_of, blocks_of),
        out_specs=(heads, heads, heads, rows_of, blocks_of, blocks_of, blocks_of),
        check_vma=False,
    )
```

```python
import functools
import math

import jax
import jax.numpy as jnp
from jax import lax
from jax.experimental import pallas as pl
from jax.experimental.pallas import tpu as pltpu
from jax.sharding import PartitionSpec as P

beta_one = 0.9
beta_two = 0.95
learn_rate = 0.01
decay_rate = 0.1
adam_eps = 1e-08
bias_one = 1.0 - 0.9**10
bias_two = 1.0 - 0.95**10

LANES = 128
HALF = LANES // 2
F32 = jnp.float32
BF16 = jnp.bfloat16


def dot(left, right, dims=((1,), (0,))):
    return lax.dot_general(left, right, (dims, ((), ())), preferred_element_type=F32)


def split(x):
    high = x.astype(BF16)
    return high, (x - high.astype(F32)).astype(BF16)


def up_to(n, multiple):
    return -(-n // multiple) * multiple


def iota(shape, axis):
    return lax.broadcasted_iota(jnp.int32, shape, axis)


def bands(taps_ref, flipped):
    taps_a, _, taps_b = taps_ref.shape
    half = (taps_b - 1) // 2
    place = iota((2 * LANES, LANES), 0) - iota((2 * LANES, LANES), 1) - (HALF - half)
    out = [jnp.zeros((2 * LANES, LANES), F32) for _ in range(taps_a)]
    for b in range(taps_b):
        here = place == (taps_b - 1 - b if flipped else b)
        for a in range(taps_a):
            out[a] = jnp.where(here, taps_ref[a, 0, b], out[a])
    return out


def fetch(pairs, sems):
    copies = [pltpu.make_async_copy(src, dst, sems.at[n]) for n, (src, dst) in enumerate(pairs)]
    for copy in copies:
        copy.start()
    return copies


def prepare(taps_hbm, w_hbm, q_hbm, k_hbm, v_hbm, w_ref, fh, fl, q32, q16, k_ref, vpad, taps_ref, w_in, q_in, sems):
    rows = q_in.shape[0]
    keys = k_ref.shape[0]
    copies = fetch(
        (
            (taps_hbm, taps_ref),
            (w_hbm, w_in),
            (q_hbm.at[0], q_in),
            (k_hbm.at[0], k_ref),
            (v_hbm.at[0], vpad.at[pl.ds(HALF, keys)]),
        ),
        sems,
    )
    q32[...] = jnp.zeros_like(q32)
    vpad[:HALF] = jnp.zeros((HALF, vpad.shape[1]), BF16)
    vpad[HALF + keys :] = jnp.zeros((vpad.shape[0] - HALF - keys, vpad.shape[1]), BF16)
    copies[0].wait()
    for a, f in enumerate(bands(taps_ref, False)):
        cols = pl.ds(a * LANES, LANES)
        fh[:, cols], fl[:, cols] = split(f)
    for copy in copies[1:]:
        copy.wait()
    w_ref[...] = w_in[...].astype(BF16)
    q32[:rows] = q_in[...].astype(F32)
    q16[...] = q32[...].astype(BF16)


def forward(pieces, taps_a, *refs):
    piece_refs, (first_ref, fh, fl, q16, k_ref, vpad) = refs[:pieces], refs[pieces : pieces + 6]
    p_ref, o_ref, pack_ref, xh, xl, y = refs[pieces + 6 :]
    keys, depth = k_ref.shape
    span = p_ref.shape[0]
    rows_up = q16.shape[0]
    blocks = keys // LANES
    scale = 1.0 / math.sqrt(depth)
    first = first_ref[0]
    for n, ref in enumerate(piece_refs):
        pack_ref[n * span : (n + 1) * span] = ref[0]
    q_all = q16[...]

    zero = jnp.zeros((rows_up, LANES), BF16)
    for ref in (xh, xl):
        ref[:rows_up, :LANES] = zero
        ref[blocks * rows_up :, LANES:] = zero
    for n in range(blocks):
        x = dot(q_all, k_ref[n * LANES : (n + 1) * LANES], ((1,), (1,))) * scale
        key = n * LANES + iota(x.shape, 1)
        pos = first - (taps_a - 1) + iota(x.shape, 0)
        high, low = split(jnp.where(key <= pos, x, 0.0))
        for ref, part in ((xh, high), (xl, low)):
            ref[n * rows_up : (n + 1) * rows_up, LANES:] = part
            ref[(n + 1) * rows_up : (n + 2) * rows_up, :LANES] = part

    left = jnp.concatenate([xh[...], xh[...], xl[...]], axis=1)
    for at in range(0, taps_a * LANES, 2 * LANES):
        cols = pl.ds(at, 2 * LANES)
        y[:, cols] = dot(left, jnp.concatenate([fh[:, cols], fl[:, cols], fh[:, cols]], axis=0))
    mixed = []
    for w in range(blocks + 1):
        total = None
        for a in range(taps_a):
            start = w * rows_up + taps_a - 1 - a
            term = y[start : start + span, a * LANES : (a + 1) * LANES]
            total = term if total is None else total + term
        mixed.append(total)
    c = jnp.concatenate(mixed, axis=1)
    key = iota(c.shape, 1) - HALF
    live = (key >= 0) & (key <= first + iota(c.shape, 0))
    top = jnp.max(jnp.where(live, c, -jnp.inf), axis=1, keepdims=True)
    terms = jnp.where(live, jnp.exp(c - top), 0.0)
    p = terms / jnp.sum(terms, axis=1, keepdims=True)
    p_ref[...] = p
    o_ref[...] = dot(p.astype(BF16), vpad[...]).astype(BF16)


def forward_turned(taps_a, first_ref, k_ref, q32, xth_ref, xtl_ref, kpad):
    keys, depth = k_ref.shape
    span = xth_ref.shape[1] // taps_a
    blocks = keys // LANES
    scale = 1.0 / math.sqrt(depth)
    kpad[...] = jnp.zeros_like(kpad)
    edge = (kpad.shape[0] - keys) // 2
    flip = (iota((LANES, LANES), 0) + iota((LANES, LANES), 1) == LANES - 1).astype(F32).astype(BF16)
    first = first_ref[0]
    for n in range(blocks):
        kpad[edge + n * LANES : edge + (n + 1) * LANES] = dot(
            flip, k_ref[keys - (n + 1) * LANES : keys - n * LANES]
        ).astype(BF16)
    for a in range(taps_a):
        start = taps_a - 1 - a
        xt = dot(kpad[...], q32[start : start + span].astype(BF16), ((1,), (1,))) * scale
        key = keys - 1 + edge - iota(xt.shape, 0)
        pos = first - a + iota(xt.shape, 1)
        cols = pl.ds(a * LANES, LANES)
        xth_ref[:, cols], xtl_ref[:, cols] = split(jnp.where(key <= pos, xt, 0.0))


def backward_scores(taps_b, up_places, w_places, payloads, by_distance, *refs):
    n_up, n_w = len({p[0] for p in up_places}), len({p[0] for p in w_places})
    up_refs, w_refs, refs = refs[:n_up], refs[n_up : n_up + n_w], refs[n_up + n_w :]
    p_ref, vpad, xth_ref, xtl_ref, o_ref, do_ref, ch, cl, own_ref, own_taps_ref = refs[:10]
    out_refs, (up, w, grad) = refs[10 : 10 + payloads], refs[10 + payloads :]
    span = p_ref.shape[0]
    keys = vpad.shape[0] - LANES
    taps_a = xth_ref.shape[1] // span
    blocks = keys // LANES
    half = (taps_b - 1) // 2
    edge = (xth_ref.shape[0] - keys) // 2

    for refs_in, places, axis, whole in ((up_refs, up_places, "tensor", up), (w_refs, w_places, "dp", w)):
        me = lax.axis_index(axis)
        for n, part, shift, at in places:
            block = refs_in[n][part]
            width = block.shape[1]
            spot = at if shift is None else lax.bitwise_xor(me, shift)
            whole[:, pl.ds(pl.multiple_of(spot * width, width), width)] = block
    do = dot(up[...], w[...], ((1,), (1,))).astype(BF16)
    do_ref[...] = do
    grad[...] = dot(o_ref[...], up[...], ((0,), (0,)))
    dp = dot(do, vpad[...], ((1,), (1,)))
    p = p_ref[...]
    high, low = split(p * (dp - jnp.sum(p * dp, axis=1, keepdims=True)))
    for n in range(blocks + 1):
        cols = slice(n * LANES, (n + 1) * LANES)
        here = slice(n * span, (n + 1) * span)
        ch[here] = high[:, cols]
        cl[here] = low[:, cols]

    window = up_to(LANES + edge - HALF + half, 16)
    right = jnp.concatenate([ch[...], cl[...]], axis=1)
    right = jnp.concatenate([right, right], axis=0)
    spot = window - 1 - (edge - HALF - half) - iota((window, LANES), 0) - iota((window, LANES), 1)
    wanted = (spot >= 0) & (spot < taps_b)
    sums = []
    for a in range(taps_a):
        cols = slice(a * LANES, (a + 1) * LANES)
        left = jnp.concatenate(
            [
                ref[n * LANES : n * LANES + window, cols]
                for ref in (xth_ref, xtl_ref)
                for n in range(blocks, -1, -1)
            ],
            axis=1,
        )
        total = dot(left, right)
        total = jnp.where(wanted, total[:, :LANES] + total[:, LANES:], 0.0)
        sums.append(jnp.sum(pltpu.roll(total, 0, 1, stride=1, stride_axis=0), axis=0, keepdims=True))
    taps = jnp.concatenate(sums + [jnp.zeros((8 - taps_a, LANES), F32)], axis=0)

    high, low = split(taps)
    mid, low = low, (taps - high.astype(F32) - low.astype(F32)).astype(BF16)
    parts = jnp.concatenate([high.astype(F32), mid.astype(F32)], axis=0).astype(BF16)
    rest = jnp.concatenate([low.astype(F32), jnp.zeros((8, LANES), F32)], axis=0).astype(BF16)
    own_taps_ref[...] = taps
    depth, share = own_ref.shape
    me = lax.axis_index("dp")

    def owned(spot):
        return grad[:, pl.ds(pl.multiple_of(spot * share, share), share)]

    own_ref[...] = owned(me)
    for n, ref in enumerate(out_refs):
        ref[:depth, :share] = owned(lax.bitwise_xor(me, n + 1) if by_distance else n).astype(BF16)
        ref[depth:, :LANES] = parts
        ref[depth:, LANES : 2 * LANES] = rest


def backward_inputs(
    rows, first_ref, taps_hbm, k_hbm, do_ref, ch, cl, p_ref, q16,
    dq_ref, dk_ref, dv_ref,
    taps_ref, k_in, bh, bl, z, sems,
):
    taps_a = taps_ref.shape[0]
    keys, depth = k_in.shape
    rows_up = q16.shape[0]
    span = do_ref.shape[0]
    blocks = keys // LANES
    scale = 1.0 / math.sqrt(depth)
    copies = fetch(((taps_hbm, taps_ref), (k_hbm.at[0], k_in)), sems)
    do = do_ref[...]
    turned = jnp.concatenate([p_ref[:, n * LANES : (n + 1) * LANES].T for n in range(blocks + 1)], axis=0).astype(BF16)
    dv_ref[0] = dot(turned, do)[HALF : HALF + keys].astype(BF16)
    copies[0].wait()
    for a, f in enumerate(bands(taps_ref, True)):
        cols = pl.ds(a * LANES, LANES)
        bh[:, cols], bl[:, cols] = split(f)
    depth_z = z.shape[0] // blocks
    for n in range(blocks):
        left_h = jnp.concatenate([ch[n * span : (n + 1) * span], ch[(n + 1) * span : (n + 2) * span]], axis=1)
        left_l = jnp.concatenate([cl[n * span : (n + 1) * span], cl[(n + 1) * span : (n + 2) * span]], axis=1)
        left = jnp.concatenate([left_h, left_h, left_l], axis=1)
        z[n * depth_z : n * depth_z + 8] = jnp.zeros((8, z.shape[1]), F32)
        z[n * depth_z + 8 + span : (n + 1) * depth_z] = jnp.zeros((depth_z - 8 - span, z.shape[1]), F32)
        for at in range(0, taps_a * LANES, 2 * LANES):
            cols = pl.ds(at, 2 * LANES)
            z[n * depth_z + 8 : n * depth_z + 8 + span, cols] = dot(
                left, jnp.concatenate([bh[:, cols], bl[:, cols], bh[:, cols]], axis=0)
            )
    for copy in copies[1:]:
        copy.wait()
    first = first_ref[0]
    dq = jnp.zeros((rows_up, depth), F32)
    for n in range(blocks):
        total = None
        for a in range(taps_a):
            start = n * depth_z + 8 - (taps_a - 1) + a
            term = z[start : start + rows_up, a * LANES : (a + 1) * LANES]
            total = term if total is None else total + term
        key = n * LANES + iota(total.shape, 1)
        pos = first - (taps_a - 1) + iota(total.shape, 0)
        ds = jnp.where(key <= pos, total, 0.0)
        here = slice(n * LANES, (n + 1) * LANES)
        dq = dq + dot(ds.astype(BF16), k_in[here])
        dk_ref[0, here] = (scale * dot(ds.T.astype(BF16), q16[...])).astype(BF16)
    dq_ref[0] = (scale * dq)[:rows].astype(BF16)


def update(last, count, span, *refs):
    payload_refs, (own_ref, own_taps_ref, w_ref, one_ref, two_ref) = refs[:-9], refs[-9:-4]
    new_ref, one_new_ref, two_new_ref, taps_ref = refs[-4:]
    taps_a, _, taps_b = taps_ref.shape
    depth, share = own_ref.shape
    grad, taps = own_ref[...], own_taps_ref[...]
    for ref in payload_refs:
        grad = grad + ref[:depth, :share].astype(F32)
        parts, rest = ref[depth:, :LANES].astype(F32), ref[depth:, LANES : 2 * LANES].astype(F32)
        taps = taps + (parts[:8] + (parts[8:] + rest[:8]))
    grad = grad / float(count)
    taps = taps / float(count * span)
    lane = iota((8, LANES), 1)
    turned = jnp.zeros((8, LANES), F32)
    for b in range(taps_b):
        turned = jnp.where(lane == b, taps[:, last - b : last - b + 1], turned)
    for a in range(taps_a):
        taps_ref[a] = turned[a : a + 1, :taps_b]
    one = beta_one * one_ref[...] + (1.0 - beta_one) * grad
    two = beta_two * two_ref[...] + (1.0 - beta_two) * grad * grad
    one_new_ref[...] = one
    two_new_ref[...] = two
    old = w_ref[...]
    new_ref[...] = old - learn_rate * ((one / bias_one) / (jnp.sqrt(two / bias_two) + adam_eps) + decay_rate * old)


def swap(x, axis, shift):
    n = lax.axis_size(axis)
    return lax.ppermute(x, axis, [(i, i ^ shift) for i in range(n)])


def few(axis):
    n = lax.axis_size(axis)
    return n <= 8 and n & (n - 1) == 0


def gathered(x, axis):
    if few(axis):
        shifts = range(lax.axis_size(axis))
        return [x] + [swap(x, axis, s) for s in shifts[1:]], [(s, slice(None), s, None) for s in shifts]
    n = lax.axis_size(axis)
    return [lax.all_gather(x, axis)], [(0, i, None, i) for i in range(n)]


def shards(queries, keys, values, conv_kernel, span_start, out_grad, proj_weight, moment_one, moment_two):
    _, rows, depth = queries.shape
    key_count = keys.shape[1]
    _, taps_a, taps_b = conv_kernel.shape
    span = out_grad.shape[1]
    blocks = key_count // LANES
    rows_up = up_to(rows, 16)
    padded = key_count + LANES
    half = (taps_b - 1) // 2
    edge = up_to(HALF + half, 16)
    wide = key_count + 2 * edge
    group_count = lax.axis_size("dp")
    share = proj_weight.shape[1]
    columns = share * group_count
    vmem = pltpu.CompilerParams(vmem_limit_bytes=24 * 2**20)
    whole = pl.BlockSpec(memory_space=pltpu.VMEM)
    hbm = pl.BlockSpec(memory_space=pltpu.HBM)
    shape = jax.ShapeDtypeStruct
    stay = lambda x: pltpu.with_memory_space_constraint(x, pltpu.HBM)
    q_hbm, k_hbm, v_hbm = stay(queries), stay(keys), stay(values)
    taps_hbm = stay(conv_kernel.transpose(1, 0, 2))
    smem = pl.BlockSpec(memory_space=pltpu.SMEM)
    taps_ref = pltpu.SMEM((taps_a, 1, taps_b), F32)
    k_in = pltpu.VMEM((key_count, depth), BF16)

    def cost(flops):
        return pl.CostEstimate(flops=flops, bytes_accessed=10**6, transcendentals=0)

    band = shape((2 * LANES, taps_a * LANES), BF16)
    proj_bf, fh, fl, q32, q16, k, vpad = pl.pallas_call(
        prepare,
        out_shape=(
            shape(proj_weight.shape, BF16),
            band,
            band,
            shape((rows_up, depth), F32),
            shape((rows_up, depth), BF16),
            shape((key_count, depth), BF16),
            shape((padded, depth), BF16),
        ),
        in_specs=[hbm] * 5,
        out_specs=(whole,) * 7,
        scratch_shapes=[
            taps_ref,
            pltpu.VMEM(proj_weight.shape, F32),
            pltpu.VMEM((rows, depth), BF16),
            pltpu.SemaphoreType.DMA((5,)),
        ],
        compiler_params=vmem,
        cost_estimate=cost(10**9),
        name="prepare",
    )(taps_hbm, stay(proj_weight), q_hbm, k_hbm, v_hbm)
    w_arrays, w_places = gathered(proj_bf, "dp")
    cores_last = few("tensor") and lax.axis_size("tensor") > 2
    pieces = [stay(out_grad)]
    if cores_last:
        pieces += [swap(out_grad, "tensor", s) for s in range(2, lax.axis_size("tensor"), 2)]
    p, attended, pack = pl.pallas_call(
        functools.partial(forward, len(pieces), taps_a),
        out_shape=(
            shape((span, padded), F32),
            shape((span, depth), BF16),
            shape((len(pieces) * span, out_grad.shape[2]), BF16),
        ),
        in_specs=[whole] * len(pieces) + [smem] + [whole] * 5,
        out_specs=(whole,) * 3,
        scratch_shapes=[
            pltpu.VMEM(((blocks + 1) * rows_up, 2 * LANES), BF16),
            pltpu.VMEM(((blocks + 1) * rows_up, 2 * LANES), BF16),
            pltpu.VMEM(((blocks + 1) * rows_up, taps_a * LANES), F32),
        ],
        compiler_params=vmem,
        cost_estimate=cost(5 * 10**9),
        name="attention_forward",
    )(*pieces, span_start, fh, fl, q16, k, vpad)
    if cores_last:
        up_arrays = [pack, swap(pack, "tensor", 1)]
        up_places = [
            (c, slice(n * span, (n + 1) * span), 2 * n + c, None) for n in range(len(pieces)) for c in (0, 1)
        ]
    else:
        up_arrays, up_places = gathered(out_grad[0], "tensor")
    xth, xtl = pl.pallas_call(
        functools.partial(forward_turned, taps_a),
        out_shape=(shape((wide, taps_a * span), BF16),) * 2,
        in_specs=[smem, whole, whole],
        out_specs=(whole,) * 2,
        scratch_shapes=[pltpu.VMEM((wide, depth), BF16)],
        compiler_params=vmem,
        cost_estimate=cost(2 * 10**9),
        name="attention_forward_turned",
    )(span_start, k, q32)

    others = group_count - 1 if few("dp") else group_count
    do, ch, cl, own, own_taps, *payloads = pl.pallas_call(
        functools.partial(backward_scores, taps_b, up_places, w_places, others, few("dp")),
        out_shape=(
            shape((span, depth), BF16),
            shape(((blocks + 1) * span, LANES), BF16),
            shape(((blocks + 1) * span, LANES), BF16),
            shape((depth, share), F32),
            shape((8, LANES), F32),
        ) + (shape((depth + 16, max(share, 2 * LANES)), BF16),) * others,
        in_specs=[whole] * (len(up_arrays) + len(w_arrays) + 5),
        out_specs=(whole,) * (5 + others),
        scratch_shapes=[
            pltpu.VMEM((span, columns), BF16),
            pltpu.VMEM((depth, columns), BF16),
            pltpu.VMEM((depth, columns), F32),
        ],
        compiler_params=vmem,
        cost_estimate=cost(2 * 10**9),
        name="attention_backward_scores",
    )(*up_arrays, *w_arrays, p, vpad, xth, xtl, attended)

    if few("dp"):
        payloads = [swap(payload, "dp", n + 1) for n, payload in enumerate(payloads)]
    else:
        sent = lax.all_to_all(jnp.stack(payloads), "dp", 0, 0)
        payloads = [jnp.where(lax.axis_index("dp") == n, jnp.zeros_like(sent[n]), sent[n]) for n in range(group_count)]

    query_grad, key_grad, value_grad = pl.pallas_call(
        functools.partial(backward_inputs, rows),
        out_shape=(shape(queries.shape, BF16), shape(keys.shape, BF16), shape(values.shape, BF16)),
        in_specs=[smem, hbm, hbm] + [whole] * 5,
        out_specs=(whole,) * 3,
        scratch_shapes=[
            taps_ref,
            k_in,
            pltpu.VMEM((2 * LANES, taps_a * LANES), BF16),
            pltpu.VMEM((2 * LANES, taps_a * LANES), BF16),
            pltpu.VMEM((blocks * (span + 32), taps_a * LANES), F32),
            pltpu.SemaphoreType.DMA((2,)),
        ],
        compiler_params=vmem,
        cost_estimate=cost(3 * 10**9),
        name="attention_backward_inputs",
    )(span_start, taps_hbm, k_hbm, do, ch, cl, p, q16)

    last = up_to(LANES + edge - HALF + half, 16) - 1 - (edge - HALF - half) - LANES
    proj_new, moment_one_new, moment_two_new, kernel_total = pl.pallas_call(
        functools.partial(update, last, group_count, span),
        out_shape=(shape(proj_weight.shape, F32),) * 3 + (shape((taps_a, 1, taps_b), F32),),
        in_specs=[whole] * (len(payloads) + 5),
        out_specs=(whole,) * 4,
        compiler_params=vmem,
        name="projection_update",
    )(*payloads, own, own_taps, proj_weight, moment_one, moment_two)
    return (
        query_grad,
        key_grad,
        value_grad,
        kernel_total.transpose(1, 0, 2),
        proj_new,
        moment_one_new,
        moment_two_new,
    )


def solution(mesh):
    heads, rows_of, blocks_of = P("dp", None, "tensor"), P("tensor", None, None), P("tensor", "dp")
    return jax.shard_map(
        shards,
        mesh=mesh,
        in_specs=(heads, heads, heads, rows_of, P("dp"), heads, blocks_of, blocks_of, blocks_of),
        out_specs=(heads, heads, heads, rows_of, blocks_of, blocks_of, blocks_of),
        check_vma=False,
    )
```

```python
import functools
import math

import jax
import jax.numpy as jnp
from jax import lax
from jax.experimental import pallas as pl
from jax.experimental.pallas import tpu as pltpu
from jax.sharding import PartitionSpec as P

beta_one = 0.9
beta_two = 0.95
learn_rate = 0.01
decay_rate = 0.1
adam_eps = 1e-08
bias_one = 1.0 - 0.9**10
bias_two = 1.0 - 0.95**10

LANES = 128
HALF = LANES // 2
F32 = jnp.float32
BF16 = jnp.bfloat16


def dot(left, right, dims=((1,), (0,))):
    return lax.dot_general(left, right, (dims, ((), ())), preferred_element_type=F32)


def split(x):
    high = x.astype(BF16)
    return high, (x - high.astype(F32)).astype(BF16)


def up_to(n, multiple):
    return -(-n // multiple) * multiple


def iota(shape, axis):
    return lax.broadcasted_iota(jnp.int32, shape, axis)


def bands(taps_ref, turned):
    taps_a, _, taps_b = taps_ref.shape
    place = iota((LANES, LANES), 0) - iota((LANES, LANES), 1)
    place = -place if turned else place
    out = [jnp.zeros((LANES, LANES), F32) for _ in range(taps_a)]
    for b in range(taps_b):
        here = place == b
        for a in range(taps_a):
            out[a] = jnp.where(here, taps_ref[a, 0, b], out[a])
    pairs = []
    for a in range(0, taps_a, 2):
        both = (out[a], out[a + 1]) if turned else (out[a + 1], out[a])
        pairs.append(jnp.concatenate(split(jnp.concatenate(both, axis=0)), axis=1))
    return pairs


def banded(high, low, bands_ref):
    pairs = bands_ref.shape[1] // (2 * LANES)
    tops = [bands_ref[:, 2 * n * LANES : (2 * n + 1) * LANES] for n in range(pairs)]
    rest = []
    for n in range(0, pairs, 2):
        term = dot(low, jnp.concatenate(tops[n : n + 2], axis=1))
        rest += [term[:, at : at + LANES] for at in range(0, term.shape[1], LANES)]
    out = []
    for n in range(pairs):
        term = dot(high, bands_ref[:, 2 * n * LANES : 2 * (n + 1) * LANES])
        out.append(term[:, :LANES] + term[:, LANES:] + rest[n])
    return out


def fetch(pairs, sems):
    copies = [pltpu.make_async_copy(src, dst, sems.at[n]) for n, (src, dst) in enumerate(pairs)]
    for copy in copies:
        copy.start()
    return copies


def prepare(
    half, taps_hbm, w_hbm, q_hbm, k_hbm, v_hbm,
    w_ref, bands_ref, q32, q16, kwin, vblk,
    taps_ref, w_in, q_in, k_in, v_in, rows32, sems,
):
    rows = q_in.shape[0]
    keys = k_in.shape[0]
    step = LANES - 2 * half
    copies = fetch(
        ((taps_hbm, taps_ref), (w_hbm, w_in), (q_hbm.at[0], q_in), (k_hbm.at[0], k_in), (v_hbm.at[0], v_in)), sems
    )
    q32[...] = jnp.zeros_like(q32)
    rows32[:8] = jnp.zeros((8, LANES), F32)
    rows32[8 + keys :] = jnp.zeros((rows32.shape[0] - 8 - keys, LANES), F32)
    copies[0].wait()
    for n, pair in enumerate(bands(taps_ref, False)):
        bands_ref[:, 2 * n * LANES : 2 * (n + 1) * LANES] = pair
    for copy in copies[1:]:
        copy.wait()
    w_ref[...] = w_in[...].astype(BF16)
    q32[:rows] = q_in[...].astype(F32)
    q16[...] = q32[...].astype(BF16)
    rows32[8 : 8 + keys] = k_in[...].astype(F32)
    for n in range(kwin.shape[0] // LANES):
        start = 8 - half + n * step
        kwin[n * LANES : (n + 1) * LANES] = rows32[start : start + LANES].astype(BF16)
    rows32[8 : 8 + keys] = v_in[...].astype(F32)
    for n in range(vblk.shape[0] // LANES):
        start = 8 + n * step
        block = rows32[start : start + LANES]
        vblk[n * LANES : (n + 1) * LANES] = jnp.where(iota(block.shape, 0) < step, block, 0.0).astype(BF16)


def forward(pieces, taps_a, half, *refs):
    piece_refs, (first_ref, bands_ref, q16, kwin, vblk) = refs[:pieces], refs[pieces : pieces + 5]
    p_ref, o_ref, pack_ref, x32, xh, xl, y = refs[pieces + 5 :]
    depth = kwin.shape[1]
    span = p_ref.shape[0]
    rows_up = q16.shape[0]
    windows = kwin.shape[0] // LANES
    step = LANES - 2 * half
    scale = 1.0 / math.sqrt(depth)
    first = first_ref[0]
    for n, ref in enumerate(piece_refs):
        pack_ref[n * span : (n + 1) * span] = ref[0]

    x32[rows_up:] = jnp.zeros((x32.shape[0] - rows_up, x32.shape[1]), F32)
    for n in range(windows):
        cols = slice(n * LANES, (n + 1) * LANES)
        here = slice(n * rows_up, (n + 1) * rows_up)
        x = dot(q16[...], kwin[cols], ((1,), (1,))) * scale
        key = n * step - half + iota(x.shape, 1)
        pos = first - (taps_a - 1) + iota(x.shape, 0)
        x = jnp.where(key <= pos, x, 0.0)
        x32[:rows_up, cols] = x
        xh[here, :LANES], xl[here, :LANES] = split(x)
        xh[here, LANES:], xl[here, LANES:] = split(x32[1 : 1 + rows_up, cols])

    for n, term in enumerate(banded(xh[...], xl[...], bands_ref)):
        y[:, n * LANES : (n + 1) * LANES] = term
    mixed = []
    for n in range(windows):
        total = None
        for pair in range(taps_a // 2):
            start = n * rows_up + taps_a - 2 - 2 * pair
            term = y[start : start + span, pair * LANES : (pair + 1) * LANES]
            total = term if total is None else total + term
        mixed.append(total)
    c = jnp.concatenate(mixed, axis=1)
    lane = iota((span, LANES), 1)
    row = iota((span, LANES), 0)
    live = jnp.concatenate([(lane < step) & (n * step + lane <= first + row) for n in range(windows)], axis=1)
    top = jnp.max(jnp.where(live, c, -jnp.inf), axis=1, keepdims=True)
    terms = jnp.where(live, jnp.exp(c - top), 0.0)
    p = terms / jnp.sum(terms, axis=1, keepdims=True)
    p_ref[...] = p
    o_ref[...] = dot(p.astype(BF16), vblk[...]).astype(BF16)


def forward_turned(taps_a, half, first_ref, kwin, q32, xth_ref, xtl_ref, kturn):
    depth = kwin.shape[1]
    span = xth_ref.shape[1] // taps_a
    windows = kwin.shape[0] // LANES
    step = LANES - 2 * half
    scale = 1.0 / math.sqrt(depth)
    first = first_ref[0]
    flip = (iota((LANES, LANES), 0) + iota((LANES, LANES), 1) == LANES - 1).astype(F32).astype(BF16)
    for n in range(windows):
        here = slice(n * LANES, (n + 1) * LANES)
        kturn[here] = dot(flip, kwin[here]).astype(BF16)
    lead = LANES - 1 - half - iota((LANES, span), 0) - iota((LANES, span), 1)
    lead = jnp.concatenate([lead + n * step for n in range(windows)], axis=0)
    for a in range(taps_a):
        start = taps_a - 1 - a
        xt = dot(kturn[...], q32[start : start + span].astype(BF16), ((1,), (1,))) * scale
        cols = pl.ds(a * span, span)
        xth_ref[:, cols], xtl_ref[:, cols] = split(jnp.where(lead <= first - a, xt, 0.0))


def backward_scores(up_places, w_places, payloads, by_distance, *refs):
    n_up, n_w = len({p[0] for p in up_places}), len({p[0] for p in w_places})
    up_refs, w_refs, refs = refs[:n_up], refs[n_up : n_up + n_w], refs[n_up + n_w :]
    p_ref, vblk, xth_ref, xtl_ref, o_ref, do_ref, dc_ref, own_ref, own_taps_ref = refs[:9]
    out_refs, (up, w, grad) = refs[9 : 9 + payloads], refs[9 + payloads :]
    span = p_ref.shape[0]
    taps_a = xth_ref.shape[1] // span
    windows = vblk.shape[0] // LANES

    for refs_in, places, axis, whole in ((up_refs, up_places, "tensor", up), (w_refs, w_places, "dp", w)):
        me = lax.axis_index(axis)
        for n, part, shift, at in places:
            block = refs_in[n][part]
            width = block.shape[1]
            spot = at if shift is None else lax.bitwise_xor(me, shift)
            whole[:, pl.ds(pl.multiple_of(spot * width, width), width)] = block
    do = dot(up[...], w[...], ((1,), (1,))).astype(BF16)
    do_ref[...] = do
    grad[...] = dot(o_ref[...], up[...], ((0,), (0,)))
    dp = dot(do, vblk[...], ((1,), (1,)))
    p = p_ref[...]
    dc = p * (dp - jnp.sum(p * dp, axis=1, keepdims=True))
    dc_ref[:8] = jnp.zeros((8, dc.shape[1]), F32)
    dc_ref[8 : 8 + span] = dc
    dc_ref[8 + span :] = jnp.zeros((dc_ref.shape[0] - 8 - span, dc.shape[1]), F32)

    right = jnp.concatenate(
        [jnp.concatenate(split(dc[:, n * LANES : (n + 1) * LANES]), axis=1) for n in range(windows)], axis=0
    )
    right = jnp.concatenate([right, right], axis=0)
    sums = []
    for a in range(taps_a):
        cols = slice(a * span, (a + 1) * span)
        left = jnp.concatenate(
            [ref[n * LANES : (n + 1) * LANES, cols] for ref in (xth_ref, xtl_ref) for n in range(windows)], axis=1
        )
        total = dot(left, right)
        turned = pltpu.roll(total[:, :LANES] + total[:, LANES:], 0, 1, stride=1, stride_axis=0)
        sums.append(jnp.sum(turned, axis=0, keepdims=True))
    taps = jnp.concatenate(sums + [jnp.zeros((8 - taps_a, LANES), F32)], axis=0)

    high, low = split(taps)
    mid, low = low, (taps - high.astype(F32) - low.astype(F32)).astype(BF16)
    parts = jnp.concatenate([high.astype(F32), mid.astype(F32)], axis=0).astype(BF16)
    rest = jnp.concatenate([low.astype(F32), jnp.zeros((8, LANES), F32)], axis=0).astype(BF16)
    own_taps_ref[...] = taps
    depth, share = own_ref.shape
    me = lax.axis_index("dp")

    def owned(spot):
        return grad[:, pl.ds(pl.multiple_of(spot * share, share), share)]

    own_ref[...] = owned(me)
    for n, ref in enumerate(out_refs):
        ref[:depth, :share] = owned(lax.bitwise_xor(me, payloads - n) if by_distance else n).astype(BF16)
        ref[depth:, :LANES] = parts
        ref[depth:, LANES : 2 * LANES] = rest


def backward_inputs(
    rows, keys, first_ref, taps_hbm, do_ref, dc_ref, p_ref, q16, kwin,
    dq_ref, dk_ref, dv_ref,
    taps_ref, bands_ref, left_h, left_l, z, sums, sems,
):
    taps_a, _, taps_b = taps_ref.shape
    half = (taps_b - 1) // 2
    step = LANES - 2 * half
    depth = kwin.shape[1]
    windows = kwin.shape[0] // LANES
    rows_up = q16.shape[0]
    scale = 1.0 / math.sqrt(depth)
    copies = fetch(((taps_hbm, taps_ref),), sems)
    first = first_ref[0]
    do = do_ref[...]
    for n in range(windows):
        cols = slice(n * LANES, (n + 1) * LANES)
        here = slice(n * rows_up, (n + 1) * rows_up)
        left_h[here, :LANES], left_l[here, :LANES] = split(dc_ref[:rows_up, cols])
        left_h[here, LANES:], left_l[here, LANES:] = split(dc_ref[1 : 1 + rows_up, cols])
        sums[n * step : n * step + LANES] = dot(p_ref[:, cols].T.astype(BF16), do)
    dv_ref[0] = sums[:keys].astype(BF16)
    copies[0].wait()
    for n, pair in enumerate(bands(taps_ref, True)):
        bands_ref[:, 2 * n * LANES : 2 * (n + 1) * LANES] = pair
    z[windows * rows_up :] = jnp.zeros((z.shape[0] - windows * rows_up, z.shape[1]), F32)
    for n, term in enumerate(banded(left_h[...], left_l[...], bands_ref)):
        z[: windows * rows_up, n * LANES : (n + 1) * LANES] = term

    sums[...] = jnp.zeros_like(sums)
    dq = jnp.zeros((rows_up, depth), F32)
    for n in range(windows):
        total = None
        for pair in range(taps_a // 2):
            start = n * rows_up + 8 - (taps_a - 1) + 2 * pair
            term = z[start : start + rows_up, pair * LANES : (pair + 1) * LANES]
            total = term if total is None else total + term
        key = n * step - half + iota(total.shape, 1)
        row = iota(total.shape, 0)
        ds = jnp.where((key <= first - (taps_a - 1) + row) & (row < rows), total, 0.0)
        dq = dq + dot(ds.astype(BF16), kwin[n * LANES : (n + 1) * LANES])
        sums[n * step : n * step + LANES] += dot(ds.T.astype(BF16), q16[...])
    dk_ref[0] = (scale * sums[half : half + keys]).astype(BF16)
    dq_ref[0] = (scale * dq)[:rows].astype(BF16)


def update(count, span, *refs):
    payload_refs, (own_ref, own_taps_ref, w_ref, one_ref, two_ref) = refs[:-9], refs[-9:-4]
    new_ref, one_new_ref, two_new_ref, taps_ref = refs[-4:]
    taps_a, _, taps_b = taps_ref.shape
    depth, share = own_ref.shape
    grad, taps = own_ref[...], own_taps_ref[...]
    for ref in payload_refs:
        grad = grad + ref[:depth, :share].astype(F32)
        parts, rest = ref[depth:, :LANES].astype(F32), ref[depth:, LANES : 2 * LANES].astype(F32)
        taps = taps + (parts[:8] + (parts[8:] + rest[:8]))
    grad = grad / float(count)
    taps = taps / float(count * span)
    lane = iota((8, LANES), 1)
    turned = jnp.zeros((8, LANES), F32)
    for b in range(taps_b):
        turned = jnp.where(lane == b, taps[:, LANES - 1 - b : LANES - b], turned)
    for a in range(taps_a):
        taps_ref[a] = turned[a : a + 1, :taps_b]
    one = beta_one * one_ref[...] + (1.0 - beta_one) * grad
    two = beta_two * two_ref[...] + (1.0 - beta_two) * grad * grad
    one_new_ref[...] = one
    two_new_ref[...] = two
    old = w_ref[...]
    new_ref[...] = old - learn_rate * ((one / bias_one) / (jnp.sqrt(two / bias_two) + adam_eps) + decay_rate * old)


def swap(x, axis, shift):
    n = lax.axis_size(axis)
    return lax.ppermute(x, axis, [(i, i ^ shift) for i in range(n)])


def few(axis):
    n = lax.axis_size(axis)
    return n <= 8 and n & (n - 1) == 0


def gathered(x, axis):
    if few(axis):
        shifts = range(lax.axis_size(axis))
        return [x] + [swap(x, axis, s) for s in shifts[1:]], [(s, slice(None), s, None) for s in shifts]
    n = lax.axis_size(axis)
    return [lax.all_gather(x, axis)], [(0, i, None, i) for i in range(n)]


def shards(queries, keys, values, conv_kernel, span_start, out_grad, proj_weight, moment_one, moment_two):
    _, rows, depth = queries.shape
    key_count = keys.shape[1]
    _, taps_a, taps_b = conv_kernel.shape
    span = out_grad.shape[1]
    half = (taps_b - 1) // 2
    step = LANES - 2 * half
    windows = -(-key_count // step)
    rows_up = up_to(rows, 16)
    wide = windows * LANES
    reach = up_to((windows - 1) * step + LANES, 8)
    pairs = taps_a // 2
    group_count = lax.axis_size("dp")
    share = proj_weight.shape[1]
    columns = share * group_count
    vmem = pltpu.CompilerParams(vmem_limit_bytes=24 * 2**20)
    whole = pl.BlockSpec(memory_space=pltpu.VMEM)
    hbm = pl.BlockSpec(memory_space=pltpu.HBM)
    shape = jax.ShapeDtypeStruct
    stay = lambda x: pltpu.with_memory_space_constraint(x, pltpu.HBM)
    q_hbm, k_hbm, v_hbm = stay(queries), stay(keys), stay(values)
    taps_hbm = stay(conv_kernel.transpose(1, 0, 2))
    smem = pl.BlockSpec(memory_space=pltpu.SMEM)
    taps_ref = pltpu.SMEM((taps_a, 1, taps_b), F32)
    k_in = pltpu.VMEM((key_count, depth), BF16)
    band = shape((2 * LANES, 2 * pairs * LANES), BF16)
    sides = pltpu.VMEM((windows * rows_up, 2 * LANES), BF16)

    def cost(flops):
        return pl.CostEstimate(flops=flops, bytes_accessed=10**6, transcendentals=0)

    proj_bf, band_rows, q32, q16, kwin, vblk = pl.pallas_call(
        functools.partial(prepare, half),
        out_shape=(
            shape(proj_weight.shape, BF16),
            band,
            shape((rows_up, depth), F32),
            shape((rows_up, depth), BF16),
            shape((wide, depth), BF16),
            shape((wide, depth), BF16),
        ),
        in_specs=[hbm] * 5,
        out_specs=(whole,) * 6,
        scratch_shapes=[
            taps_ref,
            pltpu.VMEM(proj_weight.shape, F32),
            pltpu.VMEM((rows, depth), BF16),
            k_in,
            k_in,
            pltpu.VMEM((reach + 8, depth), F32),
            pltpu.SemaphoreType.DMA((5,)),
        ],
        compiler_params=vmem,
        cost_estimate=cost(10**9),
        name="prepare",
    )(taps_hbm, stay(proj_weight), q_hbm, k_hbm, v_hbm)
    w_arrays, w_places = gathered(proj_bf, "dp")
    cores_last = few("tensor") and lax.axis_size("tensor") > 2
    pieces = [stay(out_grad)]
    if cores_last:
        pieces += [swap(out_grad, "tensor", s) for s in range(2, lax.axis_size("tensor"), 2)]
    p, attended, pack = pl.pallas_call(
        functools.partial(forward, len(pieces), taps_a, half),
        out_shape=(
            shape((span, wide), F32),
            shape((span, depth), BF16),
            shape((len(pieces) * span, out_grad.shape[2]), BF16),
        ),
        in_specs=[whole] * len(pieces) + [smem] + [whole] * 4,
        out_specs=(whole,) * 3,
        scratch_shapes=[
            pltpu.VMEM((rows_up + 8, wide), F32),
            sides,
            sides,
            pltpu.VMEM((windows * rows_up, pairs * LANES), F32),
        ],
        compiler_params=vmem,
        cost_estimate=cost(5 * 10**9),
        name="attention_forward",
    )(*pieces, span_start, band_rows, q16, kwin, vblk)
    if cores_last:
        up_arrays = [pack, swap(pack, "tensor", 1)]
        up_places = [
            (c, slice(n * span, (n + 1) * span), 2 * n + c, None) for n in range(len(pieces)) for c in (0, 1)
        ]
    else:
        up_arrays, up_places = gathered(out_grad[0], "tensor")
    xth, xtl = pl.pallas_call(
        functools.partial(forward_turned, taps_a, half),
        out_shape=(shape((wide, taps_a * span), BF16),) * 2,
        in_specs=[smem, whole, whole],
        out_specs=(whole,) * 2,
        scratch_shapes=[pltpu.VMEM((wide, depth), BF16)],
        compiler_params=vmem,
        cost_estimate=cost(2 * 10**9),
        name="attention_forward_turned",
    )(span_start, kwin, q32)

    others = group_count - 1 if few("dp") else group_count
    do, dc, own, own_taps, *payloads = pl.pallas_call(
        functools.partial(backward_scores, up_places, w_places, others, few("dp")),
        out_shape=(
            shape((span, depth), BF16),
            shape((rows_up + 8, wide), F32),
            shape((depth, share), F32),
            shape((8, LANES), F32),
        ) + (shape((depth + 16, max(share, 2 * LANES)), BF16),) * others,
        in_specs=[whole] * (len(up_arrays) + len(w_arrays) + 5),
        out_specs=(whole,) * (4 + others),
        scratch_shapes=[
            pltpu.VMEM((span, columns), BF16),
            pltpu.VMEM((depth, columns), BF16),
            pltpu.VMEM((depth, columns), F32),
        ],
        compiler_params=vmem,
        cost_estimate=cost(2 * 10**9),
        name="attention_backward_scores",
    )(*up_arrays, *w_arrays, p, vblk, xth, xtl, attended)

    if few("dp"):
        payloads = [swap(payload, "dp", others - n) for n, payload in enumerate(payloads)]
    else:
        sent = lax.all_to_all(jnp.stack(payloads), "dp", 0, 0)
        payloads = [jnp.where(lax.axis_index("dp") == n, jnp.zeros_like(sent[n]), sent[n]) for n in range(group_count)]

    query_grad, key_grad, value_grad = pl.pallas_call(
        functools.partial(backward_inputs, rows, key_count),
        out_shape=(shape(queries.shape, BF16), shape(keys.shape, BF16), shape(values.shape, BF16)),
        in_specs=[smem, hbm] + [whole] * 5,
        out_specs=(whole,) * 3,
        scratch_shapes=[
            taps_ref,
            pltpu.VMEM(band.shape, BF16),
            sides,
            sides,
            pltpu.VMEM((windows * rows_up + 8, pairs * LANES), F32),
            pltpu.VMEM((reach, depth), F32),
            pltpu.SemaphoreType.DMA((1,)),
        ],
        compiler_params=vmem,
        cost_estimate=cost(3 * 10**9),
        name="attention_backward_inputs",
    )(span_start, taps_hbm, do, dc, p, q16, kwin)

    proj_new, moment_one_new, moment_two_new, kernel_total = pl.pallas_call(
        functools.partial(update, group_count, span),
        out_shape=(shape(proj_weight.shape, F32),) * 3 + (shape((taps_a, 1, taps_b), F32),),
        in_specs=[whole] * (len(payloads) + 5),
        out_specs=(whole,) * 4,
        compiler_params=vmem,
        name="projection_update",
    )(*payloads, own, own_taps, proj_weight, moment_one, moment_two)
    return (
        query_grad,
        key_grad,
        value_grad,
        kernel_total.transpose(1, 0, 2),
        proj_new,
        moment_one_new,
        moment_two_new,
    )


def solution(mesh):
    heads, rows_of, blocks_of = P("dp", None, "tensor"), P("tensor", None, None), P("tensor", "dp")
    return jax.shard_map(
        shards,
        mesh=mesh,
        in_specs=(heads, heads, heads, rows_of, P("dp"), heads, blocks_of, blocks_of, blocks_of),
        out_specs=(heads, heads, heads, rows_of, blocks_of, blocks_of, blocks_of),
        check_vma=False,
    )
```

```python
import functools
import math

import jax
import jax.numpy as jnp
from jax import lax
from jax.experimental import pallas as pl
from jax.experimental.pallas import tpu as pltpu
from jax.sharding import PartitionSpec as P

beta_one = 0.9
beta_two = 0.95
learn_rate = 0.01
decay_rate = 0.1
adam_eps = 1e-08
bias_one = 1.0 - 0.9**10
bias_two = 1.0 - 0.95**10

LANES = 128
F32 = jnp.float32
BF16 = jnp.bfloat16


def dot(left, right, dims=((1,), (0,))):
    return lax.dot_general(left, right, (dims, ((), ())), preferred_element_type=F32)


def split(x):
    high = x.astype(BF16)
    return high, (x - high.astype(F32)).astype(BF16)


def up_to(n, multiple):
    return -(-n // multiple) * multiple


def iota(shape, axis):
    return lax.broadcasted_iota(jnp.int32, shape, axis)


def hold_bands(taps_ref, bands_ref):
    taps_a, _, taps_b = taps_ref.shape
    place = iota((LANES, LANES), 0) - iota((LANES, LANES), 1)
    out = [jnp.zeros((LANES, LANES), F32) for _ in range(taps_a)]
    for b in range(taps_b):
        here = place == b
        for a in range(taps_a):
            out[a] = jnp.where(here, taps_ref[a, 0, b], out[a])
    for a in range(0, taps_a, 2):
        cols = slice(a // 2 * LANES, (a // 2 + 1) * LANES)
        high, low = split(jnp.concatenate((out[a + 1], out[a]), axis=0))
        bands_ref[: 2 * LANES, cols] = high
        bands_ref[2 * LANES : 4 * LANES, cols] = low
        bands_ref[4 * LANES :, cols] = high


def turned_bands(bands_ref):
    pairs = bands_ref.shape[1] // LANES
    rows = []
    for n in range(pairs):
        cols = slice(n * LANES, (n + 1) * LANES)
        parts = [bands_ref[at * LANES : (at + 1) * LANES, cols] for at in (1, 0, 3, 2, 1, 0)]
        rows.append(jnp.concatenate(parts, axis=1))
    return jnp.concatenate(rows, axis=0)


def fetch(pairs, sems):
    copies = [pltpu.make_async_copy(src, dst, sems.at[n]) for n, (src, dst) in enumerate(pairs)]
    for copy in copies:
        copy.start()
    return copies


def prepare(
    half, taps_hbm, w_hbm, q_hbm, k_hbm, v_hbm,
    w_ref, bands_ref, q32, q16, kwin, vblk,
    taps_ref, w_in, q_in, k_in, v_in, rows32, sems,
):
    rows = q_in.shape[0]
    keys = k_in.shape[0]
    step = LANES - 2 * half
    copies = fetch(
        ((taps_hbm, taps_ref), (w_hbm, w_in), (q_hbm.at[0], q_in), (k_hbm.at[0], k_in), (v_hbm.at[0], v_in)), sems
    )
    q32[...] = jnp.zeros_like(q32)
    rows32[:8] = jnp.zeros((8, LANES), F32)
    rows32[8 + keys :] = jnp.zeros((rows32.shape[0] - 8 - keys, LANES), F32)
    copies[0].wait()
    hold_bands(taps_ref, bands_ref)
    for copy in copies[1:]:
        copy.wait()
    w_ref[...] = w_in[...].astype(BF16)
    q32[:rows] = q_in[...].astype(F32)
    q16[...] = q32[...].astype(BF16)
    rows32[8 : 8 + keys] = k_in[...].astype(F32)
    for n in range(kwin.shape[0] // LANES):
        start = 8 - half + n * step
        kwin[n * LANES : (n + 1) * LANES] = rows32[start : start + LANES].astype(BF16)
    rows32[8 : 8 + keys] = v_in[...].astype(F32)
    for n in range(vblk.shape[0] // LANES):
        start = 8 + n * step
        block = rows32[start : start + LANES]
        vblk[n * LANES : (n + 1) * LANES] = jnp.where(iota(block.shape, 0) < step, block, 0.0).astype(BF16)


def forward(pieces, taps_a, half, *refs):
    piece_refs, (first_ref, bands_ref, q16, kwin, vblk) = refs[:pieces], refs[pieces : pieces + 5]
    p_ref, o_ref, pack_ref, x32, xh, xl, y = refs[pieces + 5 :]
    span = p_ref.shape[0]
    rows_up = q16.shape[0]
    windows = kwin.shape[0] // LANES
    step = LANES - 2 * half
    first = first_ref[0]
    for n, ref in enumerate(piece_refs):
        pack_ref[n * span : (n + 1) * span] = ref[0]

    x32[rows_up:] = jnp.zeros((x32.shape[0] - rows_up, x32.shape[1]), F32)
    scores = dot(q16[...], kwin[...], ((1,), (1,))) * (1.0 / math.sqrt(kwin.shape[1]))
    for n in range(windows):
        cols = slice(n * LANES, (n + 1) * LANES)
        here = slice(n * rows_up, (n + 1) * rows_up)
        x = scores[:, cols]
        key = n * step - half + iota(x.shape, 1)
        pos = first - (taps_a - 1) + iota(x.shape, 0)
        x = jnp.where(key <= pos, x, 0.0)
        x32[:rows_up, cols] = x
        xh[here, :LANES], xl[here, :LANES] = split(x)
        xh[here, LANES:], xl[here, LANES:] = split(x32[1 : 1 + rows_up, cols])

    y[...] = dot(jnp.concatenate([xh[...], xh[...], xl[...]], axis=1), bands_ref[...])
    mixed = []
    for n in range(windows):
        total = None
        for pair in range(taps_a // 2):
            start = n * rows_up + taps_a - 2 - 2 * pair
            term = y[start : start + span, pair * LANES : (pair + 1) * LANES]
            total = term if total is None else total + term
        mixed.append(total)
    c = jnp.concatenate(mixed, axis=1)
    lane = iota((span, LANES), 1)
    row = iota((span, LANES), 0)
    live = jnp.concatenate([(lane < step) & (n * step + lane <= first + row) for n in range(windows)], axis=1)
    top = jnp.max(jnp.where(live, c, -jnp.inf), axis=1, keepdims=True)
    terms = jnp.where(live, jnp.exp(c - top), 0.0)
    p = terms * (1.0 / jnp.sum(terms, axis=1, keepdims=True))
    p_ref[...] = p
    o_ref[...] = dot(p.astype(BF16), vblk[...]).astype(BF16)


def forward_turned(taps_a, half, first_ref, kwin, q32, xth_ref, xtl_ref, kturn):
    span = xth_ref.shape[1] // taps_a
    windows = kwin.shape[0] // LANES
    step = LANES - 2 * half
    first = first_ref[0]
    flip = (iota((LANES, LANES), 0) + iota((LANES, LANES), 1) == LANES - 1).astype(F32).astype(BF16)
    for n in range(windows):
        here = slice(n * LANES, (n + 1) * LANES)
        kturn[here] = dot(flip, kwin[here]).astype(BF16)
    lead = LANES - 1 - half - iota((LANES, span), 0) - iota((LANES, span), 1)
    lead = jnp.concatenate([lead + n * step for n in range(windows)], axis=0)
    shifted = jnp.concatenate([q32[taps_a - 1 - a : taps_a - 1 - a + span].astype(BF16) for a in range(taps_a)], axis=0)
    xt = dot(kturn[...], shifted, ((1,), (1,)))
    for a in range(taps_a):
        cols = slice(a * span, (a + 1) * span)
        xth_ref[:, cols], xtl_ref[:, cols] = split(jnp.where(lead <= first - a, xt[:, cols], 0.0))


def backward_scores(up_places, w_places, owners, by_distance, *refs):
    n_up, n_w = len({p[0] for p in up_places}), len({p[0] for p in w_places})
    up_refs, w_refs, refs = refs[:n_up], refs[n_up : n_up + n_w], refs[n_up + n_w :]
    p_ref, vblk, xth_ref, xtl_ref, o_ref, do_ref, dc_ref, own_ref, own_taps_ref = refs[:9]
    out_refs, (up, w, grad) = refs[9 : 9 + len(owners)], refs[9 + len(owners) :]
    span = p_ref.shape[0]
    taps_a = xth_ref.shape[1] // span
    windows = vblk.shape[0] // LANES

    for refs_in, places, axis, whole in ((up_refs, up_places, "tensor", up), (w_refs, w_places, "dp", w)):
        me = lax.axis_index(axis)
        for n, part, shift, at in places:
            block = refs_in[n][part]
            width = block.shape[1]
            spot = at if shift is None else lax.bitwise_xor(me, shift)
            whole[:, pl.ds(pl.multiple_of(spot * width, width), width)] = block
    do = dot(up[...], w[...], ((1,), (1,))).astype(BF16)
    do_ref[...] = do
    grad[...] = dot(o_ref[...], up[...], ((0,), (0,)))
    dp = dot(do, vblk[...], ((1,), (1,)))
    p = p_ref[...]
    dc = p * (dp - jnp.sum(p * dp, axis=1, keepdims=True))
    dc_ref[:8] = jnp.zeros((8, dc.shape[1]), F32)
    dc_ref[8 : 8 + span] = dc
    dc_ref[8 + span :] = jnp.zeros((dc_ref.shape[0] - 8 - span, dc.shape[1]), F32)

    right = jnp.concatenate(
        [jnp.concatenate(split(dc[:, n * LANES : (n + 1) * LANES]), axis=1) for n in range(windows)], axis=0
    )
    right = jnp.concatenate([right, right], axis=0)
    sums = []
    for a in range(taps_a):
        cols = slice(a * span, (a + 1) * span)
        left = jnp.concatenate(
            [ref[n * LANES : (n + 1) * LANES, cols] for ref in (xth_ref, xtl_ref) for n in range(windows)], axis=1
        )
        total = dot(left, right)
        turned = pltpu.roll(total[:, :LANES] + total[:, LANES:], 0, 1, stride=1, stride_axis=0)
        sums.append(jnp.sum(turned, axis=0, keepdims=True))
    taps = jnp.concatenate(sums + [jnp.zeros((8 - taps_a, LANES), F32)], axis=0)

    high, low = split(taps)
    mid, low = low, (taps - high.astype(F32) - low.astype(F32)).astype(BF16)
    aside = pltpu.roll(low.astype(F32), LANES // 2, 1)
    first = jnp.where(iota(aside.shape, 1) < LANES // 2, aside, high.astype(F32))
    parts = jnp.concatenate([first, mid.astype(F32)], axis=0).astype(BF16)
    own_taps_ref[...] = taps
    depth, share = own_ref.shape
    me = lax.axis_index("dp")

    def owned(spot):
        return grad[:, pl.ds(pl.multiple_of(spot * share, share), share)]

    own_ref[...] = owned(me)
    for owner, ref in zip(owners, out_refs, strict=True):
        piece = owned(lax.bitwise_xor(me, owner) if by_distance else owner).astype(BF16)
        for n in range(share // LANES):
            ref[n * depth : (n + 1) * depth] = piece[:, n * LANES : (n + 1) * LANES]
        ref[ref.shape[0] - 16 :] = parts


def backward_inputs(
    rows, keys, taps_a, half, first_ref, bands_ref, do_ref, dc_ref, p_ref, q16, kwin,
    dq_ref, dk_ref, dv_ref,
    left_h, left_l, z, sums,
):
    step = LANES - 2 * half
    depth = kwin.shape[1]
    windows = kwin.shape[0] // LANES
    rows_up = q16.shape[0]
    scale = 1.0 / math.sqrt(depth)
    first = first_ref[0]
    do = do_ref[...]
    for n in range(windows):
        cols = slice(n * LANES, (n + 1) * LANES)
        here = slice(n * rows_up, (n + 1) * rows_up)
        left_h[here, :LANES], left_l[here, :LANES] = split(dc_ref[:rows_up, cols])
        left_h[here, LANES:], left_l[here, LANES:] = split(dc_ref[1 : 1 + rows_up, cols])
        sums[n * step : n * step + LANES] = dot(p_ref[:, cols].astype(BF16).T, do)
    dv_ref[0] = sums[:keys].astype(BF16)
    z[windows * rows_up :] = jnp.zeros((z.shape[0] - windows * rows_up, z.shape[1]), F32)
    left = jnp.concatenate([left_h[...], left_h[...], left_l[...]], axis=1)
    z[: windows * rows_up] = dot(left, turned_bands(bands_ref), ((1,), (1,)))

    lane = iota((rows_up, LANES), 1)
    row = iota((rows_up, LANES), 0)
    scores = []
    for n in range(windows):
        total = None
        for pair in range(taps_a // 2):
            start = n * rows_up + 8 - (taps_a - 1) + 2 * pair
            term = z[start : start + rows_up, pair * LANES : (pair + 1) * LANES]
            total = term if total is None else total + term
        scores.append(total)
    sums[...] = jnp.zeros_like(sums)
    dq = jnp.zeros((rows_up, depth), F32)
    for n, total in enumerate(scores):
        if n + 1 < windows:
            total = jnp.where(lane < step, total, total + pltpu.roll(scores[n + 1], step, 1))
        live = (n * step - half + lane <= first - (taps_a - 1) + row) & (row < rows)
        ds = jnp.where(live & (lane >= 2 * half) if n else live, total, 0.0)
        dq = dq + dot(ds.astype(BF16), kwin[n * LANES : (n + 1) * LANES])
        sums[n * step : n * step + LANES] += dot(ds.astype(BF16).T, q16[...])
    dk_ref[0] = (scale * sums[half : half + keys]).astype(BF16)
    dq_ref[0] = (scale * dq)[:rows].astype(BF16)


def update(count, span, *refs):
    payload_refs, (own_ref, own_taps_ref, w_ref, one_ref, two_ref) = refs[:-9], refs[-9:-4]
    new_ref, one_new_ref, two_new_ref, taps_ref = refs[-4:]
    taps_a, _, taps_b = taps_ref.shape
    depth, share = own_ref.shape
    grad, taps = own_ref[...], own_taps_ref[...]
    for ref in payload_refs:
        piece = [ref[n * depth : (n + 1) * depth] for n in range(share // LANES)]
        grad = grad + jnp.concatenate(piece, axis=1).astype(F32)
        parts = ref[ref.shape[0] - 16 :].astype(F32)
        taps = taps + (parts[:8] + (parts[8:] + pltpu.roll(parts[:8], LANES // 2, 1)))
    grad = grad * (1.0 / count)
    taps = taps * (1.0 / (math.sqrt(depth) * count * span))
    lane = iota((8, LANES), 1)
    turned = jnp.zeros((8, LANES), F32)
    for b in range(taps_b):
        turned = jnp.where(lane == b, taps[:, LANES - 1 - b : LANES - b], turned)
    for a in range(taps_a):
        taps_ref[a] = turned[a : a + 1, :taps_b]
    one = beta_one * one_ref[...] + (1.0 - beta_one) * grad
    two = beta_two * two_ref[...] + (1.0 - beta_two) * grad * grad
    one_new_ref[...] = one
    two_new_ref[...] = two
    old = w_ref[...]
    new_ref[...] = old - learn_rate * ((one * (1.0 / bias_one)) / (jnp.sqrt(two * (1.0 / bias_two)) + adam_eps) + decay_rate * old)


def swap(x, axis, shift):
    n = lax.axis_size(axis)
    return lax.ppermute(x, axis, [(i, i ^ shift) for i in range(n)])


def turns(n):
    return list(range(n // 2, n)) + list(range(n // 2 - 1, 0, -1))


def few(axis):
    n = lax.axis_size(axis)
    return n <= 8 and n & (n - 1) == 0


def gathered(x, axis):
    if few(axis):
        shifts = turns(lax.axis_size(axis))[::-1]
        arrays = [x] + [swap(x, axis, s) for s in shifts]
        return arrays, [(n, slice(None), s, None) for n, s in enumerate([0, *shifts])]
    n = lax.axis_size(axis)
    return [lax.all_gather(x, axis)], [(0, i, None, i) for i in range(n)]


def shards(queries, keys, values, conv_kernel, span_start, out_grad, proj_weight, moment_one, moment_two):
    _, rows, depth = queries.shape
    key_count = keys.shape[1]
    _, taps_a, taps_b = conv_kernel.shape
    span = out_grad.shape[1]
    half = (taps_b - 1) // 2
    step = LANES - 2 * half
    windows = -(-key_count // step)
    rows_up = up_to(rows, 16)
    wide = windows * LANES
    reach = up_to((windows - 1) * step + LANES, 8)
    pairs = taps_a // 2
    group_count = lax.axis_size("dp")
    share = proj_weight.shape[1]
    columns = share * group_count
    vmem = pltpu.CompilerParams(vmem_limit_bytes=24 * 2**20)
    whole = pl.BlockSpec(memory_space=pltpu.VMEM)
    hbm = pl.BlockSpec(memory_space=pltpu.HBM)
    shape = jax.ShapeDtypeStruct
    stay = lambda x: pltpu.with_memory_space_constraint(x, pltpu.HBM)
    q_hbm, k_hbm, v_hbm = stay(queries), stay(keys), stay(values)
    taps_hbm = stay(conv_kernel.transpose(1, 0, 2))
    smem = pl.BlockSpec(memory_space=pltpu.SMEM)
    taps_ref = pltpu.SMEM((taps_a, 1, taps_b), F32)
    k_in = pltpu.VMEM((key_count, depth), BF16)
    band = shape((6 * LANES, pairs * LANES), BF16)
    sides = pltpu.VMEM((windows * rows_up, 2 * LANES), BF16)

    def cost(flops):
        return pl.CostEstimate(flops=flops, bytes_accessed=10**6, transcendentals=0)

    proj_bf, band_rows, q32, q16, kwin, vblk = pl.pallas_call(
        functools.partial(prepare, half),
        out_shape=(
            shape(proj_weight.shape, BF16),
            band,
            shape((rows_up, depth), F32),
            shape((rows_up, depth), BF16),
            shape((wide, depth), BF16),
            shape((wide, depth), BF16),
        ),
        in_specs=[hbm] * 5,
        out_specs=(whole,) * 6,
        scratch_shapes=[
            taps_ref,
            pltpu.VMEM(proj_weight.shape, F32),
            pltpu.VMEM((rows, depth), BF16),
            k_in,
            k_in,
            pltpu.VMEM((reach + 8, depth), F32),
            pltpu.SemaphoreType.DMA((5,)),
        ],
        compiler_params=vmem,
        cost_estimate=cost(10**9),
        name="prepare",
    )(taps_hbm, stay(proj_weight), q_hbm, k_hbm, v_hbm)
    w_arrays, w_places = gathered(proj_bf, "dp")
    cores_last = few("tensor") and lax.axis_size("tensor") > 2
    pieces = [stay(out_grad)]
    if cores_last:
        pieces += [swap(out_grad, "tensor", s) for s in range(2, lax.axis_size("tensor"), 2)]
    p, attended, pack = pl.pallas_call(
        functools.partial(forward, len(pieces), taps_a, half),
        out_shape=(
            shape((span, wide), F32),
            shape((span, depth), BF16),
            shape((len(pieces) * span, out_grad.shape[2]), BF16),
        ),
        in_specs=[whole] * len(pieces) + [smem] + [whole] * 4,
        out_specs=(whole,) * 3,
        scratch_shapes=[
            pltpu.VMEM((rows_up + 8, wide), F32),
            sides,
            sides,
            pltpu.VMEM((windows * rows_up, pairs * LANES), F32),
        ],
        compiler_params=vmem,
        cost_estimate=cost(5 * 10**9),
        name="attention_forward",
    )(*pieces, span_start, band_rows, q16, kwin, vblk)
    if cores_last:
        up_arrays = [pack, swap(pack, "tensor", 1)]
        up_places = [
            (c, slice(n * span, (n + 1) * span), 2 * n + c, None) for n in range(len(pieces)) for c in (0, 1)
        ]
    else:
        up_arrays, up_places = gathered(out_grad[0], "tensor")
    xth, xtl = pl.pallas_call(
        functools.partial(forward_turned, taps_a, half),
        out_shape=(shape((wide, taps_a * span), BF16),) * 2,
        in_specs=[smem, whole, whole],
        out_specs=(whole,) * 2,
        scratch_shapes=[pltpu.VMEM((wide, depth), BF16)],
        compiler_params=vmem,
        cost_estimate=cost(2 * 10**9),
        name="attention_forward_turned",
    )(span_start, kwin, q32)

    owners = turns(group_count) if few("dp") else list(range(group_count))
    others = len(owners)
    do, dc, own, own_taps, *payloads = pl.pallas_call(
        functools.partial(backward_scores, up_places, w_places, owners, few("dp")),
        out_shape=(
            shape((span, depth), BF16),
            shape((rows_up + 8, wide), F32),
            shape((depth, share), F32),
            shape((8, LANES), F32),
        ) + (shape((depth * (share // LANES) + 16, LANES), BF16),) * others,
        in_specs=[whole] * (len(up_arrays) + len(w_arrays) + 5),
        out_specs=(whole,) * (4 + others),
        scratch_shapes=[
            pltpu.VMEM((span, columns), BF16),
            pltpu.VMEM((depth, columns), BF16),
            pltpu.VMEM((depth, columns), F32),
        ],
        compiler_params=vmem,
        cost_estimate=cost(2 * 10**9),
        name="attention_backward_scores",
    )(*up_arrays, *w_arrays, p, vblk, xth, xtl, attended)

    if few("dp"):
        payloads = [swap(payload, "dp", owner) for owner, payload in zip(owners, payloads, strict=True)]
    else:
        sent = lax.all_to_all(jnp.stack(payloads), "dp", 0, 0)
        payloads = [jnp.where(lax.axis_index("dp") == n, jnp.zeros_like(sent[n]), sent[n]) for n in range(group_count)]

    query_grad, key_grad, value_grad = pl.pallas_call(
        functools.partial(backward_inputs, rows, key_count, taps_a, half),
        out_shape=(shape(queries.shape, BF16), shape(keys.shape, BF16), shape(values.shape, BF16)),
        in_specs=[smem] + [whole] * 6,
        out_specs=(whole,) * 3,
        scratch_shapes=[
            sides,
            sides,
            pltpu.VMEM((windows * rows_up + 8, pairs * LANES), F32),
            pltpu.VMEM((reach, depth), F32),
        ],
        compiler_params=vmem,
        cost_estimate=cost(3 * 10**9),
        name="attention_backward_inputs",
    )(span_start, band_rows, do, dc, p, q16, kwin)

    proj_new, moment_one_new, moment_two_new, kernel_total = pl.pallas_call(
        functools.partial(update, group_count, span),
        out_shape=(shape(proj_weight.shape, F32),) * 3 + (shape((taps_a, 1, taps_b), F32),),
        in_specs=[whole] * (len(payloads) + 5),
        out_specs=(whole,) * 4,
        compiler_params=vmem,
        name="projection_update",
    )(*payloads, own, own_taps, proj_weight, moment_one, moment_two)
    return (
        query_grad,
        key_grad,
        value_grad,
        kernel_total.transpose(1, 0, 2),
        proj_new,
        moment_one_new,
        moment_two_new,
    )


def solution(mesh):
    heads, rows_of, blocks_of = P("dp", None, "tensor"), P("tensor", None, None), P("tensor", "dp")
    return jax.shard_map(
        shards,
        mesh=mesh,
        in_specs=(heads, heads, heads, rows_of, P("dp"), heads, blocks_of, blocks_of, blocks_of),
        out_specs=(heads, heads, heads, rows_of, blocks_of, blocks_of, blocks_of),
        check_vma=False,
    )
```

```python
import functools
import math

import jax
import jax.numpy as jnp
from jax import lax
from jax.experimental import pallas as pl
from jax.experimental.pallas import tpu as pltpu
from jax.sharding import PartitionSpec as P

beta_one = 0.9
beta_two = 0.95
learn_rate = 0.01
decay_rate = 0.1
adam_eps = 1e-08
bias_one = 1.0 - 0.9**10
bias_two = 1.0 - 0.95**10

LANES = 128
F32 = jnp.float32
BF16 = jnp.bfloat16


def dot(left, right, dims=((1,), (0,))):
    return lax.dot_general(left, right, (dims, ((), ())), preferred_element_type=F32)


def split(x):
    high = x.astype(BF16)
    return high, (x - high.astype(F32)).astype(BF16)


def up_to(n, multiple):
    return -(-n // multiple) * multiple


def iota(shape, axis):
    return lax.broadcasted_iota(jnp.int32, shape, axis)


def hold_bands(taps_ref, bands_ref):
    taps_a, _, taps_b = taps_ref.shape
    place = iota((LANES, LANES), 0) - iota((LANES, LANES), 1)
    out = [jnp.zeros((LANES, LANES), F32) for _ in range(taps_a)]
    for b in range(taps_b):
        here = place == b
        for a in range(taps_a):
            out[a] = jnp.where(here, taps_ref[a, 0, b], out[a])
    for a in range(0, taps_a, 2):
        cols = slice(a // 2 * LANES, (a // 2 + 1) * LANES)
        high, low = split(jnp.concatenate((out[a + 1], out[a]), axis=0))
        bands_ref[: 2 * LANES, cols] = high
        bands_ref[2 * LANES : 4 * LANES, cols] = low
        bands_ref[4 * LANES :, cols] = high


def turned_bands(bands_ref):
    pairs = bands_ref.shape[1] // LANES
    rows = []
    for n in range(pairs):
        cols = slice(n * LANES, (n + 1) * LANES)
        parts = [bands_ref[at * LANES : (at + 1) * LANES, cols] for at in (1, 0, 3, 2, 1, 0)]
        rows.append(jnp.concatenate(parts, axis=1))
    return jnp.concatenate(rows, axis=0)


def fetch(pairs, sems):
    copies = [pltpu.make_async_copy(src, dst, sems.at[n]) for n, (src, dst) in enumerate(pairs)]
    for copy in copies:
        copy.start()
    return copies


def prepare(
    half, taps_hbm, w_hbm, q_hbm, k_hbm, v_hbm,
    w_ref, bands_ref, q32, q16, kwin, vblk,
    taps_ref, w_in, q_in, k_in, v_in, rows32, sems,
):
    rows = q_in.shape[0]
    keys = k_in.shape[0]
    step = LANES - 2 * half
    copies = fetch(
        ((taps_hbm, taps_ref), (w_hbm, w_in), (q_hbm.at[0], q_in), (k_hbm.at[0], k_in), (v_hbm.at[0], v_in)), sems
    )
    q32[...] = jnp.zeros_like(q32)
    rows32[:8] = jnp.zeros((8, LANES), F32)
    rows32[8 + keys :] = jnp.zeros((rows32.shape[0] - 8 - keys, LANES), F32)
    copies[0].wait()
    hold_bands(taps_ref, bands_ref)
    copies[3].wait()
    rows32[8 : 8 + keys] = k_in[...].astype(F32)
    for n in range(kwin.shape[0] // LANES):
        start = 8 - half + n * step
        kwin[n * LANES : (n + 1) * LANES] = rows32[start : start + LANES].astype(BF16)
    copies[1].wait()
    w_ref[...] = w_in[...].astype(BF16)
    copies[2].wait()
    q32[:rows] = q_in[...].astype(F32)
    q16[...] = q32[...].astype(BF16)
    copies[4].wait()
    rows32[8 : 8 + keys] = v_in[...].astype(F32)
    for n in range(vblk.shape[0] // LANES):
        start = 8 + n * step
        block = rows32[start : start + LANES]
        vblk[n * LANES : (n + 1) * LANES] = jnp.where(iota(block.shape, 0) < step, block, 0.0).astype(BF16)


def forward(pieces, taps_a, half, *refs):
    piece_refs, (first_ref, bands_ref, q16, kwin, vblk) = refs[:pieces], refs[pieces : pieces + 5]
    p_ref, o_ref, pack_ref, x32, xh, xl, y = refs[pieces + 5 :]
    span = p_ref.shape[0]
    rows_up = q16.shape[0]
    windows = kwin.shape[0] // LANES
    step = LANES - 2 * half
    first = first_ref[0]
    for n, ref in enumerate(piece_refs):
        pack_ref[n * span : (n + 1) * span] = ref[0]

    x32[rows_up:] = jnp.zeros((x32.shape[0] - rows_up, x32.shape[1]), F32)
    scores = dot(q16[...], kwin[...], ((1,), (1,))) * (1.0 / math.sqrt(kwin.shape[1]))
    for n in range(windows):
        cols = slice(n * LANES, (n + 1) * LANES)
        here = slice(n * rows_up, (n + 1) * rows_up)
        x = scores[:, cols]
        key = n * step - half + iota(x.shape, 1)
        pos = first - (taps_a - 1) + iota(x.shape, 0)
        x = jnp.where(key <= pos, x, 0.0)
        x32[:rows_up, cols] = x
        xh[here, :LANES], xl[here, :LANES] = split(x)
        xh[here, LANES:], xl[here, LANES:] = split(x32[1 : 1 + rows_up, cols])

    y[...] = dot(jnp.concatenate([xh[...], xh[...], xl[...]], axis=1), bands_ref[...])
    mixed = []
    for n in range(windows):
        total = None
        for pair in range(taps_a // 2):
            start = n * rows_up + taps_a - 2 - 2 * pair
            term = y[start : start + span, pair * LANES : (pair + 1) * LANES]
            total = term if total is None else total + term
        mixed.append(total)
    c = jnp.concatenate(mixed, axis=1)
    lane = iota((span, LANES), 1)
    row = iota((span, LANES), 0)
    live = jnp.concatenate([(lane < step) & (n * step + lane <= first + row) for n in range(windows)], axis=1)
    top = jnp.max(jnp.where(live, c, -jnp.inf), axis=1, keepdims=True)
    terms = jnp.where(live, jnp.exp(c - top), 0.0)
    p = terms * (1.0 / jnp.sum(terms, axis=1, keepdims=True))
    p_ref[...] = p
    o_ref[...] = dot(p.astype(BF16), vblk[...]).astype(BF16)


def forward_turned(taps_a, half, first_ref, kwin, q32, xth_ref, xtl_ref, kturn):
    span = xth_ref.shape[1] // taps_a
    windows = kwin.shape[0] // LANES
    step = LANES - 2 * half
    first = first_ref[0]
    flip = (iota((LANES, LANES), 0) + iota((LANES, LANES), 1) == LANES - 1).astype(F32).astype(BF16)
    for n in range(windows):
        here = slice(n * LANES, (n + 1) * LANES)
        kturn[here] = dot(flip, kwin[here]).astype(BF16)
    lead = LANES - 1 - half - iota((LANES, span), 0) - iota((LANES, span), 1)
    lead = jnp.concatenate([lead + n * step for n in range(windows)], axis=0)
    shifted = jnp.concatenate([q32[taps_a - 1 - a : taps_a - 1 - a + span].astype(BF16) for a in range(taps_a)], axis=0)
    xt = dot(kturn[...], shifted, ((1,), (1,)))
    for a in range(taps_a):
        cols = slice(a * span, (a + 1) * span)
        xth_ref[:, cols], xtl_ref[:, cols] = split(jnp.where(lead <= first - a, xt[:, cols], 0.0))


def backward_scores(up_places, w_places, owners, by_distance, *refs):
    n_up, n_w = len({p[0] for p in up_places}), len({p[0] for p in w_places})
    up_refs, w_refs, refs = refs[:n_up], refs[n_up : n_up + n_w], refs[n_up + n_w :]
    p_ref, vblk, xth_ref, xtl_ref, o_ref, do_ref, dc_ref, own_ref, own_taps_ref = refs[:9]
    out_refs, (up, w, grad) = refs[9 : 9 + len(owners)], refs[9 + len(owners) :]
    span = p_ref.shape[0]
    taps_a = xth_ref.shape[1] // span
    windows = vblk.shape[0] // LANES

    for refs_in, places, axis, whole in ((up_refs, up_places, "tensor", up), (w_refs, w_places, "dp", w)):
        me = lax.axis_index(axis)
        for n, part, shift, at in places:
            block = refs_in[n][part]
            width = block.shape[1]
            spot = at if shift is None else lax.bitwise_xor(me, shift)
            whole[:, pl.ds(pl.multiple_of(spot * width, width), width)] = block
    do = dot(up[...], w[...], ((1,), (1,))).astype(BF16)
    do_ref[...] = do
    grad[...] = dot(o_ref[...], up[...], ((0,), (0,)))
    dp = dot(do, vblk[...], ((1,), (1,)))
    p = p_ref[...]
    dc = p * (dp - jnp.sum(p * dp, axis=1, keepdims=True))
    dc_ref[:8] = jnp.zeros((8, dc.shape[1]), F32)
    dc_ref[8 : 8 + span] = dc
    dc_ref[8 + span :] = jnp.zeros((dc_ref.shape[0] - 8 - span, dc.shape[1]), F32)

    right = jnp.concatenate(
        [jnp.concatenate(split(dc[:, n * LANES : (n + 1) * LANES]), axis=1) for n in range(windows)], axis=0
    )
    right = jnp.concatenate([right, right], axis=0)
    sums = []
    for a in range(taps_a):
        cols = slice(a * span, (a + 1) * span)
        left = jnp.concatenate(
            [ref[n * LANES : (n + 1) * LANES, cols] for ref in (xth_ref, xtl_ref) for n in range(windows)], axis=1
        )
        total = dot(left, right)
        turned = pltpu.roll(total[:, :LANES] + total[:, LANES:], 0, 1, stride=1, stride_axis=0)
        sums.append(jnp.sum(turned, axis=0, keepdims=True))
    taps = jnp.concatenate(sums + [jnp.zeros((8 - taps_a, LANES), F32)], axis=0)

    high, low = split(taps)
    mid, low = low, (taps - high.astype(F32) - low.astype(F32)).astype(BF16)
    aside = pltpu.roll(low.astype(F32), LANES // 2, 1)
    first = jnp.where(iota(aside.shape, 1) < LANES // 2, aside, high.astype(F32))
    parts = jnp.concatenate([first, mid.astype(F32)], axis=0).astype(BF16)
    own_taps_ref[...] = taps
    depth, share = own_ref.shape
    me = lax.axis_index("dp")

    def owned(spot):
        return grad[:, pl.ds(pl.multiple_of(spot * share, share), share)]

    own_ref[...] = owned(me)
    for owner, ref in zip(owners, out_refs, strict=True):
        piece = owned(lax.bitwise_xor(me, owner) if by_distance else owner).astype(BF16)
        for n in range(share // LANES):
            ref[n * depth : (n + 1) * depth] = piece[:, n * LANES : (n + 1) * LANES]
        ref[ref.shape[0] - 16 :] = parts


def backward_inputs(
    rows, keys, taps_a, half, first_ref, bands_ref, do_ref, dc_ref, p_ref, q16, kwin,
    dq_ref, dk_ref, dv_ref,
    left_h, left_l, z, sums,
):
    step = LANES - 2 * half
    depth = kwin.shape[1]
    windows = kwin.shape[0] // LANES
    rows_up = q16.shape[0]
    scale = 1.0 / math.sqrt(depth)
    first = first_ref[0]
    do = do_ref[...]
    for n in range(windows):
        cols = slice(n * LANES, (n + 1) * LANES)
        here = slice(n * rows_up, (n + 1) * rows_up)
        left_h[here, :LANES], left_l[here, :LANES] = split(dc_ref[:rows_up, cols])
        left_h[here, LANES:], left_l[here, LANES:] = split(dc_ref[1 : 1 + rows_up, cols])
        sums[n * step : n * step + LANES] = dot(p_ref[:, cols].astype(BF16).T, do)
    dv_ref[0] = sums[:keys].astype(BF16)
    z[windows * rows_up :] = jnp.zeros((z.shape[0] - windows * rows_up, z.shape[1]), F32)
    left = jnp.concatenate([left_h[...], left_h[...], left_l[...]], axis=1)
    z[: windows * rows_up] = dot(left, turned_bands(bands_ref), ((1,), (1,)))

    lane = iota((rows_up, LANES), 1)
    row = iota((rows_up, LANES), 0)
    scores = []
    for n in range(windows):
        total = None
        for pair in range(taps_a // 2):
            start = n * rows_up + 8 - (taps_a - 1) + 2 * pair
            term = z[start : start + rows_up, pair * LANES : (pair + 1) * LANES]
            total = term if total is None else total + term
        scores.append(total)
    sums[...] = jnp.zeros_like(sums)
    dq = jnp.zeros((rows_up, depth), F32)
    for n, total in enumerate(scores):
        if n + 1 < windows:
            total = jnp.where(lane < step, total, total + pltpu.roll(scores[n + 1], step, 1))
        live = (n * step - half + lane <= first - (taps_a - 1) + row) & (row < rows)
        ds = jnp.where(live & (lane >= 2 * half) if n else live, total, 0.0)
        dq = dq + dot(ds.astype(BF16), kwin[n * LANES : (n + 1) * LANES])
        sums[n * step : n * step + LANES] += dot(ds.astype(BF16).T, q16[...])
    dk_ref[0] = (scale * sums[half : half + keys]).astype(BF16)
    dq_ref[0] = (scale * dq)[:rows].astype(BF16)


def update(count, span, *refs):
    payload_refs, (own_ref, own_taps_ref, w_ref, one_ref, two_ref) = refs[:-9], refs[-9:-4]
    new_ref, one_new_ref, two_new_ref, taps_ref = refs[-4:]
    taps_a, _, taps_b = taps_ref.shape
    depth, share = own_ref.shape
    grad, taps = own_ref[...], own_taps_ref[...]
    for ref in payload_refs:
        piece = [ref[n * depth : (n + 1) * depth] for n in range(share // LANES)]
        grad = grad + jnp.concatenate(piece, axis=1).astype(F32)
        parts = ref[ref.shape[0] - 16 :].astype(F32)
        taps = taps + (parts[:8] + (parts[8:] + pltpu.roll(parts[:8], LANES // 2, 1)))
    grad = grad * (1.0 / count)
    taps = taps * (1.0 / (math.sqrt(depth) * count * span))
    lane = iota((8, LANES), 1)
    turned = jnp.zeros((8, LANES), F32)
    for b in range(taps_b):
        turned = jnp.where(lane == b, taps[:, LANES - 1 - b : LANES - b], turned)
    for a in range(taps_a):
        taps_ref[a] = turned[a : a + 1, :taps_b]
    one = beta_one * one_ref[...] + (1.0 - beta_one) * grad
    two = beta_two * two_ref[...] + (1.0 - beta_two) * grad * grad
    one_new_ref[...] = one
    two_new_ref[...] = two
    old = w_ref[...]
    new_ref[...] = old - learn_rate * ((one * (1.0 / bias_one)) / (jnp.sqrt(two * (1.0 / bias_two)) + adam_eps) + decay_rate * old)


def swap(x, axis, shift):
    n = lax.axis_size(axis)
    return lax.ppermute(x, axis, [(i, i ^ shift) for i in range(n)])


def turns(n):
    return list(range(n // 2, n)) + list(range(n // 2 - 1, 0, -1))


def few(axis):
    n = lax.axis_size(axis)
    return n <= 8 and n & (n - 1) == 0


def gathered(x, axis):
    if few(axis):
        shifts = turns(lax.axis_size(axis))[::-1]
        arrays = [x] + [swap(x, axis, s) for s in shifts]
        return arrays, [(n, slice(None), s, None) for n, s in enumerate([0, *shifts])]
    n = lax.axis_size(axis)
    return [lax.all_gather(x, axis)], [(0, i, None, i) for i in range(n)]


def shards(queries, keys, values, conv_kernel, span_start, out_grad, proj_weight, moment_one, moment_two):
    _, rows, depth = queries.shape
    key_count = keys.shape[1]
    _, taps_a, taps_b = conv_kernel.shape
    span = out_grad.shape[1]
    half = (taps_b - 1) // 2
    step = LANES - 2 * half
    windows = -(-key_count // step)
    rows_up = up_to(rows, 16)
    wide = windows * LANES
    reach = up_to((windows - 1) * step + LANES, 8)
    pairs = taps_a // 2
    group_count = lax.axis_size("dp")
    share = proj_weight.shape[1]
    columns = share * group_count
    vmem = pltpu.CompilerParams(vmem_limit_bytes=24 * 2**20)
    whole = pl.BlockSpec(memory_space=pltpu.VMEM)
    hbm = pl.BlockSpec(memory_space=pltpu.HBM)
    shape = jax.ShapeDtypeStruct
    stay = lambda x: pltpu.with_memory_space_constraint(x, pltpu.HBM)
    q_hbm, k_hbm, v_hbm = stay(queries), stay(keys), stay(values)
    taps_hbm = stay(conv_kernel.transpose(1, 0, 2))
    smem = pl.BlockSpec(memory_space=pltpu.SMEM)
    taps_ref = pltpu.SMEM((taps_a, 1, taps_b), F32)
    k_in = pltpu.VMEM((key_count, depth), BF16)
    band = shape((6 * LANES, pairs * LANES), BF16)
    sides = pltpu.VMEM((windows * rows_up, 2 * LANES), BF16)

    def cost(flops):
        return pl.CostEstimate(flops=flops, bytes_accessed=10**6, transcendentals=0)

    proj_bf, band_rows, q32, q16, kwin, vblk = pl.pallas_call(
        functools.partial(prepare, half),
        out_shape=(
            shape(proj_weight.shape, BF16),
            band,
            shape((rows_up, depth), F32),
            shape((rows_up, depth), BF16),
            shape((wide, depth), BF16),
            shape((wide, depth), BF16),
        ),
        in_specs=[hbm] * 5,
        out_specs=(whole,) * 6,
        scratch_shapes=[
            taps_ref,
            pltpu.VMEM(proj_weight.shape, F32),
            pltpu.VMEM((rows, depth), BF16),
            k_in,
            k_in,
            pltpu.VMEM((reach + 8, depth), F32),
            pltpu.SemaphoreType.DMA((5,)),
        ],
        compiler_params=vmem,
        cost_estimate=cost(10**9),
        name="prepare",
    )(taps_hbm, stay(proj_weight), q_hbm, k_hbm, v_hbm)
    w_arrays, w_places = gathered(proj_bf, "dp")
    cores_last = few("tensor") and lax.axis_size("tensor") > 2
    pieces = [stay(out_grad)]
    if cores_last:
        pieces += [swap(out_grad, "tensor", s) for s in range(2, lax.axis_size("tensor"), 2)]
    p, attended, pack = pl.pallas_call(
        functools.partial(forward, len(pieces), taps_a, half),
        out_shape=(
            shape((span, wide), F32),
            shape((span, depth), BF16),
            shape((len(pieces) * span, out_grad.shape[2]), BF16),
        ),
        in_specs=[whole] * len(pieces) + [smem] + [whole] * 4,
        out_specs=(whole,) * 3,
        scratch_shapes=[
            pltpu.VMEM((rows_up + 8, wide), F32),
            sides,
            sides,
            pltpu.VMEM((windows * rows_up, pairs * LANES), F32),
        ],
        compiler_params=vmem,
        cost_estimate=cost(5 * 10**9),
        name="attention_forward",
    )(*pieces, span_start, band_rows, q16, kwin, vblk)
    if cores_last:
        up_arrays = [pack, swap(pack, "tensor", 1)]
        up_places = [
            (c, slice(n * span, (n + 1) * span), 2 * n + c, None) for n in range(len(pieces)) for c in (0, 1)
        ]
    else:
        up_arrays, up_places = gathered(out_grad[0], "tensor")
    xth, xtl = pl.pallas_call(
        functools.partial(forward_turned, taps_a, half),
        out_shape=(shape((wide, taps_a * span), BF16),) * 2,
        in_specs=[smem, whole, whole],
        out_specs=(whole,) * 2,
        scratch_shapes=[pltpu.VMEM((wide, depth), BF16)],
        compiler_params=vmem,
        cost_estimate=cost(2 * 10**9),
        name="attention_forward_turned",
    )(span_start, kwin, q32)

    owners = list(range(group_count))
    if few("dp"):
        owners = owners[group_count // 2 : 0 : -1] + owners[group_count // 2 + 1 :]
    others = len(owners)
    do, dc, own, own_taps, *payloads = pl.pallas_call(
        functools.partial(backward_scores, up_places, w_places, owners, few("dp")),
        out_shape=(
            shape((span, depth), BF16),
            shape((rows_up + 8, wide), F32),
            shape((depth, share), F32),
            shape((8, LANES), F32),
        ) + (shape((depth * (share // LANES) + 16, LANES), BF16),) * others,
        in_specs=[whole] * (len(up_arrays) + len(w_arrays) + 5),
        out_specs=(whole,) * (4 + others),
        scratch_shapes=[
            pltpu.VMEM((span, columns), BF16),
            pltpu.VMEM((depth, columns), BF16),
            pltpu.VMEM((depth, columns), F32),
        ],
        compiler_params=vmem,
        cost_estimate=cost(2 * 10**9),
        name="attention_backward_scores",
    )(*up_arrays, *w_arrays, p, vblk, xth, xtl, attended)

    if few("dp"):
        payloads = [swap(payload, "dp", owner) for owner, payload in zip(owners, payloads, strict=True)]
    else:
        sent = lax.all_to_all(jnp.stack(payloads), "dp", 0, 0)
        payloads = [jnp.where(lax.axis_index("dp") == n, jnp.zeros_like(sent[n]), sent[n]) for n in range(group_count)]

    query_grad, key_grad, value_grad = pl.pallas_call(
        functools.partial(backward_inputs, rows, key_count, taps_a, half),
        out_shape=(shape(queries.shape, BF16), shape(keys.shape, BF16), shape(values.shape, BF16)),
        in_specs=[smem] + [whole] * 6,
        out_specs=(whole,) * 3,
        scratch_shapes=[
            sides,
            sides,
            pltpu.VMEM((windows * rows_up + 8, pairs * LANES), F32),
            pltpu.VMEM((reach, depth), F32),
        ],
        compiler_params=vmem,
        cost_estimate=cost(3 * 10**9),
        name="attention_backward_inputs",
    )(span_start, band_rows, do, dc, p, q16, kwin)

    proj_new, moment_one_new, moment_two_new, kernel_total = pl.pallas_call(
        functools.partial(update, group_count, span),
        out_shape=(shape(proj_weight.shape, F32),) * 3 + (shape((taps_a, 1, taps_b), F32),),
        in_specs=[whole] * (len(payloads) + 5),
        out_specs=(whole,) * 4,
        compiler_params=vmem,
        name="projection_update",
    )(*payloads, own, own_taps, proj_weight, moment_one, moment_two)
    return (
        query_grad,
        key_grad,
        value_grad,
        kernel_total.transpose(1, 0, 2),
        proj_new,
        moment_one_new,
        moment_two_new,
    )


def solution(mesh):
    heads, rows_of, blocks_of = P("dp", None, "tensor"), P("tensor", None, None), P("tensor", "dp")
    return jax.shard_map(
        shards,
        mesh=mesh,
        in_specs=(heads, heads, heads, rows_of, P("dp"), heads, blocks_of, blocks_of, blocks_of),
        out_specs=(heads, heads, heads, rows_of, blocks_of, blocks_of, blocks_of),
        check_vma=False,
    )
```

```python
import functools
import math

import jax
import jax.numpy as jnp
from jax import lax
from jax.experimental import pallas as pl
from jax.experimental.pallas import tpu as pltpu
from jax.sharding import PartitionSpec as P

beta_one = 0.9
beta_two = 0.95
learn_rate = 0.01
decay_rate = 0.1
adam_eps = 1e-08
bias_one = 1.0 - 0.9**10
bias_two = 1.0 - 0.95**10

LANES = 128
GROUP = 2
F32 = jnp.float32
BF16 = jnp.bfloat16


def dot(left, right, dims=((1,), (0,))):
    return lax.dot_general(left, right, (dims, ((), ())), preferred_element_type=F32)


def split(x):
    high = x.astype(BF16)
    return high, (x - high.astype(F32)).astype(BF16)


def up_to(n, multiple):
    return -(-n // multiple) * multiple


def iota(shape, axis):
    return lax.broadcasted_iota(jnp.int32, shape, axis)


def hold_bands(taps_ref, scale, bands_ref):
    taps_a, _, taps_b = taps_ref.shape
    lane = iota((1, LANES), 1)
    out = []
    for a in range(taps_a):
        row = jnp.zeros((1, LANES), F32)
        for b in range(taps_b):
            row = jnp.where(lane == (LANES - b) % LANES, taps_ref[a, 0, b], row)
        out.append(pltpu.roll(jnp.broadcast_to(row, (LANES, LANES)), 0, 1, stride=1, stride_axis=0))
    height = GROUP * LANES
    for n in range(taps_a // GROUP):
        cols = slice(n * LANES, (n + 1) * LANES)
        high, low = split(jnp.concatenate(out[n * GROUP : (n + 1) * GROUP][::-1], axis=0) * scale)
        bands_ref[:height, cols] = high
        bands_ref[height : 2 * height, cols] = low
        bands_ref[2 * height :, cols] = high


def turned_bands(bands_ref):
    spots = [part * GROUP + at for part in range(3) for at in range(GROUP - 1, -1, -1)]
    rows = []
    for n in range(bands_ref.shape[1] // LANES):
        cols = slice(n * LANES, (n + 1) * LANES)
        rows.append(jnp.concatenate([bands_ref[at * LANES : (at + 1) * LANES, cols] for at in spots], axis=1))
    return jnp.concatenate(rows, axis=0)


def fetch(pairs, sems):
    copies = [pltpu.make_async_copy(src, dst, sems.at[n]) for n, (src, dst) in enumerate(pairs)]
    for copy in copies:
        copy.start()
    return copies


def prepare(
    taps_hbm, w_hbm, q_hbm,
    w_ref, bands_ref, q32, q16,
    taps_ref, w_in, q_in, sems,
):
    rows = q_in.shape[0]
    copies = fetch(((taps_hbm, taps_ref), (w_hbm, w_in), (q_hbm.at[0], q_in)), sems)
    q32[...] = jnp.zeros_like(q32)
    copies[0].wait()
    hold_bands(taps_ref, 1.0 / math.sqrt(q_in.shape[1]), bands_ref)
    copies[1].wait()
    w_ref[...] = w_in[...].astype(BF16)
    copies[2].wait()
    q32[:rows] = q_in[...].astype(F32)
    rows_up = q16.shape[0] // GROUP
    for n in range(GROUP):
        q16[n * rows_up : (n + 1) * rows_up] = q32[n : n + rows_up].astype(BF16)


def by_blocks(rows_ref, out, rows32, start, live):
    rows = rows_ref.shape[1]
    rows32[:8] = jnp.zeros((8, LANES), F32)
    rows32[8 : 8 + rows] = rows_ref[0].astype(F32)
    rows32[8 + rows :] = jnp.zeros((rows32.shape[0] - 8 - rows, LANES), F32)
    count = out.shape[0] // LANES
    step = (rows32.shape[0] - 8 - LANES) // (count - 1)
    for n in range(count):
        block = rows32[8 + start + n * step : 8 + start + n * step + LANES]
        if live < LANES:
            block = jnp.where(iota(block.shape, 0) < live, block, 0.0)
        out[n * LANES : (n + 1) * LANES] = block.astype(BF16)


def forward(pieces, taps_a, half, *refs):
    piece_refs, (first_ref, bands_ref, q16, k_ref) = refs[:pieces], refs[pieces : pieces + 4]
    p_ref, kwin, pack_ref, rows32, xh, xl, y = refs[pieces + 4 :]
    span = p_ref.shape[0]
    rows_up = q16.shape[0] // GROUP
    windows = kwin.shape[0] // LANES
    step = LANES - 2 * half
    first = first_ref[0]
    for n, ref in enumerate(piece_refs):
        pack_ref[n * span : (n + 1) * span] = ref[0]

    by_blocks(k_ref, kwin, rows32, -half, LANES)

    scores = dot(q16[...], kwin[...], ((1,), (1,)))
    pos = first - (taps_a - 1) + iota((rows_up, LANES), 0) - iota((rows_up, LANES), 1)
    for n in range(windows):
        here = slice(n * rows_up, (n + 1) * rows_up)
        for at in range(GROUP):
            x = scores[at * rows_up : (at + 1) * rows_up, n * LANES : (n + 1) * LANES]
            cols = slice(at * LANES, (at + 1) * LANES)
            xh[here, cols], xl[here, cols] = split(jnp.where(pos >= n * step - half - at, x, 0.0))

    y[...] = dot(jnp.concatenate([xh[...], xh[...], xl[...]], axis=1), bands_ref[...])
    mixed = []
    for n in range(windows):
        total = None
        for group in range(taps_a // GROUP):
            start = n * rows_up + taps_a - GROUP * (group + 1)
            term = y[start : start + span, group * LANES : (group + 1) * LANES]
            total = term if total is None else total + term
        mixed.append(total)
    c = jnp.concatenate(mixed, axis=1)
    lane = iota((span, LANES), 1)
    row = iota((span, LANES), 0)
    live = jnp.concatenate([(lane < step) & (n * step + lane <= first + row) for n in range(windows)], axis=1)
    c = jnp.where(live, c, -jnp.inf)
    terms = jnp.exp(c - jnp.max(c, axis=1, keepdims=True))
    p = terms * (1.0 / jnp.sum(terms, axis=1, keepdims=True))
    p_ref[...] = p


def forward_turned(taps_a, half, first_ref, kwin, q32, p_ref, v_ref, xth_ref, xtl_ref, vblk, o_ref, kturn, rows32):
    span = xth_ref.shape[1] // taps_a
    windows = kwin.shape[0] // LANES
    step = LANES - 2 * half
    first = first_ref[0]
    by_blocks(v_ref, vblk, rows32, 0, step)
    o_ref[...] = dot(p_ref[...].astype(BF16), vblk[...]).astype(BF16)
    flip = (iota((LANES, LANES), 0) + iota((LANES, LANES), 1) == LANES - 1).astype(F32).astype(BF16)
    for n in range(windows):
        here = slice(n * LANES, (n + 1) * LANES)
        kturn[here] = dot(flip, kwin[here]).astype(BF16)
    lead = LANES - 1 - half - iota((LANES, span), 0) - iota((LANES, span), 1)
    lead = jnp.concatenate([lead + n * step for n in range(windows)], axis=0)
    shifted = jnp.concatenate([q32[taps_a - 1 - a : taps_a - 1 - a + span].astype(BF16) for a in range(taps_a)], axis=0)
    xt = dot(kturn[...], shifted, ((1,), (1,)))
    for a in range(taps_a):
        cols = slice(a * span, (a + 1) * span)
        xth_ref[:, cols], xtl_ref[:, cols] = split(jnp.where(lead <= first - a, xt[:, cols], 0.0))


def backward_scores(up_places, w_places, owners, by_distance, *refs):
    n_up, n_w = len({p[0] for p in up_places}), len({p[0] for p in w_places})
    up_refs, w_refs, refs = refs[:n_up], refs[n_up : n_up + n_w], refs[n_up + n_w :]
    p_ref, vblk, xth_ref, xtl_ref, o_ref, do_ref, own_ref, own_taps_ref = refs[:8]
    out_refs, (up, grad) = refs[8 : 8 + len(owners)], refs[8 + len(owners) :]
    span = p_ref.shape[0]
    taps_a = xth_ref.shape[1] // span
    windows = vblk.shape[0] // LANES

    def columns(places, axis):
        me = lax.axis_index(axis)
        return [(n, part, at if shift is None else lax.bitwise_xor(me, shift)) for n, part, shift, at in places]

    for n, part, spot in columns(up_places, "tensor"):
        block = up_refs[n][part]
        width = block.shape[1]
        up[:, pl.ds(pl.multiple_of(spot * width, width), width)] = block
    do = None
    for n, part, spot in columns(w_places, "dp"):
        block = w_refs[n][part]
        width = block.shape[1]
        term = dot(up[:, pl.ds(pl.multiple_of(spot * width, width), width)], block, ((1,), (1,)))
        do = term if do is None else do + term
    do = do.astype(BF16)
    do_ref[...] = do
    grad[...] = dot(o_ref[...], up[...], ((0,), (0,)))
    dc = scores_grad(p_ref[...], do, vblk[...])

    right = jnp.concatenate(
        [jnp.concatenate(split(dc[:, n * LANES : (n + 1) * LANES]), axis=1) for n in range(windows)], axis=0
    )
    right = jnp.concatenate([right, right], axis=0)
    sums = []
    for a in range(taps_a):
        cols = slice(a * span, (a + 1) * span)
        left = jnp.concatenate(
            [ref[n * LANES : (n + 1) * LANES, cols] for ref in (xth_ref, xtl_ref) for n in range(windows)], axis=1
        )
        total = dot(left, right)
        turned = pltpu.roll(total[:, :LANES] + total[:, LANES:], 0, 1, stride=1, stride_axis=0)
        sums.append(jnp.sum(turned, axis=0, keepdims=True))
    taps = jnp.concatenate(sums + [jnp.zeros((8 - taps_a, LANES), F32)], axis=0)

    high, low = split(taps)
    mid, low = low, (taps - high.astype(F32) - low.astype(F32)).astype(BF16)
    aside = pltpu.roll(low.astype(F32), LANES // 2, 1)
    first = jnp.where(iota(aside.shape, 1) < LANES // 2, aside, high.astype(F32))
    parts = jnp.concatenate([first, mid.astype(F32)], axis=0).astype(BF16)
    own_taps_ref[...] = taps
    depth, share = own_ref.shape
    me = lax.axis_index("dp")

    def owned(spot):
        return grad[:, pl.ds(pl.multiple_of(spot * share, share), share)]

    own_ref[...] = owned(me)
    for owner, ref in zip(owners, out_refs, strict=True):
        piece = owned(lax.bitwise_xor(me, owner) if by_distance else owner).astype(BF16)
        for n in range(share // LANES):
            ref[n * depth : (n + 1) * depth] = piece[:, n * LANES : (n + 1) * LANES]
        ref[ref.shape[0] - 16 :] = parts


def scores_grad(p, do, vblk):
    dp = dot(do, vblk, ((1,), (1,)))
    return p * (dp - jnp.sum(p * dp, axis=1, keepdims=True))


def backward_inputs(
    rows, keys, taps_a, half, first_ref, bands_ref, do_ref, p_ref, vblk, q16, kwin,
    dq_ref, dk_ref, dv_ref,
    dc_ref, left_h, left_l, z, sums,
):
    step = LANES - 2 * half
    depth = kwin.shape[1]
    windows = kwin.shape[0] // LANES
    rows_up = q16.shape[0] // GROUP
    scale = 1.0 / math.sqrt(depth)
    first = first_ref[0]
    do = do_ref[...]
    span = do.shape[0]
    dc_ref[:8] = jnp.zeros((8, dc_ref.shape[1]), F32)
    dc_ref[8 : 8 + span] = scores_grad(p_ref[...], do, vblk[...])
    dc_ref[8 + span :] = jnp.zeros((dc_ref.shape[0] - 8 - span, dc_ref.shape[1]), F32)
    for n in range(windows):
        cols = slice(n * LANES, (n + 1) * LANES)
        here = slice(n * rows_up, (n + 1) * rows_up)
        for at in range(GROUP):
            there = slice(at * LANES, (at + 1) * LANES)
            left_h[here, there], left_l[here, there] = split(dc_ref[at : at + rows_up, cols])
        sums[n * step : n * step + LANES] = dot(p_ref[:, cols].astype(BF16).T, do)
    dv_ref[0] = sums[:keys].astype(BF16)
    z[windows * rows_up :] = jnp.zeros((z.shape[0] - windows * rows_up, z.shape[1]), F32)
    left = jnp.concatenate([left_h[...], left_h[...], left_l[...]], axis=1)
    z[: windows * rows_up] = dot(left, turned_bands(bands_ref), ((1,), (1,)))

    lane = iota((rows_up, LANES), 1)
    row = iota((rows_up, LANES), 0)
    scores = []
    for n in range(windows):
        total = None
        for group in range(taps_a // GROUP):
            start = n * rows_up + 8 - (taps_a - 1) + GROUP * group
            term = z[start : start + rows_up, group * LANES : (group + 1) * LANES]
            total = term if total is None else total + term
        scores.append(total)
    sums[...] = jnp.zeros_like(sums)
    dq = jnp.zeros((rows_up, depth), F32)
    for n, total in enumerate(scores):
        if n + 1 < windows:
            total = jnp.where(lane < step, total, total + pltpu.roll(scores[n + 1], step, 1))
        live = (n * step - half + lane <= first - (taps_a - 1) + row) & (row < rows)
        ds = jnp.where(live & (lane >= 2 * half) if n else live, total * (1.0 / scale), 0.0)
        dq = dq + dot(ds.astype(BF16), kwin[n * LANES : (n + 1) * LANES])
        sums[n * step : n * step + LANES] += dot(ds.astype(BF16).T, q16[:rows_up])
    dk_ref[0] = (scale * sums[half : half + keys]).astype(BF16)
    dq_ref[0] = (scale * dq)[:rows].astype(BF16)


def update(count, span, *refs):
    payload_refs, (own_ref, own_taps_ref, w_ref, one_ref, two_ref) = refs[:-9], refs[-9:-4]
    new_ref, one_new_ref, two_new_ref, taps_ref = refs[-4:]
    taps_a, _, taps_b = taps_ref.shape
    depth, share = own_ref.shape
    grad, taps = own_ref[...], own_taps_ref[...]
    for ref in payload_refs:
        piece = [ref[n * depth : (n + 1) * depth] for n in range(share // LANES)]
        grad = grad + jnp.concatenate(piece, axis=1).astype(F32)
        parts = ref[ref.shape[0] - 16 :].astype(F32)
        taps = taps + (parts[:8] + (parts[8:] + pltpu.roll(parts[:8], LANES // 2, 1)))
    grad = grad * (1.0 / count)
    taps = taps * (1.0 / (math.sqrt(depth) * count * span))
    lane = iota((8, LANES), 1)
    turned = jnp.zeros((8, LANES), F32)
    for b in range(taps_b):
        turned = jnp.where(lane == b, taps[:, LANES - 1 - b : LANES - b], turned)
    for a in range(taps_a):
        taps_ref[a] = turned[a : a + 1, :taps_b]
    one = beta_one * one_ref[...] + (1.0 - beta_one) * grad
    two = beta_two * two_ref[...] + (1.0 - beta_two) * grad * grad
    one_new_ref[...] = one
    two_new_ref[...] = two
    old = w_ref[...]
    new_ref[...] = old - learn_rate * ((one * (1.0 / bias_one)) / (jnp.sqrt(two * (1.0 / bias_two)) + adam_eps) + decay_rate * old)


def swap(x, axis, shift):
    n = lax.axis_size(axis)
    return lax.ppermute(x, axis, [(i, i ^ shift) for i in range(n)])


def turns(n):
    return list(range(n // 2, n)) + list(range(n // 2 - 1, 0, -1))


def few(axis):
    n = lax.axis_size(axis)
    return n <= 8 and n & (n - 1) == 0


def gathered(x, axis):
    if few(axis):
        order = turns(lax.axis_size(axis))
        shifts = (order[1:] + order[:1])[::-1]
        arrays = [x] + [swap(x, axis, s) for s in shifts]
        return arrays, [(n, slice(None), s, None) for n, s in enumerate([0, *shifts])]
    n = lax.axis_size(axis)
    return [lax.all_gather(x, axis)], [(0, i, None, i) for i in range(n)]


def shards(queries, keys, values, conv_kernel, span_start, out_grad, proj_weight, moment_one, moment_two):
    _, rows, depth = queries.shape
    key_count = keys.shape[1]
    _, taps_a, taps_b = conv_kernel.shape
    span = out_grad.shape[1]
    half = (taps_b - 1) // 2
    step = LANES - 2 * half
    windows = -(-key_count // step)
    rows_up = up_to(rows, 16)
    wide = windows * LANES
    reach = up_to((windows - 1) * step + LANES, 8)
    groups = taps_a // GROUP
    group_count = lax.axis_size("dp")
    share = proj_weight.shape[1]
    columns = share * group_count
    vmem = pltpu.CompilerParams(vmem_limit_bytes=24 * 2**20)
    whole = pl.BlockSpec(memory_space=pltpu.VMEM)
    hbm = pl.BlockSpec(memory_space=pltpu.HBM)
    shape = jax.ShapeDtypeStruct
    stay = lambda x: pltpu.with_memory_space_constraint(x, pltpu.HBM)
    q_hbm = stay(queries)
    taps_hbm = stay(conv_kernel.transpose(1, 0, 2))
    smem = pl.BlockSpec(memory_space=pltpu.SMEM)
    taps_ref = pltpu.SMEM((taps_a, 1, taps_b), F32)
    rows32 = pltpu.VMEM(((windows - 1) * step + LANES + 8, depth), F32)
    band = shape((3 * GROUP * LANES, groups * LANES), BF16)
    sides = pltpu.VMEM((windows * rows_up, GROUP * LANES), BF16)

    def cost(flops):
        return pl.CostEstimate(flops=flops, bytes_accessed=10**6, transcendentals=0)

    proj_bf, band_rows, q32, q16 = pl.pallas_call(
        prepare,
        out_shape=(
            shape(proj_weight.shape, BF16),
            band,
            shape((rows_up + 8, depth), F32),
            shape((GROUP * rows_up, depth), BF16),
        ),
        in_specs=[hbm] * 3,
        out_specs=(whole,) * 4,
        scratch_shapes=[
            taps_ref,
            pltpu.VMEM(proj_weight.shape, F32),
            pltpu.VMEM((rows, depth), BF16),
            pltpu.SemaphoreType.DMA((3,)),
        ],
        compiler_params=vmem,
        cost_estimate=cost(5 * 10**9),
        name="prepare",
    )(taps_hbm, stay(proj_weight), q_hbm)
    w_arrays, w_places = gathered(proj_bf, "dp")
    cores_last = few("tensor") and lax.axis_size("tensor") > 2
    pieces = [stay(out_grad)]
    if cores_last:
        pieces += [swap(out_grad, "tensor", s) for s in range(2, lax.axis_size("tensor"), 2)]
    p, kwin, pack = pl.pallas_call(
        functools.partial(forward, len(pieces), taps_a, half),
        out_shape=(
            shape((span, wide), F32),
            shape((wide, depth), BF16),
            shape((len(pieces) * span, out_grad.shape[2]), BF16),
        ),
        in_specs=[whole] * len(pieces) + [smem] + [whole] * 3,
        out_specs=(whole,) * 3,
        scratch_shapes=[
            rows32,
            sides,
            sides,
            pltpu.VMEM((windows * rows_up, groups * LANES), F32),
        ],
        compiler_params=vmem,
        cost_estimate=cost(5 * 10**9),
        name="attention_forward",
    )(*pieces, span_start, band_rows, q16, keys)
    if cores_last:
        up_arrays = [pack, swap(pack, "tensor", 1)]
        up_places = [
            (c, slice(n * span, (n + 1) * span), 2 * n + c, None) for n in range(len(pieces)) for c in (0, 1)
        ]
    else:
        up_arrays, up_places = gathered(out_grad[0], "tensor")
    xth, xtl, vblk, attended = pl.pallas_call(
        functools.partial(forward_turned, taps_a, half),
        out_shape=(shape((wide, taps_a * span), BF16),) * 2 + (shape((wide, depth), BF16), shape((span, depth), BF16)),
        in_specs=[smem] + [whole] * 4,
        out_specs=(whole,) * 4,
        scratch_shapes=[pltpu.VMEM((wide, depth), BF16), rows32],
        compiler_params=vmem,
        cost_estimate=cost(2 * 10**9),
        name="attention_forward_turned",
    )(span_start, kwin, q32, p, values)

    owners = turns(group_count) if few("dp") else list(range(group_count))
    others = len(owners)
    do, own, own_taps, *payloads = pl.pallas_call(
        functools.partial(backward_scores, up_places, w_places, owners, few("dp")),
        out_shape=(
            shape((span, depth), BF16),
            shape((depth, share), F32),
            shape((8, LANES), F32),
        ) + (shape((depth * (share // LANES) + 16, LANES), BF16),) * others,
        in_specs=[whole] * (len(up_arrays) + len(w_arrays) + 5),
        out_specs=(whole,) * (3 + others),
        scratch_shapes=[
            pltpu.VMEM((span, columns), BF16),
            pltpu.VMEM((depth, columns), F32),
        ],
        compiler_params=vmem,
        cost_estimate=cost(2 * 10**9),
        name="attention_backward_scores",
    )(*up_arrays, *w_arrays, p, vblk, xth, xtl, attended)

    if few("dp"):
        payloads = [swap(payload, "dp", owner) for owner, payload in zip(owners, payloads, strict=True)]
    else:
        sent = lax.all_to_all(jnp.stack(payloads), "dp", 0, 0)
        payloads = [jnp.where(lax.axis_index("dp") == n, jnp.zeros_like(sent[n]), sent[n]) for n in range(group_count)]

    query_grad, key_grad, value_grad = pl.pallas_call(
        functools.partial(backward_inputs, rows, key_count, taps_a, half),
        out_shape=(shape(queries.shape, BF16), shape(keys.shape, BF16), shape(values.shape, BF16)),
        in_specs=[smem] + [whole] * 6,
        out_specs=(whole,) * 3,
        scratch_shapes=[
            pltpu.VMEM((rows_up + 8, wide), F32),
            sides,
            sides,
            pltpu.VMEM((windows * rows_up + 8, groups * LANES), F32),
            pltpu.VMEM((reach, depth), F32),
        ],
        compiler_params=vmem,
        cost_estimate=cost(3 * 10**9),
        name="attention_backward_inputs",
    )(span_start, band_rows, do, p, vblk, q16, kwin)

    proj_new, moment_one_new, moment_two_new, kernel_total = pl.pallas_call(
        functools.partial(update, group_count, span),
        out_shape=(shape(proj_weight.shape, F32),) * 3 + (shape((taps_a, 1, taps_b), F32),),
        in_specs=[whole] * (len(payloads) + 5),
        out_specs=(whole,) * 4,
        compiler_params=vmem,
        name="projection_update",
    )(*payloads, own, own_taps, proj_weight, moment_one, moment_two)
    return (
        query_grad,
        key_grad,
        value_grad,
        kernel_total.transpose(1, 0, 2),
        proj_new,
        moment_one_new,
        moment_two_new,
    )


def solution(mesh):
    heads, rows_of, blocks_of = P("dp", None, "tensor"), P("tensor", None, None), P("tensor", "dp")
    return jax.shard_map(
        shards,
        mesh=mesh,
        in_specs=(heads, heads, heads, rows_of, P("dp"), heads, blocks_of, blocks_of, blocks_of),
        out_specs=(heads, heads, heads, rows_of, blocks_of, blocks_of, blocks_of),
        check_vma=False,
    )
```

```python
import functools
import math

import jax
import jax.numpy as jnp
from jax import lax
from jax.experimental import pallas as pl
from jax.experimental.pallas import tpu as pltpu
from jax.sharding import PartitionSpec as P

beta_one = 0.9
beta_two = 0.95
learn_rate = 0.01
decay_rate = 0.1
adam_eps = 1e-08
bias_one = 1.0 - 0.9**10
bias_two = 1.0 - 0.95**10

LANES = 128
GROUP = 2
F32 = jnp.float32
BF16 = jnp.bfloat16


def dot(left, right, dims=((1,), (0,))):
    return lax.dot_general(left, right, (dims, ((), ())), preferred_element_type=F32)


def split(x):
    high = x.astype(BF16)
    return high, (x - high.astype(F32)).astype(BF16)


def up_to(n, multiple):
    return -(-n // multiple) * multiple


def iota(shape, axis):
    return lax.broadcasted_iota(jnp.int32, shape, axis)


def hold_bands(taps_ref, scale, bands_ref):
    taps_a, _, taps_b = taps_ref.shape
    lane = iota((1, LANES), 1)
    out = []
    for a in range(taps_a):
        row = jnp.zeros((1, LANES), F32)
        for b in range(taps_b):
            row = jnp.where(lane == (LANES - b) % LANES, taps_ref[a, 0, b], row)
        out.append(pltpu.roll(jnp.broadcast_to(row, (LANES, LANES)), 0, 1, stride=1, stride_axis=0))
    height = GROUP * LANES
    for n in range(taps_a // GROUP):
        cols = slice(n * LANES, (n + 1) * LANES)
        high, low = split(jnp.concatenate(out[n * GROUP : (n + 1) * GROUP][::-1], axis=0) * scale)
        bands_ref[:height, cols] = high
        bands_ref[height : 2 * height, cols] = low
        bands_ref[2 * height :, cols] = high


def turned_bands(bands_ref):
    spots = [part * GROUP + at for part in range(3) for at in range(GROUP - 1, -1, -1)]
    rows = []
    for n in range(bands_ref.shape[1] // LANES):
        cols = slice(n * LANES, (n + 1) * LANES)
        rows.append(jnp.concatenate([bands_ref[at * LANES : (at + 1) * LANES, cols] for at in spots], axis=1))
    return jnp.concatenate(rows, axis=0)


def fetch(pairs, sems):
    copies = [pltpu.make_async_copy(src, dst, sems.at[n]) for n, (src, dst) in enumerate(pairs)]
    for copy in copies:
        copy.start()
    return copies


def prepare(
    taps_hbm, w_hbm, q_hbm, grad_hbm,
    w_ref, bands_ref, q32, q16, grad_ref,
    taps_ref, w_in, q_in, sems,
):
    rows = q_in.shape[0]
    copies = fetch(((taps_hbm, taps_ref), (w_hbm, w_in), (q_hbm.at[0], q_in), (grad_hbm, grad_ref)), sems)
    q32[...] = jnp.zeros_like(q32)
    copies[0].wait()
    hold_bands(taps_ref, 1.0 / math.sqrt(q_in.shape[1]), bands_ref)
    copies[1].wait()
    w_ref[...] = w_in[...].astype(BF16)
    copies[2].wait()
    q32[:rows] = q_in[...].astype(F32)
    rows_up = q16.shape[0] // GROUP
    for n in range(GROUP):
        q16[n * rows_up : (n + 1) * rows_up] = q32[n : n + rows_up].astype(BF16)
    copies[3].wait()


def by_blocks(rows_ref, out, rows32, start, live):
    rows = rows_ref.shape[1]
    rows32[:8] = jnp.zeros((8, LANES), F32)
    rows32[8 : 8 + rows] = rows_ref[0].astype(F32)
    rows32[8 + rows :] = jnp.zeros((rows32.shape[0] - 8 - rows, LANES), F32)
    count = out.shape[0] // LANES
    step = (rows32.shape[0] - 8 - LANES) // (count - 1)
    for n in range(count):
        block = rows32[8 + start + n * step : 8 + start + n * step + LANES]
        if live < LANES:
            block = jnp.where(iota(block.shape, 0) < live, block, 0.0)
        out[n * LANES : (n + 1) * LANES] = block.astype(BF16)


def forward(pieces, taps_a, half, *refs):
    piece_refs, (first_ref, bands_ref, q16, k_ref) = refs[:pieces], refs[pieces : pieces + 4]
    p_ref, kwin, pack_ref, rows32, xh, xl, y = refs[pieces + 4 :]
    span = p_ref.shape[0]
    rows_up = q16.shape[0] // GROUP
    windows = kwin.shape[0] // LANES
    step = LANES - 2 * half
    first = first_ref[0]
    for n, ref in enumerate(piece_refs):
        pack_ref[n * span : (n + 1) * span] = ref[0]

    by_blocks(k_ref, kwin, rows32, -half, LANES)

    scores = dot(q16[...], kwin[...], ((1,), (1,)))
    pos = first - (taps_a - 1) + iota((rows_up, LANES), 0) - iota((rows_up, LANES), 1)
    for n in range(windows):
        here = slice(n * rows_up, (n + 1) * rows_up)
        for at in range(GROUP):
            x = scores[at * rows_up : (at + 1) * rows_up, n * LANES : (n + 1) * LANES]
            cols = slice(at * LANES, (at + 1) * LANES)
            xh[here, cols], xl[here, cols] = split(jnp.where(pos >= n * step - half - at, x, 0.0))

    y[...] = dot(jnp.concatenate([xh[...], xh[...], xl[...]], axis=1), bands_ref[...])
    mixed = []
    for n in range(windows):
        total = None
        for group in range(taps_a // GROUP):
            start = n * rows_up + taps_a - GROUP * (group + 1)
            term = y[start : start + span, group * LANES : (group + 1) * LANES]
            total = term if total is None else total + term
        mixed.append(total)
    c = jnp.concatenate(mixed, axis=1)
    lane = iota((span, LANES), 1)
    row = iota((span, LANES), 0)
    live = jnp.concatenate([(lane < step) & (n * step + lane <= first + row) for n in range(windows)], axis=1)
    c = jnp.where(live, c, -jnp.inf)
    terms = jnp.exp(c - jnp.max(c, axis=1, keepdims=True))
    p = terms * (1.0 / jnp.sum(terms, axis=1, keepdims=True))
    p_ref[...] = p


def forward_turned(taps_a, half, first_ref, kwin, q32, p_ref, v_ref, xth_ref, xtl_ref, vblk, o_ref, kturn, rows32):
    span = xth_ref.shape[1] // taps_a
    windows = kwin.shape[0] // LANES
    step = LANES - 2 * half
    first = first_ref[0]
    by_blocks(v_ref, vblk, rows32, 0, step)
    o_ref[...] = dot(p_ref[...].astype(BF16), vblk[...]).astype(BF16)
    flip = (iota((LANES, LANES), 0) + iota((LANES, LANES), 1) == LANES - 1).astype(F32).astype(BF16)
    for n in range(windows):
        here = slice(n * LANES, (n + 1) * LANES)
        kturn[here] = dot(flip, kwin[here]).astype(BF16)
    lead = LANES - 1 - half - iota((LANES, span), 0) - iota((LANES, span), 1)
    lead = jnp.concatenate([lead + n * step for n in range(windows)], axis=0)
    shifted = jnp.concatenate([q32[taps_a - 1 - a : taps_a - 1 - a + span].astype(BF16) for a in range(taps_a)], axis=0)
    xt = dot(kturn[...], shifted, ((1,), (1,)))
    for a in range(taps_a):
        cols = slice(a * span, (a + 1) * span)
        xth_ref[:, cols], xtl_ref[:, cols] = split(jnp.where(lead <= first - a, xt[:, cols], 0.0))


def backward_scores(up_places, w_places, owners, by_distance, *refs):
    n_up, n_w = len({p[0] for p in up_places}), len({p[0] for p in w_places})
    up_refs, w_refs, refs = refs[:n_up], refs[n_up : n_up + n_w], refs[n_up + n_w :]
    p_ref, vblk, xth_ref, xtl_ref, o_ref, do_ref, own_ref, own_taps_ref = refs[:8]
    out_refs, (up, grad) = refs[8 : 8 + len(owners)], refs[8 + len(owners) :]
    span = p_ref.shape[0]
    taps_a = xth_ref.shape[1] // span
    windows = vblk.shape[0] // LANES

    def columns(places, axis):
        me = lax.axis_index(axis)
        return [(n, part, at if shift is None else lax.bitwise_xor(me, shift)) for n, part, shift, at in places]

    for n, part, spot in columns(up_places, "tensor"):
        block = up_refs[n][part]
        width = block.shape[1]
        up[:, pl.ds(pl.multiple_of(spot * width, width), width)] = block
    do = None
    for n, part, spot in columns(w_places, "dp"):
        block = w_refs[n][part]
        width = block.shape[1]
        term = dot(up[:, pl.ds(pl.multiple_of(spot * width, width), width)], block, ((1,), (1,)))
        do = term if do is None else do + term
    do = do.astype(BF16)
    do_ref[...] = do
    grad[...] = dot(o_ref[...], up[...], ((0,), (0,)))
    dc = scores_grad(p_ref[...], do, vblk[...])

    right = jnp.concatenate(
        [jnp.concatenate(split(dc[:, n * LANES : (n + 1) * LANES]), axis=1) for n in range(windows)], axis=0
    )
    right = jnp.concatenate([right, right], axis=0)
    sums = []
    for a in range(taps_a):
        cols = slice(a * span, (a + 1) * span)
        left = jnp.concatenate(
            [ref[n * LANES : (n + 1) * LANES, cols] for ref in (xth_ref, xtl_ref) for n in range(windows)], axis=1
        )
        total = dot(left, right)
        turned = pltpu.roll(total[:, :LANES] + total[:, LANES:], 0, 1, stride=1, stride_axis=0)
        sums.append(jnp.sum(turned, axis=0, keepdims=True))
    taps = jnp.concatenate(sums + [jnp.zeros((8 - taps_a, LANES), F32)], axis=0)

    high, low = split(taps)
    mid, low = low, (taps - high.astype(F32) - low.astype(F32)).astype(BF16)
    aside = pltpu.roll(low.astype(F32), LANES // 2, 1)
    first = jnp.where(iota(aside.shape, 1) < LANES // 2, aside, high.astype(F32))
    parts = jnp.concatenate([first, mid.astype(F32)], axis=0).astype(BF16)
    own_taps_ref[...] = taps
    depth, share = own_ref.shape
    me = lax.axis_index("dp")

    def owned(spot):
        return grad[:, pl.ds(pl.multiple_of(spot * share, share), share)]

    own_ref[...] = owned(me)
    for owner, ref in zip(owners, out_refs, strict=True):
        piece = owned(lax.bitwise_xor(me, owner) if by_distance else owner).astype(BF16)
        for n in range(share // LANES):
            ref[n * depth : (n + 1) * depth] = piece[:, n * LANES : (n + 1) * LANES]
        ref[ref.shape[0] - 16 :] = parts


def scores_grad(p, do, vblk):
    dp = dot(do, vblk, ((1,), (1,)))
    return p * (dp - jnp.sum(p * dp, axis=1, keepdims=True))


def backward_inputs(
    rows, keys, taps_a, half, first_ref, bands_ref, do_ref, p_ref, vblk, q16, kwin,
    dq_ref, dk_ref, dv_ref,
    dc_ref, left_h, left_l, z, sums,
):
    step = LANES - 2 * half
    depth = kwin.shape[1]
    windows = kwin.shape[0] // LANES
    rows_up = q16.shape[0] // GROUP
    scale = 1.0 / math.sqrt(depth)
    first = first_ref[0]
    do = do_ref[...]
    span = do.shape[0]
    dc_ref[:8] = jnp.zeros((8, dc_ref.shape[1]), F32)
    dc_ref[8 : 8 + span] = scores_grad(p_ref[...], do, vblk[...])
    dc_ref[8 + span :] = jnp.zeros((dc_ref.shape[0] - 8 - span, dc_ref.shape[1]), F32)
    for n in range(windows):
        cols = slice(n * LANES, (n + 1) * LANES)
        here = slice(n * rows_up, (n + 1) * rows_up)
        for at in range(GROUP):
            there = slice(at * LANES, (at + 1) * LANES)
            left_h[here, there], left_l[here, there] = split(dc_ref[at : at + rows_up, cols])
        sums[n * step : n * step + LANES] = dot(p_ref[:, cols].astype(BF16).T, do)
    dv_ref[0] = sums[:keys].astype(BF16)
    z[windows * rows_up :] = jnp.zeros((z.shape[0] - windows * rows_up, z.shape[1]), F32)
    left = jnp.concatenate([left_h[...], left_h[...], left_l[...]], axis=1)
    z[: windows * rows_up] = dot(left, turned_bands(bands_ref), ((1,), (1,)))

    lane = iota((rows_up, LANES), 1)
    row = iota((rows_up, LANES), 0)
    scores = []
    for n in range(windows):
        total = None
        for group in range(taps_a // GROUP):
            start = n * rows_up + 8 - (taps_a - 1) + GROUP * group
            term = z[start : start + rows_up, group * LANES : (group + 1) * LANES]
            total = term if total is None else total + term
        scores.append(total)
    sums[...] = jnp.zeros_like(sums)
    dq = jnp.zeros((rows_up, depth), F32)
    for n, total in enumerate(scores):
        if n + 1 < windows:
            total = jnp.where(lane < step, total, total + pltpu.roll(scores[n + 1], step, 1))
        live = (n * step - half + lane <= first - (taps_a - 1) + row) & (row < rows)
        ds = jnp.where(live & (lane >= 2 * half) if n else live, total * (1.0 / scale), 0.0)
        dq = dq + dot(ds.astype(BF16), kwin[n * LANES : (n + 1) * LANES])
        sums[n * step : n * step + LANES] += dot(ds.astype(BF16).T, q16[:rows_up])
    dk_ref[0] = (scale * sums[half : half + keys]).astype(BF16)
    dq_ref[0] = (scale * dq)[:rows].astype(BF16)


def update(count, span, *refs):
    payload_refs, (own_ref, own_taps_ref, w_ref, one_ref, two_ref) = refs[:-9], refs[-9:-4]
    new_ref, one_new_ref, two_new_ref, taps_ref = refs[-4:]
    taps_a, _, taps_b = taps_ref.shape
    depth, share = own_ref.shape
    grad, taps = own_ref[...], own_taps_ref[...]
    for ref in payload_refs:
        piece = [ref[n * depth : (n + 1) * depth] for n in range(share // LANES)]
        grad = grad + jnp.concatenate(piece, axis=1).astype(F32)
        parts = ref[ref.shape[0] - 16 :].astype(F32)
        taps = taps + (parts[:8] + (parts[8:] + pltpu.roll(parts[:8], LANES // 2, 1)))
    grad = grad * (1.0 / count)
    taps = taps * (1.0 / (math.sqrt(depth) * count * span))
    lane = iota((8, LANES), 1)
    turned = jnp.zeros((8, LANES), F32)
    for b in range(taps_b):
        turned = jnp.where(lane == b, taps[:, LANES - 1 - b : LANES - b], turned)
    for a in range(taps_a):
        taps_ref[a] = turned[a : a + 1, :taps_b]
    one = beta_one * one_ref[...] + (1.0 - beta_one) * grad
    two = beta_two * two_ref[...] + (1.0 - beta_two) * grad * grad
    one_new_ref[...] = one
    two_new_ref[...] = two
    old = w_ref[...]
    new_ref[...] = old - learn_rate * ((one * (1.0 / bias_one)) / (jnp.sqrt(two * (1.0 / bias_two)) + adam_eps) + decay_rate * old)


def swap(x, axis, shift):
    n = lax.axis_size(axis)
    return lax.ppermute(x, axis, [(i, i ^ shift) for i in range(n)])


def turns(n):
    return list(range(n // 2, n)) + list(range(n // 2 - 1, 0, -1))


def few(axis):
    n = lax.axis_size(axis)
    return n <= 8 and n & (n - 1) == 0


def gathered(x, axis):
    if few(axis):
        shifts = turns(lax.axis_size(axis))[::-1]
        arrays = [x] + [swap(x, axis, s) for s in shifts]
        return arrays, [(n, slice(None), s, None) for n, s in enumerate([0, *shifts])]
    n = lax.axis_size(axis)
    return [lax.all_gather(x, axis)], [(0, i, None, i) for i in range(n)]


def shards(queries, keys, values, conv_kernel, span_start, out_grad, proj_weight, moment_one, moment_two):
    _, rows, depth = queries.shape
    key_count = keys.shape[1]
    _, taps_a, taps_b = conv_kernel.shape
    span = out_grad.shape[1]
    half = (taps_b - 1) // 2
    step = LANES - 2 * half
    windows = -(-key_count // step)
    rows_up = up_to(rows, 16)
    wide = windows * LANES
    reach = up_to((windows - 1) * step + LANES, 8)
    groups = taps_a // GROUP
    group_count = lax.axis_size("dp")
    share = proj_weight.shape[1]
    columns = share * group_count
    vmem = pltpu.CompilerParams(vmem_limit_bytes=24 * 2**20)
    whole = pl.BlockSpec(memory_space=pltpu.VMEM)
    hbm = pl.BlockSpec(memory_space=pltpu.HBM)
    shape = jax.ShapeDtypeStruct
    stay = lambda x: pltpu.with_memory_space_constraint(x, pltpu.HBM)
    q_hbm = stay(queries)
    taps_hbm = stay(conv_kernel.transpose(1, 0, 2))
    smem = pl.BlockSpec(memory_space=pltpu.SMEM)
    taps_ref = pltpu.SMEM((taps_a, 1, taps_b), F32)
    rows32 = pltpu.VMEM(((windows - 1) * step + LANES + 8, depth), F32)
    band = shape((3 * GROUP * LANES, groups * LANES), BF16)
    sides = pltpu.VMEM((windows * rows_up, GROUP * LANES), BF16)

    def cost(flops):
        return pl.CostEstimate(flops=flops, bytes_accessed=10**6, transcendentals=0)

    proj_bf, band_rows, q32, q16, local_grad = pl.pallas_call(
        prepare,
        out_shape=(
            shape(proj_weight.shape, BF16),
            band,
            shape((rows_up + 8, depth), F32),
            shape((GROUP * rows_up, depth), BF16),
            shape(out_grad.shape, BF16),
        ),
        in_specs=[hbm] * 4,
        out_specs=(whole,) * 5,
        scratch_shapes=[
            taps_ref,
            pltpu.VMEM(proj_weight.shape, F32),
            pltpu.VMEM((rows, depth), BF16),
            pltpu.SemaphoreType.DMA((4,)),
        ],
        compiler_params=vmem,
        cost_estimate=cost(5 * 10**9),
        name="prepare",
    )(taps_hbm, stay(proj_weight), q_hbm, stay(out_grad))
    w_arrays, w_places = gathered(proj_bf, "dp")
    cores_last = few("tensor") and lax.axis_size("tensor") > 2
    pieces = [local_grad]
    if cores_last:
        pieces += [swap(out_grad, "tensor", s) for s in range(2, lax.axis_size("tensor"), 2)]
    p, kwin, pack = pl.pallas_call(
        functools.partial(forward, len(pieces), taps_a, half),
        out_shape=(
            shape((span, wide), F32),
            shape((wide, depth), BF16),
            shape((len(pieces) * span, out_grad.shape[2]), BF16),
        ),
        in_specs=[whole] * len(pieces) + [smem] + [whole] * 3,
        out_specs=(whole,) * 3,
        scratch_shapes=[
            rows32,
            sides,
            sides,
            pltpu.VMEM((windows * rows_up, groups * LANES), F32),
        ],
        compiler_params=vmem,
        cost_estimate=cost(5 * 10**9),
        name="attention_forward",
    )(*pieces, span_start, band_rows, q16, keys)
    if cores_last:
        up_arrays = [pack, swap(pack, "tensor", 1)]
        up_places = [
            (c, slice(n * span, (n + 1) * span), 2 * n + c, None) for n in range(len(pieces)) for c in (0, 1)
        ]
    else:
        up_arrays, up_places = gathered(out_grad[0], "tensor")
    xth, xtl, vblk, attended = pl.pallas_call(
        functools.partial(forward_turned, taps_a, half),
        out_shape=(shape((wide, taps_a * span), BF16),) * 2 + (shape((wide, depth), BF16), shape((span, depth), BF16)),
        in_specs=[smem] + [whole] * 4,
        out_specs=(whole,) * 4,
        scratch_shapes=[pltpu.VMEM((wide, depth), BF16), rows32],
        compiler_params=vmem,
        cost_estimate=cost(2 * 10**9),
        name="attention_forward_turned",
    )(span_start, kwin, q32, p, values)

    owners = list(range(group_count))
    if few("dp"):
        owners = owners[group_count // 2 : 0 : -1] + owners[group_count // 2 + 1 :]
    others = len(owners)
    do, own, own_taps, *payloads = pl.pallas_call(
        functools.partial(backward_scores, up_places, w_places, owners, few("dp")),
        out_shape=(
            shape((span, depth), BF16),
            shape((depth, share), F32),
            shape((8, LANES), F32),
        ) + (shape((depth * (share // LANES) + 16, LANES), BF16),) * others,
        in_specs=[whole] * (len(up_arrays) + len(w_arrays) + 5),
        out_specs=(whole,) * (3 + others),
        scratch_shapes=[
            pltpu.VMEM((span, columns), BF16),
            pltpu.VMEM((depth, columns), F32),
        ],
        compiler_params=vmem,
        cost_estimate=cost(2 * 10**9),
        name="attention_backward_scores",
    )(*up_arrays, *w_arrays, p, vblk, xth, xtl, attended)

    if few("dp"):
        payloads = [swap(payload, "dp", owner) for owner, payload in zip(owners, payloads, strict=True)]
    else:
        sent = lax.all_to_all(jnp.stack(payloads), "dp", 0, 0)
        payloads = [jnp.where(lax.axis_index("dp") == n, jnp.zeros_like(sent[n]), sent[n]) for n in range(group_count)]

    query_grad, key_grad, value_grad = pl.pallas_call(
        functools.partial(backward_inputs, rows, key_count, taps_a, half),
        out_shape=(shape(queries.shape, BF16), shape(keys.shape, BF16), shape(values.shape, BF16)),
        in_specs=[smem] + [whole] * 6,
        out_specs=(whole,) * 3,
        scratch_shapes=[
            pltpu.VMEM((rows_up + 8, wide), F32),
            sides,
            sides,
            pltpu.VMEM((windows * rows_up + 8, groups * LANES), F32),
            pltpu.VMEM((reach, depth), F32),
        ],
        compiler_params=vmem,
        cost_estimate=cost(3 * 10**9),
        name="attention_backward_inputs",
    )(span_start, band_rows, do, p, vblk, q16, kwin)

    proj_new, moment_one_new, moment_two_new, kernel_total = pl.pallas_call(
        functools.partial(update, group_count, span),
        out_shape=(shape(proj_weight.shape, F32),) * 3 + (shape((taps_a, 1, taps_b), F32),),
        in_specs=[whole] * (len(payloads) + 5),
        out_specs=(whole,) * 4,
        compiler_params=vmem,
        name="projection_update",
    )(*payloads, own, own_taps, proj_weight, moment_one, moment_two)
    return (
        query_grad,
        key_grad,
        value_grad,
        kernel_total.transpose(1, 0, 2),
        proj_new,
        moment_one_new,
        moment_two_new,
    )


def solution(mesh):
    heads, rows_of, blocks_of = P("dp", None, "tensor"), P("tensor", None, None), P("tensor", "dp")
    return jax.shard_map(
        shards,
        mesh=mesh,
        in_specs=(heads, heads, heads, rows_of, P("dp"), heads, blocks_of, blocks_of, blocks_of),
        out_specs=(heads, heads, heads, rows_of, blocks_of, blocks_of, blocks_of),
        check_vma=False,
    )
```

```python
import functools
import math

import jax
import jax.numpy as jnp
from jax import lax
from jax.experimental import pallas as pl
from jax.experimental.pallas import tpu as pltpu
from jax.sharding import PartitionSpec as P

beta_one = 0.9
beta_two = 0.95
learn_rate = 0.01
decay_rate = 0.1
adam_eps = 1e-08
bias_one = 1.0 - 0.9**10
bias_two = 1.0 - 0.95**10

LANES = 128
GROUP = 2
F32 = jnp.float32
BF16 = jnp.bfloat16


def dot(left, right, dims=((1,), (0,))):
    return lax.dot_general(left, right, (dims, ((), ())), preferred_element_type=F32)


def split(x):
    high = x.astype(BF16)
    return high, (x - high.astype(F32)).astype(BF16)


def up_to(n, multiple):
    return -(-n // multiple) * multiple


def iota(shape, axis):
    return lax.broadcasted_iota(jnp.int32, shape, axis)


def hold_bands(taps_ref, scale, bands_ref):
    taps_a, _, taps_b = taps_ref.shape
    lane = iota((1, LANES), 1)
    out = []
    for a in range(taps_a):
        row = jnp.zeros((1, LANES), F32)
        for b in range(taps_b):
            row = jnp.where(lane == (LANES - b) % LANES, taps_ref[a, 0, b], row)
        out.append(pltpu.roll(jnp.broadcast_to(row, (LANES, LANES)), 0, 1, stride=1, stride_axis=0))
    height = GROUP * LANES
    for n in range(taps_a // GROUP):
        cols = slice(n * LANES, (n + 1) * LANES)
        high, low = split(jnp.concatenate(out[n * GROUP : (n + 1) * GROUP][::-1], axis=0) * scale)
        bands_ref[:height, cols] = high
        bands_ref[height : 2 * height, cols] = low
        bands_ref[2 * height :, cols] = high


def turned_bands(bands_ref):
    spots = [part * GROUP + at for part in range(3) for at in range(GROUP - 1, -1, -1)]
    rows = []
    for n in range(bands_ref.shape[1] // LANES):
        cols = slice(n * LANES, (n + 1) * LANES)
        rows.append(jnp.concatenate([bands_ref[at * LANES : (at + 1) * LANES, cols] for at in spots], axis=1))
    return jnp.concatenate(rows, axis=0)


def fetch(pairs, sems):
    copies = [pltpu.make_async_copy(src, dst, sems.at[n]) for n, (src, dst) in enumerate(pairs)]
    for copy in copies:
        copy.start()
    return copies


def prepare(
    taps_hbm, w_hbm, q_hbm, grad_hbm,
    w_ref, bands_ref, q32, q16, grad_ref,
    taps_ref, w_in, q_in, sems,
):
    rows = q_in.shape[0]
    copies = fetch(((taps_hbm, taps_ref), (w_hbm, w_in), (q_hbm.at[0], q_in), (grad_hbm, grad_ref)), sems)
    q32[...] = jnp.zeros_like(q32)
    copies[0].wait()
    hold_bands(taps_ref, 1.0 / math.sqrt(q_in.shape[1]), bands_ref)
    copies[1].wait()
    w_ref[...] = w_in[...].astype(BF16)
    copies[2].wait()
    q32[:rows] = q_in[...].astype(F32)
    rows_up = q16.shape[0] // GROUP
    for n in range(GROUP):
        q16[n * rows_up : (n + 1) * rows_up] = q32[n : n + rows_up].astype(BF16)
    copies[3].wait()


def by_blocks(rows_ref, out, rows32, start, live):
    rows = rows_ref.shape[1]
    rows32[:8] = jnp.zeros((8, LANES), F32)
    rows32[8 : 8 + rows] = rows_ref[0].astype(F32)
    rows32[8 + rows :] = jnp.zeros((rows32.shape[0] - 8 - rows, LANES), F32)
    count = out.shape[0] // LANES
    step = (rows32.shape[0] - 8 - LANES) // (count - 1)
    for n in range(count):
        block = rows32[8 + start + n * step : 8 + start + n * step + LANES]
        if live < LANES:
            block = jnp.where(iota(block.shape, 0) < live, block, 0.0)
        out[n * LANES : (n + 1) * LANES] = block.astype(BF16)


def forward(pieces, taps_a, half, *refs):
    piece_refs, (first_ref, bands_ref, q16, k_ref) = refs[:pieces], refs[pieces : pieces + 4]
    p_ref, kwin, pack_ref, rows32, xh, xl, y = refs[pieces + 4 :]
    span = p_ref.shape[0]
    rows_up = q16.shape[0] // GROUP
    windows = kwin.shape[0] // LANES
    step = LANES - 2 * half
    first = first_ref[0]
    for n, ref in enumerate(piece_refs):
        pack_ref[n * span : (n + 1) * span] = ref[0]

    by_blocks(k_ref, kwin, rows32, -half, LANES)

    scores = dot(q16[...], kwin[...], ((1,), (1,)))
    pos = first - (taps_a - 1) + iota((rows_up, LANES), 0) - iota((rows_up, LANES), 1)
    for n in range(windows):
        here = slice(n * rows_up, (n + 1) * rows_up)
        for at in range(GROUP):
            x = scores[at * rows_up : (at + 1) * rows_up, n * LANES : (n + 1) * LANES]
            cols = slice(at * LANES, (at + 1) * LANES)
            xh[here, cols], xl[here, cols] = split(jnp.where(pos >= n * step - half - at, x, 0.0))

    y[...] = dot(jnp.concatenate([xh[...], xh[...], xl[...]], axis=1), bands_ref[...])
    mixed = []
    for n in range(windows):
        total = None
        for group in range(taps_a // GROUP):
            start = n * rows_up + taps_a - GROUP * (group + 1)
            term = y[start : start + span, group * LANES : (group + 1) * LANES]
            total = term if total is None else total + term
        mixed.append(total)
    c = jnp.concatenate(mixed, axis=1)
    lane = iota((span, LANES), 1)
    row = iota((span, LANES), 0)
    live = jnp.concatenate([(lane < step) & (n * step + lane <= first + row) for n in range(windows)], axis=1)
    c = jnp.where(live, c, -jnp.inf)
    terms = jnp.exp(c - jnp.max(c, axis=1, keepdims=True))
    p = terms * (1.0 / jnp.sum(terms, axis=1, keepdims=True))
    p_ref[...] = p


def forward_turned(taps_a, half, first_ref, kwin, q32, p_ref, v_ref, xth_ref, xtl_ref, vblk, o_ref, kturn, rows32):
    span = xth_ref.shape[1] // taps_a
    windows = kwin.shape[0] // LANES
    step = LANES - 2 * half
    first = first_ref[0]
    by_blocks(v_ref, vblk, rows32, 0, step)
    o_ref[...] = dot(p_ref[...].astype(BF16), vblk[...]).astype(BF16)
    flip = (iota((LANES, LANES), 0) + iota((LANES, LANES), 1) == LANES - 1).astype(F32).astype(BF16)
    for n in range(windows):
        here = slice(n * LANES, (n + 1) * LANES)
        kturn[here] = dot(flip, kwin[here]).astype(BF16)
    lead = LANES - 1 - half - iota((LANES, span), 0) - iota((LANES, span), 1)
    lead = jnp.concatenate([lead + n * step for n in range(windows)], axis=0)
    shifted = jnp.concatenate([q32[taps_a - 1 - a : taps_a - 1 - a + span].astype(BF16) for a in range(taps_a)], axis=0)
    xt = dot(kturn[...], shifted, ((1,), (1,)))
    for a in range(taps_a):
        cols = slice(a * span, (a + 1) * span)
        xth_ref[:, cols], xtl_ref[:, cols] = split(jnp.where(lead <= first - a, xt[:, cols], 0.0))


def spots(places, axis):
    me = lax.axis_index(axis)
    return [(n, part, at if shift is None else lax.bitwise_xor(me, shift)) for n, part, shift, at in places]


def backward_columns(places, *refs):
    *up_refs, o_ref, up, grad = refs
    for n, part, spot in spots(places, "tensor"):
        block = up_refs[n][part]
        width = block.shape[1]
        up[:, pl.ds(pl.multiple_of(spot * width, width), width)] = block
    grad[...] = dot(o_ref[...], up[...], ((0,), (0,)))


def backward_scores(places, owners, by_distance, *refs):
    n_w = len({p[0] for p in places})
    w_refs, refs = refs[:n_w], refs[n_w:]
    up, grad, p_ref, vblk, xth_ref, xtl_ref, do_ref, own_ref, own_taps_ref, *out_refs = refs
    span = p_ref.shape[0]
    taps_a = xth_ref.shape[1] // span
    windows = vblk.shape[0] // LANES

    do = None
    for n, part, spot in spots(places, "dp"):
        block = w_refs[n][part]
        width = block.shape[1]
        term = dot(up[:, pl.ds(pl.multiple_of(spot * width, width), width)], block, ((1,), (1,)))
        do = term if do is None else do + term
    do = do.astype(BF16)
    do_ref[...] = do
    dc = scores_grad(p_ref[...], do, vblk[...])

    right = jnp.concatenate(
        [jnp.concatenate(split(dc[:, n * LANES : (n + 1) * LANES]), axis=1) for n in range(windows)], axis=0
    )
    right = jnp.concatenate([right, right], axis=0)
    sums = []
    for a in range(taps_a):
        cols = slice(a * span, (a + 1) * span)
        left = jnp.concatenate(
            [ref[n * LANES : (n + 1) * LANES, cols] for ref in (xth_ref, xtl_ref) for n in range(windows)], axis=1
        )
        total = dot(left, right)
        turned = pltpu.roll(total[:, :LANES] + total[:, LANES:], 0, 1, stride=1, stride_axis=0)
        sums.append(jnp.sum(turned, axis=0, keepdims=True))
    taps = jnp.concatenate(sums + [jnp.zeros((8 - taps_a, LANES), F32)], axis=0)

    high, low = split(taps)
    mid, low = low, (taps - high.astype(F32) - low.astype(F32)).astype(BF16)
    aside = pltpu.roll(low.astype(F32), LANES // 2, 1)
    first = jnp.where(iota(aside.shape, 1) < LANES // 2, aside, high.astype(F32))
    parts = jnp.concatenate([first, mid.astype(F32)], axis=0).astype(BF16)
    own_taps_ref[...] = taps
    depth, share = own_ref.shape
    me = lax.axis_index("dp")

    def owned(spot):
        return grad[:, pl.ds(pl.multiple_of(spot * share, share), share)]

    own_ref[...] = owned(me)
    for owner, ref in zip(owners, out_refs, strict=True):
        piece = owned(lax.bitwise_xor(me, owner) if by_distance else owner).astype(BF16)
        for n in range(share // LANES):
            ref[n * depth : (n + 1) * depth] = piece[:, n * LANES : (n + 1) * LANES]
        ref[ref.shape[0] - 16 :] = parts


def scores_grad(p, do, vblk):
    dp = dot(do, vblk, ((1,), (1,)))
    return p * (dp - jnp.sum(p * dp, axis=1, keepdims=True))


def backward_inputs(
    rows, keys, taps_a, half, first_ref, bands_ref, do_ref, p_ref, vblk, q16, kwin,
    dq_ref, dk_ref, dv_ref,
    dc_ref, left_h, left_l, z, sums,
):
    step = LANES - 2 * half
    depth = kwin.shape[1]
    windows = kwin.shape[0] // LANES
    rows_up = q16.shape[0] // GROUP
    scale = 1.0 / math.sqrt(depth)
    first = first_ref[0]
    do = do_ref[...]
    span = do.shape[0]
    dc_ref[:8] = jnp.zeros((8, dc_ref.shape[1]), F32)
    dc_ref[8 : 8 + span] = scores_grad(p_ref[...], do, vblk[...])
    dc_ref[8 + span :] = jnp.zeros((dc_ref.shape[0] - 8 - span, dc_ref.shape[1]), F32)
    for n in range(windows):
        cols = slice(n * LANES, (n + 1) * LANES)
        here = slice(n * rows_up, (n + 1) * rows_up)
        for at in range(GROUP):
            there = slice(at * LANES, (at + 1) * LANES)
            left_h[here, there], left_l[here, there] = split(dc_ref[at : at + rows_up, cols])
        sums[n * step : n * step + LANES] = dot(p_ref[:, cols].astype(BF16).T, do)
    dv_ref[0] = sums[:keys].astype(BF16)
    z[windows * rows_up :] = jnp.zeros((z.shape[0] - windows * rows_up, z.shape[1]), F32)
    left = jnp.concatenate([left_h[...], left_h[...], left_l[...]], axis=1)
    z[: windows * rows_up] = dot(left, turned_bands(bands_ref), ((1,), (1,)))

    lane = iota((rows_up, LANES), 1)
    row = iota((rows_up, LANES), 0)
    scores = []
    for n in range(windows):
        total = None
        for group in range(taps_a // GROUP):
            start = n * rows_up + 8 - (taps_a - 1) + GROUP * group
            term = z[start : start + rows_up, group * LANES : (group + 1) * LANES]
            total = term if total is None else total + term
        scores.append(total)
    sums[...] = jnp.zeros_like(sums)
    dq = jnp.zeros((rows_up, depth), F32)
    for n, total in enumerate(scores):
        if n + 1 < windows:
            total = jnp.where(lane < step, total, total + pltpu.roll(scores[n + 1], step, 1))
        live = (n * step - half + lane <= first - (taps_a - 1) + row) & (row < rows)
        ds = jnp.where(live & (lane >= 2 * half) if n else live, total * (1.0 / scale), 0.0)
        dq = dq + dot(ds.astype(BF16), kwin[n * LANES : (n + 1) * LANES])
        sums[n * step : n * step + LANES] += dot(ds.astype(BF16).T, q16[:rows_up])
    dk_ref[0] = (scale * sums[half : half + keys]).astype(BF16)
    dq_ref[0] = (scale * dq)[:rows].astype(BF16)


def update(count, span, *refs):
    payload_refs, (own_ref, own_taps_ref, w_ref, one_ref, two_ref) = refs[:-9], refs[-9:-4]
    new_ref, one_new_ref, two_new_ref, taps_ref = refs[-4:]
    taps_a, _, taps_b = taps_ref.shape
    depth, share = own_ref.shape
    grad, taps = own_ref[...], own_taps_ref[...]
    for ref in payload_refs:
        piece = [ref[n * depth : (n + 1) * depth] for n in range(share // LANES)]
        grad = grad + jnp.concatenate(piece, axis=1).astype(F32)
        parts = ref[ref.shape[0] - 16 :].astype(F32)
        taps = taps + (parts[:8] + (parts[8:] + pltpu.roll(parts[:8], LANES // 2, 1)))
    grad = grad * (1.0 / count)
    taps = taps * (1.0 / (math.sqrt(depth) * count * span))
    lane = iota((8, LANES), 1)
    turned = jnp.zeros((8, LANES), F32)
    for b in range(taps_b):
        turned = jnp.where(lane == b, taps[:, LANES - 1 - b : LANES - b], turned)
    for a in range(taps_a):
        taps_ref[a] = turned[a : a + 1, :taps_b]
    one = beta_one * one_ref[...] + (1.0 - beta_one) * grad
    two = beta_two * two_ref[...] + (1.0 - beta_two) * grad * grad
    one_new_ref[...] = one
    two_new_ref[...] = two
    old = w_ref[...]
    new_ref[...] = old - learn_rate * ((one * (1.0 / bias_one)) / (jnp.sqrt(two * (1.0 / bias_two)) + adam_eps) + decay_rate * old)


def swap(x, axis, shift):
    n = lax.axis_size(axis)
    return lax.ppermute(x, axis, [(i, i ^ shift) for i in range(n)])


def turns(n):
    return list(range(n // 2, n)) + list(range(n // 2 - 1, 0, -1))


def few(axis):
    n = lax.axis_size(axis)
    return n <= 8 and n & (n - 1) == 0


def gathered(x, axis):
    if few(axis):
        shifts = turns(lax.axis_size(axis))[::-1]
        arrays = [x] + [swap(x, axis, s) for s in shifts]
        return arrays, [(n, slice(None), s, None) for n, s in enumerate([0, *shifts])]
    n = lax.axis_size(axis)
    return [lax.all_gather(x, axis)], [(0, i, None, i) for i in range(n)]


def shards(queries, keys, values, conv_kernel, span_start, out_grad, proj_weight, moment_one, moment_two):
    _, rows, depth = queries.shape
    key_count = keys.shape[1]
    _, taps_a, taps_b = conv_kernel.shape
    span = out_grad.shape[1]
    half = (taps_b - 1) // 2
    step = LANES - 2 * half
    windows = -(-key_count // step)
    rows_up = up_to(rows, 16)
    wide = windows * LANES
    reach = up_to((windows - 1) * step + LANES, 8)
    groups = taps_a // GROUP
    group_count = lax.axis_size("dp")
    share = proj_weight.shape[1]
    columns = share * group_count
    vmem = pltpu.CompilerParams(vmem_limit_bytes=24 * 2**20)
    whole = pl.BlockSpec(memory_space=pltpu.VMEM)
    hbm = pl.BlockSpec(memory_space=pltpu.HBM)
    shape = jax.ShapeDtypeStruct
    stay = lambda x: pltpu.with_memory_space_constraint(x, pltpu.HBM)
    q_hbm = stay(queries)
    taps_hbm = stay(conv_kernel.transpose(1, 0, 2))
    smem = pl.BlockSpec(memory_space=pltpu.SMEM)
    taps_ref = pltpu.SMEM((taps_a, 1, taps_b), F32)
    rows32 = pltpu.VMEM(((windows - 1) * step + LANES + 8, depth), F32)
    band = shape((3 * GROUP * LANES, groups * LANES), BF16)
    sides = pltpu.VMEM((windows * rows_up, GROUP * LANES), BF16)

    def cost(flops):
        return pl.CostEstimate(flops=flops, bytes_accessed=10**6, transcendentals=0)

    proj_bf, band_rows, q32, q16, local_grad = pl.pallas_call(
        prepare,
        out_shape=(
            shape(proj_weight.shape, BF16),
            band,
            shape((rows_up + 8, depth), F32),
            shape((GROUP * rows_up, depth), BF16),
            shape(out_grad.shape, BF16),
        ),
        in_specs=[hbm] * 4,
        out_specs=(whole,) * 5,
        scratch_shapes=[
            taps_ref,
            pltpu.VMEM(proj_weight.shape, F32),
            pltpu.VMEM((rows, depth), BF16),
            pltpu.SemaphoreType.DMA((4,)),
        ],
        compiler_params=vmem,
        cost_estimate=cost(5 * 10**9),
        name="prepare",
    )(taps_hbm, stay(proj_weight), q_hbm, stay(out_grad))
    w_arrays, w_places = gathered(proj_bf, "dp")
    cores_last = few("tensor") and lax.axis_size("tensor") > 2
    pieces = [local_grad]
    if cores_last:
        pieces += [swap(out_grad, "tensor", s) for s in range(2, lax.axis_size("tensor"), 2)]
    p, kwin, pack = pl.pallas_call(
        functools.partial(forward, len(pieces), taps_a, half),
        out_shape=(
            shape((span, wide), F32),
            shape((wide, depth), BF16),
            shape((len(pieces) * span, out_grad.shape[2]), BF16),
        ),
        in_specs=[whole] * len(pieces) + [smem] + [whole] * 3,
        out_specs=(whole,) * 3,
        scratch_shapes=[
            rows32,
            sides,
            sides,
            pltpu.VMEM((windows * rows_up, groups * LANES), F32),
        ],
        compiler_params=vmem,
        cost_estimate=cost(5 * 10**9),
        name="attention_forward",
    )(*pieces, span_start, band_rows, q16, keys)
    if cores_last:
        up_arrays = [pack, swap(pack, "tensor", 1)]
        up_places = [
            (c, slice(n * span, (n + 1) * span), 2 * n + c, None) for n in range(len(pieces)) for c in (0, 1)
        ]
    else:
        up_arrays, up_places = gathered(out_grad[0], "tensor")
    xth, xtl, vblk, attended = pl.pallas_call(
        functools.partial(forward_turned, taps_a, half),
        out_shape=(shape((wide, taps_a * span), BF16),) * 2 + (shape((wide, depth), BF16), shape((span, depth), BF16)),
        in_specs=[smem] + [whole] * 4,
        out_specs=(whole,) * 4,
        scratch_shapes=[pltpu.VMEM((wide, depth), BF16), rows32],
        compiler_params=vmem,
        cost_estimate=cost(2 * 10**9),
        name="attention_forward_turned",
    )(span_start, kwin, q32, p, values)

    owners = list(range(group_count))
    if few("dp"):
        owners = owners[group_count // 2 : 0 : -1] + owners[group_count // 2 + 1 :]
    others = len(owners)
    up, grad = pl.pallas_call(
        functools.partial(backward_columns, up_places),
        out_shape=(shape((span, columns), BF16), shape((depth, columns), F32)),
        in_specs=[whole] * (len(up_arrays) + 1),
        out_specs=(whole,) * 2,
        compiler_params=vmem,
        cost_estimate=cost(10**9),
        name="attention_backward_columns",
    )(*up_arrays, attended)
    do, own, own_taps, *payloads = pl.pallas_call(
        functools.partial(backward_scores, w_places, owners, few("dp")),
        out_shape=(
            shape((span, depth), BF16),
            shape((depth, share), F32),
            shape((8, LANES), F32),
        ) + (shape((depth * (share // LANES) + 16, LANES), BF16),) * others,
        in_specs=[whole] * (len(w_arrays) + 6),
        out_specs=(whole,) * (3 + others),
        compiler_params=vmem,
        cost_estimate=cost(2 * 10**9),
        name="attention_backward_scores",
    )(*w_arrays, up, grad, p, vblk, xth, xtl)

    if few("dp"):
        payloads = [swap(payload, "dp", owner) for owner, payload in zip(owners, payloads, strict=True)]
    else:
        sent = lax.all_to_all(jnp.stack(payloads), "dp", 0, 0)
        payloads = [jnp.where(lax.axis_index("dp") == n, jnp.zeros_like(sent[n]), sent[n]) for n in range(group_count)]

    query_grad, key_grad, value_grad = pl.pallas_call(
        functools.partial(backward_inputs, rows, key_count, taps_a, half),
        out_shape=(shape(queries.shape, BF16), shape(keys.shape, BF16), shape(values.shape, BF16)),
        in_specs=[smem] + [whole] * 6,
        out_specs=(whole,) * 3,
        scratch_shapes=[
            pltpu.VMEM((rows_up + 8, wide), F32),
            sides,
            sides,
            pltpu.VMEM((windows * rows_up + 8, groups * LANES), F32),
            pltpu.VMEM((reach, depth), F32),
        ],
        compiler_params=vmem,
        cost_estimate=cost(3 * 10**9),
        name="attention_backward_inputs",
    )(span_start, band_rows, do, p, vblk, q16, kwin)

    proj_new, moment_one_new, moment_two_new, kernel_total = pl.pallas_call(
        functools.partial(update, group_count, span),
        out_shape=(shape(proj_weight.shape, F32),) * 3 + (shape((taps_a, 1, taps_b), F32),),
        in_specs=[whole] * (len(payloads) + 5),
        out_specs=(whole,) * 4,
        compiler_params=vmem,
        name="projection_update",
    )(*payloads, own, own_taps, proj_weight, moment_one, moment_two)
    return (
        query_grad,
        key_grad,
        value_grad,
        kernel_total.transpose(1, 0, 2),
        proj_new,
        moment_one_new,
        moment_two_new,
    )


def solution(mesh):
    heads, rows_of, blocks_of = P("dp", None, "tensor"), P("tensor", None, None), P("tensor", "dp")
    return jax.shard_map(
        shards,
        mesh=mesh,
        in_specs=(heads, heads, heads, rows_of, P("dp"), heads, blocks_of, blocks_of, blocks_of),
        out_specs=(heads, heads, heads, rows_of, blocks_of, blocks_of, blocks_of),
        check_vma=False,
    )
```

```python
import functools
import math

import jax
import jax.numpy as jnp
from jax import lax
from jax.experimental import pallas as pl
from jax.experimental.pallas import tpu as pltpu
from jax.sharding import PartitionSpec as P

beta_one = 0.9
beta_two = 0.95
learn_rate = 0.01
decay_rate = 0.1
adam_eps = 1e-08
bias_one = 1.0 - 0.9**10
bias_two = 1.0 - 0.95**10

LANES = 128
GROUP = 2
F32 = jnp.float32
BF16 = jnp.bfloat16


def dot(left, right, dims=((1,), (0,))):
    return lax.dot_general(left, right, (dims, ((), ())), preferred_element_type=F32)


def split(x):
    high = x.astype(BF16)
    return high, (x - high.astype(F32)).astype(BF16)


def up_to(n, multiple):
    return -(-n // multiple) * multiple


def iota(shape, axis):
    return lax.broadcasted_iota(jnp.int32, shape, axis)


def hold_bands(taps_ref, scale, bands_ref):
    taps_a, _, taps_b = taps_ref.shape
    lane = iota((1, LANES), 1)
    out = []
    for a in range(taps_a):
        row = jnp.zeros((1, LANES), F32)
        for b in range(taps_b):
            row = jnp.where(lane == (LANES - b) % LANES, taps_ref[a, 0, b], row)
        out.append(pltpu.roll(jnp.broadcast_to(row, (LANES, LANES)), 0, 1, stride=1, stride_axis=0))
    height = GROUP * LANES
    for n in range(taps_a // GROUP):
        cols = slice(n * LANES, (n + 1) * LANES)
        high, low = split(jnp.concatenate(out[n * GROUP : (n + 1) * GROUP][::-1], axis=0) * scale)
        bands_ref[:height, cols] = high
        bands_ref[height : 2 * height, cols] = low
        bands_ref[2 * height :, cols] = high


def turned_bands(bands_ref):
    spots = [part * GROUP + at for part in range(3) for at in range(GROUP - 1, -1, -1)]
    rows = []
    for n in range(bands_ref.shape[1] // LANES):
        cols = slice(n * LANES, (n + 1) * LANES)
        rows.append(jnp.concatenate([bands_ref[at * LANES : (at + 1) * LANES, cols] for at in spots], axis=1))
    return jnp.concatenate(rows, axis=0)


def fetch(pairs, sems):
    copies = [pltpu.make_async_copy(src, dst, sems.at[n]) for n, (src, dst) in enumerate(pairs)]
    for copy in copies:
        copy.start()
    return copies


def prepare(
    taps_hbm, w_hbm, q_hbm, grad_hbm,
    w_ref, bands_ref, q32, q16, grad_ref,
    taps_ref, w_in, q_in, sems,
):
    rows = q_in.shape[0]
    copies = fetch(((taps_hbm, taps_ref), (w_hbm, w_in), (q_hbm.at[0], q_in), (grad_hbm, grad_ref)), sems)
    q32[...] = jnp.zeros_like(q32)
    copies[0].wait()
    hold_bands(taps_ref, 1.0 / math.sqrt(q_in.shape[1]), bands_ref)
    copies[1].wait()
    w_ref[...] = w_in[...].astype(BF16)
    copies[2].wait()
    q32[:rows] = q_in[...].astype(F32)
    rows_up = q16.shape[0] // GROUP
    for n in range(GROUP):
        q16[n * rows_up : (n + 1) * rows_up] = q32[n : n + rows_up].astype(BF16)
    copies[3].wait()


def by_blocks(rows_ref, out, rows32, start, live):
    rows = rows_ref.shape[1]
    rows32[:8] = jnp.zeros((8, LANES), F32)
    rows32[8 : 8 + rows] = rows_ref[0].astype(F32)
    rows32[8 + rows :] = jnp.zeros((rows32.shape[0] - 8 - rows, LANES), F32)
    count = out.shape[0] // LANES
    step = (rows32.shape[0] - 8 - LANES) // (count - 1)
    for n in range(count):
        block = rows32[8 + start + n * step : 8 + start + n * step + LANES]
        if live < LANES:
            block = jnp.where(iota(block.shape, 0) < live, block, 0.0)
        out[n * LANES : (n + 1) * LANES] = block.astype(BF16)


def forward(pieces, taps_a, half, *refs):
    piece_refs, (first_ref, bands_ref, q16, k_ref) = refs[:pieces], refs[pieces : pieces + 4]
    p_ref, kwin, pack_ref, rows32, xh, xl, y = refs[pieces + 4 :]
    span = p_ref.shape[0]
    rows_up = q16.shape[0] // GROUP
    windows = kwin.shape[0] // LANES
    step = LANES - 2 * half
    first = first_ref[0]
    for n, ref in enumerate(piece_refs):
        pack_ref[n * span : (n + 1) * span] = ref[0]

    by_blocks(k_ref, kwin, rows32, -half, LANES)

    scores = dot(q16[...], kwin[...], ((1,), (1,)))
    pos = first - (taps_a - 1) + iota((rows_up, LANES), 0) - iota((rows_up, LANES), 1)
    for n in range(windows):
        here = slice(n * rows_up, (n + 1) * rows_up)
        for at in range(GROUP):
            x = scores[at * rows_up : (at + 1) * rows_up, n * LANES : (n + 1) * LANES]
            cols = slice(at * LANES, (at + 1) * LANES)
            xh[here, cols], xl[here, cols] = split(jnp.where(pos >= n * step - half - at, x, 0.0))

    y[...] = dot(jnp.concatenate([xh[...], xh[...], xl[...]], axis=1), bands_ref[...])
    mixed = []
    for n in range(windows):
        total = None
        for group in range(taps_a // GROUP):
            start = n * rows_up + taps_a - GROUP * (group + 1)
            term = y[start : start + span, group * LANES : (group + 1) * LANES]
            total = term if total is None else total + term
        mixed.append(total)
    c = jnp.concatenate(mixed, axis=1)
    lane = iota((span, LANES), 1)
    row = iota((span, LANES), 0)
    ahead = jnp.where(lane < step, lane - row, windows * LANES + span)
    live = jnp.concatenate([ahead <= first - n * step for n in range(windows)], axis=1)
    c = jnp.where(live, c, -jnp.inf)
    terms = jnp.exp(c - jnp.max(c, axis=1, keepdims=True))
    p = terms * (1.0 / jnp.sum(terms, axis=1, keepdims=True))
    p_ref[...] = p


def forward_turned(taps_a, half, first_ref, kwin, q32, p_ref, v_ref, xth_ref, xtl_ref, vblk, o_ref, kturn, rows32):
    span = xth_ref.shape[1] // taps_a
    windows = kwin.shape[0] // LANES
    step = LANES - 2 * half
    first = first_ref[0]
    by_blocks(v_ref, vblk, rows32, 0, step)
    o_ref[...] = dot(p_ref[...].astype(BF16), vblk[...]).astype(BF16)
    flip = (iota((LANES, LANES), 0) + iota((LANES, LANES), 1) == LANES - 1).astype(F32).astype(BF16)
    for n in range(windows):
        here = slice(n * LANES, (n + 1) * LANES)
        kturn[here] = dot(flip, kwin[here]).astype(BF16)
    lead = LANES - 1 - half - iota((LANES, span), 0) - iota((LANES, span), 1)
    lead = jnp.concatenate([lead + n * step for n in range(windows)], axis=0)
    shifted = jnp.concatenate([q32[taps_a - 1 - a : taps_a - 1 - a + span].astype(BF16) for a in range(taps_a)], axis=0)
    xt = dot(kturn[...], shifted, ((1,), (1,)))
    for a in range(taps_a):
        cols = slice(a * span, (a + 1) * span)
        xth_ref[:, cols], xtl_ref[:, cols] = split(jnp.where(lead <= first - a, xt[:, cols], 0.0))


def spots(places, axis):
    me = lax.axis_index(axis)
    return [(n, part, at if shift is None else lax.bitwise_xor(me, shift)) for n, part, shift, at in places]


def backward_columns(places, *refs):
    *up_refs, o_ref, up, grad = refs
    for n, part, spot in spots(places, "tensor"):
        block = up_refs[n][part]
        width = block.shape[1]
        up[:, pl.ds(pl.multiple_of(spot * width, width), width)] = block
    grad[...] = dot(o_ref[...], up[...], ((0,), (0,)))


def backward_scores(places, owners, by_distance, *refs):
    n_w = len({p[0] for p in places})
    w_refs, refs = refs[:n_w], refs[n_w:]
    up, grad, p_ref, vblk, xth_ref, xtl_ref, do_ref, own_ref, own_taps_ref, *out_refs = refs
    span = p_ref.shape[0]
    taps_a = xth_ref.shape[1] // span
    windows = vblk.shape[0] // LANES

    do = None
    for n, part, spot in spots(places, "dp"):
        block = w_refs[n][part]
        width = block.shape[1]
        term = dot(up[:, pl.ds(pl.multiple_of(spot * width, width), width)], block, ((1,), (1,)))
        do = term if do is None else do + term
    do = do.astype(BF16)
    do_ref[...] = do
    dc = scores_grad(p_ref[...], do, vblk[...])

    right = jnp.concatenate(
        [jnp.concatenate(split(dc[:, n * LANES : (n + 1) * LANES]), axis=1) for n in range(windows)], axis=0
    )
    right = jnp.concatenate([right, right], axis=0)
    sums = []
    for a in range(taps_a):
        cols = slice(a * span, (a + 1) * span)
        left = jnp.concatenate(
            [ref[n * LANES : (n + 1) * LANES, cols] for ref in (xth_ref, xtl_ref) for n in range(windows)], axis=1
        )
        total = dot(left, right)
        turned = pltpu.roll(total[:, :LANES] + total[:, LANES:], 0, 1, stride=1, stride_axis=0)
        sums.append(jnp.sum(turned, axis=0, keepdims=True))
    taps = jnp.concatenate(sums + [jnp.zeros((8 - taps_a, LANES), F32)], axis=0)

    high, low = split(taps)
    mid, low = low, (taps - high.astype(F32) - low.astype(F32)).astype(BF16)
    aside = pltpu.roll(low.astype(F32), LANES // 2, 1)
    first = jnp.where(iota(aside.shape, 1) < LANES // 2, aside, high.astype(F32))
    parts = jnp.concatenate([first, mid.astype(F32)], axis=0).astype(BF16)
    own_taps_ref[...] = taps
    depth, share = own_ref.shape
    me = lax.axis_index("dp")

    def owned(spot):
        return grad[:, pl.ds(pl.multiple_of(spot * share, share), share)]

    own_ref[...] = owned(me)
    for owner, ref in zip(owners, out_refs, strict=True):
        piece = owned(lax.bitwise_xor(me, owner) if by_distance else owner).astype(BF16)
        for n in range(share // LANES):
            ref[n * depth : (n + 1) * depth] = piece[:, n * LANES : (n + 1) * LANES]
        ref[ref.shape[0] - 16 :] = parts


def scores_grad(p, do, vblk):
    dp = dot(do, vblk, ((1,), (1,)))
    return p * (dp - jnp.sum(p * dp, axis=1, keepdims=True))


def backward_inputs(
    rows, keys, taps_a, half, first_ref, bands_ref, do_ref, p_ref, vblk, q16, kwin,
    dq_ref, dk_ref, dv_ref,
    dc_ref, left_h, left_l, z, sums,
):
    step = LANES - 2 * half
    depth = kwin.shape[1]
    windows = kwin.shape[0] // LANES
    rows_up = q16.shape[0] // GROUP
    scale = 1.0 / math.sqrt(depth)
    first = first_ref[0]
    do = do_ref[...]
    span = do.shape[0]
    dc_ref[:8] = jnp.zeros((8, dc_ref.shape[1]), F32)
    dc_ref[8 : 8 + span] = scores_grad(p_ref[...], do, vblk[...])
    dc_ref[8 + span :] = jnp.zeros((dc_ref.shape[0] - 8 - span, dc_ref.shape[1]), F32)
    for n in range(windows):
        cols = slice(n * LANES, (n + 1) * LANES)
        here = slice(n * rows_up, (n + 1) * rows_up)
        for at in range(GROUP):
            there = slice(at * LANES, (at + 1) * LANES)
            left_h[here, there], left_l[here, there] = split(dc_ref[at : at + rows_up, cols])
        sums[n * step : n * step + LANES] = dot(p_ref[:, cols].astype(BF16).T, do)
    dv_ref[0] = sums[:keys].astype(BF16)
    z[windows * rows_up :] = jnp.zeros((z.shape[0] - windows * rows_up, z.shape[1]), F32)
    left = jnp.concatenate([left_h[...], left_h[...], left_l[...]], axis=1)
    z[: windows * rows_up] = dot(left, turned_bands(bands_ref), ((1,), (1,)))

    lane = iota((rows_up, LANES), 1)
    row = iota((rows_up, LANES), 0)
    scores = []
    for n in range(windows):
        total = None
        for group in range(taps_a // GROUP):
            start = n * rows_up + 8 - (taps_a - 1) + GROUP * group
            term = z[start : start + rows_up, group * LANES : (group + 1) * LANES]
            total = term if total is None else total + term
        scores.append(total)
    sums[...] = jnp.zeros_like(sums)
    dq = jnp.zeros((rows_up, depth), F32)
    for n, total in enumerate(scores):
        if n + 1 < windows:
            total = jnp.where(lane < step, total, total + pltpu.roll(scores[n + 1], step, 1))
        live = (n * step - half + lane <= first - (taps_a - 1) + row) & (row < rows)
        ds = jnp.where(live & (lane >= 2 * half) if n else live, total * (1.0 / scale), 0.0)
        dq = dq + dot(ds.astype(BF16), kwin[n * LANES : (n + 1) * LANES])
        sums[n * step : n * step + LANES] += dot(ds.astype(BF16).T, q16[:rows_up])
    dk_ref[0] = (scale * sums[half : half + keys]).astype(BF16)
    dq_ref[0] = (scale * dq)[:rows].astype(BF16)


def update(count, span, *refs):
    payload_refs, (own_ref, own_taps_ref, w_ref, one_ref, two_ref) = refs[:-9], refs[-9:-4]
    new_ref, one_new_ref, two_new_ref, taps_ref = refs[-4:]
    taps_a, _, taps_b = taps_ref.shape
    depth, share = own_ref.shape
    grad, taps = own_ref[...], own_taps_ref[...]
    for ref in payload_refs:
        piece = [ref[n * depth : (n + 1) * depth] for n in range(share // LANES)]
        grad = grad + jnp.concatenate(piece, axis=1).astype(F32)
        parts = ref[ref.shape[0] - 16 :].astype(F32)
        taps = taps + (parts[:8] + (parts[8:] + pltpu.roll(parts[:8], LANES // 2, 1)))
    grad = grad * (1.0 / count)
    taps = taps * (1.0 / (math.sqrt(depth) * count * span))
    lane = iota((8, LANES), 1)
    turned = jnp.zeros((8, LANES), F32)
    for b in range(taps_b):
        turned = jnp.where(lane == b, taps[:, LANES - 1 - b : LANES - b], turned)
    for a in range(taps_a):
        taps_ref[a] = turned[a : a + 1, :taps_b]
    one = beta_one * one_ref[...] + (1.0 - beta_one) * grad
    two = beta_two * two_ref[...] + (1.0 - beta_two) * grad * grad
    one_new_ref[...] = one
    two_new_ref[...] = two
    old = w_ref[...]
    new_ref[...] = old - learn_rate * ((one * (1.0 / bias_one)) / (jnp.sqrt(two * (1.0 / bias_two)) + adam_eps) + decay_rate * old)


def swap(x, axis, shift):
    n = lax.axis_size(axis)
    return lax.ppermute(x, axis, [(i, i ^ shift) for i in range(n)])


def turns(n):
    return list(range(n // 2, n)) + list(range(n // 2 - 1, 0, -1))


def few(axis):
    n = lax.axis_size(axis)
    return n <= 8 and n & (n - 1) == 0


def gathered(x, axis):
    if few(axis):
        shifts = turns(lax.axis_size(axis))[::-1]
        arrays = [x] + [swap(x, axis, s) for s in shifts]
        return arrays, [(n, slice(None), s, None) for n, s in enumerate([0, *shifts])]
    n = lax.axis_size(axis)
    return [lax.all_gather(x, axis)], [(0, i, None, i) for i in range(n)]


def shards(queries, keys, values, conv_kernel, span_start, out_grad, proj_weight, moment_one, moment_two):
    _, rows, depth = queries.shape
    key_count = keys.shape[1]
    _, taps_a, taps_b = conv_kernel.shape
    span = out_grad.shape[1]
    half = (taps_b - 1) // 2
    step = LANES - 2 * half
    windows = -(-key_count // step)
    rows_up = up_to(rows, 16)
    wide = windows * LANES
    reach = up_to((windows - 1) * step + LANES, 8)
    groups = taps_a // GROUP
    group_count = lax.axis_size("dp")
    share = proj_weight.shape[1]
    columns = share * group_count
    vmem = pltpu.CompilerParams(vmem_limit_bytes=24 * 2**20)
    whole = pl.BlockSpec(memory_space=pltpu.VMEM)
    hbm = pl.BlockSpec(memory_space=pltpu.HBM)
    shape = jax.ShapeDtypeStruct
    stay = lambda x: pltpu.with_memory_space_constraint(x, pltpu.HBM)
    q_hbm = stay(queries)
    taps_hbm = stay(conv_kernel.transpose(1, 0, 2))
    smem = pl.BlockSpec(memory_space=pltpu.SMEM)
    taps_ref = pltpu.SMEM((taps_a, 1, taps_b), F32)
    rows32 = pltpu.VMEM(((windows - 1) * step + LANES + 8, depth), F32)
    band = shape((3 * GROUP * LANES, groups * LANES), BF16)
    sides = pltpu.VMEM((windows * rows_up, GROUP * LANES), BF16)

    def cost(flops):
        return pl.CostEstimate(flops=flops, bytes_accessed=10**6, transcendentals=0)

    proj_bf, band_rows, q32, q16, local_grad = pl.pallas_call(
        prepare,
        out_shape=(
            shape(proj_weight.shape, BF16),
            band,
            shape((rows_up + 8, depth), F32),
            shape((GROUP * rows_up, depth), BF16),
            shape(out_grad.shape, BF16),
        ),
        in_specs=[hbm] * 4,
        out_specs=(whole,) * 5,
        scratch_shapes=[
            taps_ref,
            pltpu.VMEM(proj_weight.shape, F32),
            pltpu.VMEM((rows, depth), BF16),
            pltpu.SemaphoreType.DMA((4,)),
        ],
        compiler_params=vmem,
        cost_estimate=cost(5 * 10**9),
        name="prepare",
    )(taps_hbm, stay(proj_weight), q_hbm, stay(out_grad))
    w_arrays, w_places = gathered(proj_bf, "dp")
    cores_last = few("tensor") and lax.axis_size("tensor") > 2
    pieces = [local_grad]
    if cores_last:
        pieces += [swap(out_grad, "tensor", s) for s in range(2, lax.axis_size("tensor"), 2)]
    p, kwin, pack = pl.pallas_call(
        functools.partial(forward, len(pieces), taps_a, half),
        out_shape=(
            shape((span, wide), F32),
            shape((wide, depth), BF16),
            shape((len(pieces) * span, out_grad.shape[2]), BF16),
        ),
        in_specs=[whole] * len(pieces) + [smem] + [whole] * 3,
        out_specs=(whole,) * 3,
        scratch_shapes=[
            rows32,
            sides,
            sides,
            pltpu.VMEM((windows * rows_up, groups * LANES), F32),
        ],
        compiler_params=vmem,
        cost_estimate=cost(5 * 10**9),
        name="attention_forward",
    )(*pieces, span_start, band_rows, q16, keys)
    if cores_last:
        up_arrays = [pack, swap(pack, "tensor", 1)]
        up_places = [
            (c, slice(n * span, (n + 1) * span), 2 * n + c, None) for n in range(len(pieces)) for c in (0, 1)
        ]
    else:
        up_arrays, up_places = gathered(out_grad[0], "tensor")
    xth, xtl, vblk, attended = pl.pallas_call(
        functools.partial(forward_turned, taps_a, half),
        out_shape=(shape((wide, taps_a * span), BF16),) * 2 + (shape((wide, depth), BF16), shape((span, depth), BF16)),
        in_specs=[smem] + [whole] * 4,
        out_specs=(whole,) * 4,
        scratch_shapes=[pltpu.VMEM((wide, depth), BF16), rows32],
        compiler_params=vmem,
        cost_estimate=cost(2 * 10**9),
        name="attention_forward_turned",
    )(span_start, kwin, q32, p, values)

    owners = list(range(group_count))
    if few("dp"):
        owners = owners[group_count // 2 : 0 : -1] + owners[group_count // 2 + 1 :]
    others = len(owners)
    up, grad = pl.pallas_call(
        functools.partial(backward_columns, up_places),
        out_shape=(shape((span, columns), BF16), shape((depth, columns), F32)),
        in_specs=[whole] * (len(up_arrays) + 1),
        out_specs=(whole,) * 2,
        compiler_params=vmem,
        cost_estimate=cost(10**9),
        name="attention_backward_columns",
    )(*up_arrays, attended)
    do, own, own_taps, *payloads = pl.pallas_call(
        functools.partial(backward_scores, w_places, owners, few("dp")),
        out_shape=(
            shape((span, depth), BF16),
            shape((depth, share), F32),
            shape((8, LANES), F32),
        ) + (shape((depth * (share // LANES) + 16, LANES), BF16),) * others,
        in_specs=[whole] * (len(w_arrays) + 6),
        out_specs=(whole,) * (3 + others),
        compiler_params=vmem,
        cost_estimate=cost(2 * 10**9),
        name="attention_backward_scores",
    )(*w_arrays, up, grad, p, vblk, xth, xtl)

    if few("dp"):
        payloads = [swap(payload, "dp", owner) for owner, payload in zip(owners, payloads, strict=True)]
    else:
        sent = lax.all_to_all(jnp.stack(payloads), "dp", 0, 0)
        payloads = [jnp.where(lax.axis_index("dp") == n, jnp.zeros_like(sent[n]), sent[n]) for n in range(group_count)]

    query_grad, key_grad, value_grad = pl.pallas_call(
        functools.partial(backward_inputs, rows, key_count, taps_a, half),
        out_shape=(shape(queries.shape, BF16), shape(keys.shape, BF16), shape(values.shape, BF16)),
        in_specs=[smem] + [whole] * 6,
        out_specs=(whole,) * 3,
        scratch_shapes=[
            pltpu.VMEM((rows_up + 8, wide), F32),
            sides,
            sides,
            pltpu.VMEM((windows * rows_up + 8, groups * LANES), F32),
            pltpu.VMEM((reach, depth), F32),
        ],
        compiler_params=vmem,
        cost_estimate=cost(3 * 10**9),
        name="attention_backward_inputs",
    )(span_start, band_rows, do, p, vblk, q16, kwin)

    proj_new, moment_one_new, moment_two_new, kernel_total = pl.pallas_call(
        functools.partial(update, group_count, span),
        out_shape=(shape(proj_weight.shape, F32),) * 3 + (shape((taps_a, 1, taps_b), F32),),
        in_specs=[whole] * (len(payloads) + 5),
        out_specs=(whole,) * 4,
        compiler_params=vmem,
        name="projection_update",
    )(*payloads, own, own_taps, proj_weight, moment_one, moment_two)
    return (
        query_grad,
        key_grad,
        value_grad,
        kernel_total.transpose(1, 0, 2),
        proj_new,
        moment_one_new,
        moment_two_new,
    )


def solution(mesh):
    heads, rows_of, blocks_of = P("dp", None, "tensor"), P("tensor", None, None), P("tensor", "dp")
    return jax.shard_map(
        shards,
        mesh=mesh,
        in_specs=(heads, heads, heads, rows_of, P("dp"), heads, blocks_of, blocks_of, blocks_of),
        out_specs=(heads, heads, heads, rows_of, blocks_of, blocks_of, blocks_of),
        check_vma=False,
    )
```
